32 devices in a mesh: groups: 2 (over y), seq: 16 (over z, x, core).
Axes of the slice: x: 2, y: 2, z: 4, core: 2. Of those that a mesh axis runs over, the one named last changes fastest.
Arguments:
- pool_kv: bfloat16 [3072, 1024], P(('groups', 'seq')), parts along dimension 0, may hold values from -6 to 6
- pool_slot: int32 [32], P('groups'), parts along dimension 0, may hold values from 0 to 15, each once
- passage_order: int32 [32], P('groups'), parts along dimension 0, may hold values from 0 to 15, each once
- passage_start: int32 [32], P('groups'), parts along dimension 0, may hold values from 0 to 6784, as said below
- recompute_pos: int32 [32, 56], P('groups'), parts along dimension 0, may hold values from 0 to 383, as said below
- page_table: int32 [3072], P('groups'), parts along dimension 0, may hold values from 0 to 1535, as said below
- fresh_q: bfloat16 [1792, 1024], P(('groups', 'seq')), parts along dimension 0, may hold values from -64 to 64
- fresh_kv: bfloat16 [1792, 256], P(('groups', 'seq')), parts along dimension 0, may hold values from -64 to 64
Outputs:
- attended: bfloat16 [1792, 1024], P(('groups', 'seq')), parts along dimension 0
- decode_cache: bfloat16 [3072, 1024], P(('groups', 'seq')), parts along dimension 0
The draws below stay inside these ranges and needn't reach their ends.
There are 2 independent parts, one for each index of `groups`. The reference program is written for one: setup_inputs(seed, part) draws one part's arguments, and reference() takes and returns one part's arrays. A program takes and returns all parts, laid end to end along the dimension named above; each array names one. Nothing has to cross between parts.
Inputs may be any that keep to these rules, and one draw needn't show every extreme that they name: `passage_start`: increases by at least 384 from one passage to the next; the first is 0 and the last is (15) * 384 + 1024. `recompute_pos`: each row holds 56 different positions of its passage in increasing order. `page_table`: every row of the decode cache receives exactly one page; of the 96 pages of one passage at most 6 go to the 96 rows of one owner, and that many do for some owner.
All inputs are finite; a program needn't handle non-finite values.
Results may differ from the reference program's by a relative error of at most 0.0075.
The reference program's roundings to bfloat16 on the way count: a program that leaves them out, or rounds other values in their place, can miss the bound.
Values may be sent and summed in bfloat16 or wider, within the bound.
No kernel may reach another device: no remote copies, remote signals or barrier semaphores. Data moves between devices by JAX's collectives and lax.ppermute only.
A program may use at most 256 MiB of HBM per device.

```python
import jax
import jax.numpy as jnp
from jax import lax

HD = 128
GROUP = 8
TOK_DEV = 384
PAGE = 4
GAP = 1024
PASSAGES = 16
SEL = 56
P_DEV = 96
CONTEXT = 6144


def draw_passage_start(key, part):
    extra = jnp.sort(jax.random.randint(jax.random.fold_in(key, 3), (PASSAGES,), 0, GAP + 1))
    extra = extra.at[0].set(0).at[PASSAGES - 1].set(GAP)
    return (jnp.arange(PASSAGES, dtype=jnp.int32) * TOK_DEV + extra).astype(jnp.int32)


def draw_recompute_pos(key, part):
    row_keys = jax.random.split(jax.random.fold_in(key, 5), PASSAGES)

    def one_row(row_key):
        return jnp.sort(jax.random.permutation(row_key, TOK_DEV)[:SEL])
    return jax.vmap(one_row)(row_keys).astype(jnp.int32)


def draw_page_table(key, part):
    split_keys = jax.random.split(jax.random.fold_in(key, 9), 4)
    owner_map = jax.random.permutation(split_keys[0], PASSAGES)
    device_shift = jax.random.permutation(split_keys[1], PASSAGES)
    spread = max(PASSAGES, P_DEV)
    page_offset = jax.random.permutation(split_keys[2], spread)[:P_DEV] % PASSAGES
    slot_keys = jax.random.split(split_keys[3], PASSAGES)
    slot_order = jax.vmap(lambda slot_key: jax.random.permutation(slot_key, P_DEV))(slot_keys)
    owners = owner_map[(device_shift[:, None] + page_offset[None, :]) % PASSAGES]
    page_slots = slot_order[owners, jnp.arange(P_DEV)[None, :]]
    return (owners * P_DEV + page_slots).reshape(-1).astype(jnp.int32)


def fresh_parts(key):
    split_keys = jax.random.split(jax.random.fold_in(key, 11), 4)
    row_count = PASSAGES * SEL
    query_rows = jnp.clip(jax.random.normal(split_keys[1], (row_count, GROUP * HD)) * 3.0, -20.0, 20.0)
    key_rows = jnp.clip(jax.random.normal(split_keys[2], (row_count, HD)), -6.0, 6.0)
    value_rows = jnp.clip(jax.random.normal(split_keys[3], (row_count, HD)), -6.0, 6.0)
    return (query_rows, jnp.concatenate([key_rows, value_rows], axis=1))


def draw_fresh_q(key, part):
    return fresh_parts(key)[0].astype(jnp.bfloat16)


def draw_fresh_kv(key, part):
    return fresh_parts(key)[1].astype(jnp.bfloat16)


def shard_levels(rng, extent, cuts, smallest, top_value):
    gain, own = 1.0, jax.random.fold_in(rng, 6)
    for axis_at, parts in cuts:
        steps = jnp.exp(jax.random.uniform(jax.random.fold_in(own, axis_at), (parts,), jnp.float32, smallest / len(cuts), top_value / len(cuts)))
        gain = gain * jnp.repeat(steps, extent[axis_at] // parts).reshape([-1 if axis == axis_at else 1 for axis in range(len(extent))])
    return gain


def centred(stream_key, shape, scale, reach, cuts=(), kind=jnp.bfloat16):
    drawn = scale * jax.random.normal(stream_key, shape, jnp.float32)
    if cuts:
        drawn = drawn * shard_levels(stream_key, shape, cuts, -0.22, 0.18)
    return jnp.clip(drawn, -reach, reach).astype(kind)


def setup_inputs(seed: int = 0, part: int = 0) -> dict:
    keys = jax.random.split(jax.random.key(seed), 9)
    part_splits = jax.random.split(jax.random.fold_in(keys[8], part), 9)
    pool_kv = centred(part_splits[0], (PASSAGES * P_DEV, PAGE * 2 * HD), 1.0, 6.0, ((0, 16),))
    pool_slot = jax.random.permutation(part_splits[1], PASSAGES).astype(jnp.int32)
    passage_order = jax.random.permutation(part_splits[2], PASSAGES).astype(jnp.int32)
    passage_start = draw_passage_start(jax.random.fold_in(jax.random.fold_in(keys[8], part), 71), part)
    recompute_pos = draw_recompute_pos(jax.random.fold_in(jax.random.fold_in(keys[8], part), 71), part)
    page_table = draw_page_table(jax.random.fold_in(jax.random.fold_in(keys[8], part), 71), part)
    fresh_q = draw_fresh_q(jax.random.fold_in(jax.random.fold_in(keys[8], part), 71), part)
    fresh_kv = draw_fresh_kv(jax.random.fold_in(jax.random.fold_in(keys[8], part), 71), part)
    return {"pool_kv": pool_kv, "pool_slot": pool_slot, "passage_order": passage_order, "passage_start": passage_start, "recompute_pos": recompute_pos, "page_table": page_table, "fresh_q": fresh_q, "fresh_kv": fresh_kv}


ROPE_BASE = 500000.0


def rotate_pos(vector, positions):
    half_dim = vector.shape[-1] // 2
    frequency = ROPE_BASE ** (-(jnp.arange(half_dim, dtype=jnp.float32) * (2.0 / vector.shape[-1])))
    angles = positions.astype(jnp.float32)[..., None] * frequency
    cosine = jnp.cos(angles)
    sine = jnp.sin(angles)
    lower_half = vector[..., :half_dim]
    upper_half = vector[..., half_dim:]
    return jnp.concatenate([lower_half * cosine - upper_half * sine, upper_half * cosine + lower_half * sine], axis=-1)


def reference(pool_kv, pool_slot, passage_order, passage_start, recompute_pos, page_table, fresh_q, fresh_kv):
    page_ids = jnp.arange(P_DEV, dtype=jnp.int32)
    passage_ids = jnp.arange(PASSAGES, dtype=jnp.int32)
    spot_index = pool_slot[passage_order][:, None] * P_DEV + page_ids[None, :]
    pool_rows = (spot_index % PASSAGES) * P_DEV + spot_index // PASSAGES
    cached = pool_kv[pool_rows.reshape(-1)].reshape(PASSAGES, TOK_DEV, 2, HD)
    start_grid = jnp.broadcast_to(passage_start[:, None], (PASSAGES, TOK_DEV))
    shifted = rotate_pos(cached[:, :, 0, :].astype(jnp.float32), start_grid)
    fresh_rows = fresh_kv.reshape(PASSAGES, SEL, 2 * HD)
    fresh_pos = passage_start[:, None] + recompute_pos
    fresh_keys = rotate_pos(fresh_rows[:, :, :HD].astype(jnp.float32), fresh_pos)
    passage_grid = jnp.broadcast_to(passage_ids[:, None], (PASSAGES, SEL))
    key_rows = shifted.at[passage_grid, recompute_pos].set(fresh_keys).astype(jnp.bfloat16)
    value_rows = cached[:, :, 1, :].at[passage_grid, recompute_pos].set(fresh_rows[:, :, HD:])
    page_rows = jnp.stack([key_rows, value_rows], axis=2).reshape(PASSAGES * P_DEV, PAGE * 2 * HD)
    decode_cache = jnp.zeros_like(page_rows).at[page_table].set(page_rows)
    queries = rotate_pos(fresh_q.reshape(PASSAGES, SEL, GROUP, HD).astype(jnp.float32), fresh_pos[:, :, None]).astype(jnp.bfloat16)
    flat_keys = key_rows.reshape(CONTEXT, HD)
    flat_values = value_rows.reshape(CONTEXT, HD)
    key_index = jnp.arange(CONTEXT, dtype=jnp.int32)
    query_places = passage_ids[:, None] * TOK_DEV + recompute_pos

    def attend_passage(inputs):
        query_rows, query_place = inputs
        flat_queries = query_rows.reshape(SEL * GROUP, HD)
        limit = jnp.repeat(query_place, GROUP)
        scores = jnp.dot(flat_queries, flat_keys.T, preferred_element_type=jnp.float32) * (HD ** -0.5)
        allowed = key_index[None, :] <= limit[:, None]
        peak_score = jnp.max(jnp.where(allowed, scores, -jnp.inf), axis=1, keepdims=True)
        weights = jnp.where(allowed, jnp.exp(scores - peak_score), 0.0)
        weight_sum = jnp.sum(weights, axis=1, keepdims=True)
        mixed = jnp.dot(weights.astype(jnp.bfloat16), flat_values, preferred_element_type=jnp.float32) / weight_sum
        return mixed.astype(jnp.bfloat16).reshape(SEL, GROUP * HD)

    attended = lax.map(attend_passage, (queries, query_places)).reshape(PASSAGES * SEL, GROUP * HD)
    return attended, decode_cache
```

```python
from functools import partial

import jax
import jax.numpy as jnp
import numpy as np
from jax import lax
from jax.experimental import pallas as pl
from jax.experimental.pallas import tpu as pltpu
from jax.sharding import PartitionSpec as P

GROUP = 8
PAGE = 4
ROPE_BASE = 500000.0
FAR = float(2**23)
MASKED = -1e30
LOWEST = -1e29
TILE = 16

f32 = jnp.float32
bf16 = jnp.bfloat16


def round_up(value, step):
    return -(-value // step) * step


def frequencies(head_dim):
    half = head_dim // 2
    index = np.arange(half, dtype=np.float32) * np.float32(2.0 / head_dim)
    one = np.power(np.float32(ROPE_BASE), -index).astype(np.float32)
    return np.concatenate([one, one])[None, :]


def ring_place(chip, chips):
    return jnp.where(chip % 2 == 0, chip // 2, chips - 1 - chip // 2)


def ring_chip(place, chips):
    return jnp.where(place < chips // 2, 2 * place, 2 * (chips - 1 - place) + 1)


def ring_order(chips):
    return list(range(0, chips, 2)) + list(range(chips - 1, 0, -2))


def ring_pairs(chips, shift):
    order = ring_order(chips)
    return [
        (order[p] * 2 + core, order[(p + shift) % chips] * 2 + core)
        for p in range(chips)
        for core in range(2)
    ]


def turned(vector, cosine, signed_sine):
    half = vector.shape[1] // 2
    return vector * cosine + pltpu.roll(vector, half, 1) * signed_sine


def prep_kernel(
    seq_count, slot_ref, order_ref, start_ref, freq_ref, picked_ref, pool_ref, q_ref, kv_ref,
    chunk_ref, queries_ref, fresh_ref, heads_ref,
):
    pages = pool_ref.shape[0]
    sel = kv_ref.shape[0]
    head_dim = freq_ref.shape[1]
    pair = 2 * head_dim
    extra = chunk_ref.shape[0] - pages
    me = lax.axis_index("seq")
    sign = jnp.where(lax.broadcasted_iota(jnp.int32, (1, head_dim), 1) < head_dim // 2, -1.0, 1.0)
    spot = lax.broadcasted_iota(jnp.int32, (pages, head_dim), 0) * seq_count + me

    def place(k, start):
        low = slot_ref[order_ref[k]] * pages
        return jnp.where(jnp.logical_and(spot >= low, spot < low + pages), start_ref[k], start)

    start = lax.fori_loop(0, seq_count, place, jnp.zeros((pages, head_dim), jnp.int32), unroll=8)
    angle = start.astype(f32) * freq_ref[...]
    cosine, sine = jnp.cos(angle), jnp.sin(angle) * sign
    for u in range(PAGE):
        keys = slice(u * pair, u * pair + head_dim)
        values = slice(u * pair + head_dim, (u + 1) * pair)
        chunk_ref[:pages, keys] = turned(pool_ref[:, keys].astype(f32), cosine, sine).astype(bf16)
        chunk_ref[:pages, values] = pool_ref[:, values]

    row = jnp.broadcast_to(picked_ref[pl.ds(me, 1), :].astype(f32), (sel, sel))
    same = lax.broadcasted_iota(jnp.int32, (sel, sel), 0) == lax.broadcasted_iota(
        jnp.int32, (sel, sel), 1
    )
    picked = jnp.sum(jnp.where(same, row, 0.0), axis=1, keepdims=True)
    angle = (picked + start_ref[me].astype(f32)) * freq_ref[...]
    cosine, sine = jnp.cos(angle), jnp.sin(angle) * sign
    fresh_ref[...] = jnp.zeros_like(fresh_ref)
    fresh_ref[:sel, :head_dim] = turned(kv_ref[:, :head_dim].astype(f32), cosine, sine)
    fresh_ref[:sel, head_dim:] = kv_ref[:, head_dim:].astype(f32)
    for u in range(PAGE):
        chunk_ref[pages:, u * pair : (u + 1) * pair] = fresh_ref[
            u * extra : (u + 1) * extra, :
        ].astype(bf16)
    for h in range(GROUP):
        head = q_ref[:, h * head_dim : (h + 1) * head_dim].astype(f32)
        heads_ref[h * sel : (h + 1) * sel, :] = turned(head, cosine, sine)
    queries_ref[...] = heads_ref[...].astype(bf16)


def chunk_rows(pieces):
    parts = []
    width = pieces[0].shape[1] // PAGE
    for u in range(PAGE):
        for piece in pieces:
            parts.append(piece[:, u * width : (u + 1) * width])
    return jnp.concatenate(parts, axis=0)


def visit_kernel(seq_count, steps, layout, first, last, *refs):
    piece_count = sum(layout)
    pieces = refs[:piece_count]
    own_q, other_q, meta_ref, limit_ref, wanted_ref = refs[piece_count : piece_count + 5]
    refs = refs[piece_count + 5 :]
    if not first:
        old_ref, old_pages_ref = refs[:2]
        refs = refs[2:]
    head_dim = own_q.shape[1]
    factor = float(head_dim**-0.5 * np.log2(np.e))
    chips = seq_count // 2
    me = lax.axis_index("seq")
    core, here = me % 2, ring_place(me // 2, chips)
    lanes = lax.broadcasted_iota(jnp.int32, meta_ref.shape, 1)
    blocks, places, at = [], [], 0
    for step, count in zip(steps, layout):
        source = ring_chip((here - step + chips) % chips, chips) * 2 + core
        places.append(
            jnp.sum(jnp.where(lanes == source, meta_ref[...], 0.0), axis=1, keepdims=True)
        )
        blocks.append(chunk_rows(pieces[at : at + count]))
        at += count
    blended = jnp.concatenate(blocks, axis=0) if len(blocks) > 1 else blocks[0]
    place = jnp.concatenate(places, axis=0) if len(places) > 1 else places[0]
    queries = jnp.concatenate([own_q[...], other_q[...]], axis=0)
    flipped = blended.T

    scores = lax.dot_general(
        blended[:, :head_dim], queries, (((1,), (1,)), ((), ())), preferred_element_type=f32
    )
    scores = jnp.where(place <= limit_ref[...], scores, MASKED)
    peak = jnp.max(scores, axis=0, keepdims=True)
    if first:
        new_peak = jnp.maximum(peak, LOWEST)
    else:
        old_peak = old_ref[head_dim : head_dim + 1, :]
        new_peak = jnp.maximum(peak, old_peak)
        fade = jnp.exp2((old_peak - new_peak) * factor)
    weights = jnp.exp2((scores - new_peak) * factor)
    total = jnp.sum(weights, axis=0, keepdims=True)
    mixed = jnp.dot(flipped[head_dim:, :], weights.astype(bf16), preferred_element_type=f32)
    chosen = jnp.where(place == wanted_ref[...], 1.0, 0.0).astype(bf16)
    picked = jnp.dot(flipped, chosen, preferred_element_type=f32)
    if not first:
        total = total + old_ref[head_dim + 1 : head_dim + 2, :] * fade
        mixed = mixed + old_ref[:head_dim, :] * fade
        picked = picked + old_pages_ref[...].astype(f32)
    picked = picked.astype(bf16)
    count = mixed.shape[1]
    tail = jnp.concatenate([new_peak, total, jnp.zeros((6, count), f32)], axis=0)
    if not last:
        new_ref, new_pages_ref = refs
        new_ref[:head_dim, :] = mixed
        new_ref[head_dim:, :] = tail
        new_pages_ref[...] = picked
    else:
        mine_ref, my_pages_ref, theirs_ref, their_pages_ref = refs
        half = count // 2
        mine_ref[:head_dim, :] = mixed[:, :half]
        mine_ref[head_dim:, :] = tail[:, :half]
        theirs_ref[:head_dim, :] = pltpu.roll(mixed, half, 1)[:, :half]
        theirs_ref[head_dim:, :] = pltpu.roll(tail, half, 1)[:, :half]
        wide = picked.shape[1] // 2
        my_pages_ref[...] = picked[:, :wide]
        their_pages_ref[...] = picked[:, wide:]


def join_kernel(mine_ref, my_pages_ref, got_ref, got_pages_ref, out_ref, pages_ref):
    head_dim = mine_ref.shape[0] - 8
    factor = float(head_dim**-0.5 * np.log2(np.e))
    peaks = [ref[head_dim : head_dim + 1, :] for ref in (mine_ref, got_ref)]
    top = jnp.maximum(peaks[0], peaks[1])
    fades = [jnp.exp2((peak - top) * factor) for peak in peaks]
    total = (
        mine_ref[head_dim + 1 : head_dim + 2, :] * fades[0]
        + got_ref[head_dim + 1 : head_dim + 2, :] * fades[1]
    )
    mixed = (mine_ref[:head_dim, :] * fades[0] + got_ref[:head_dim, :] * fades[1]) / total
    flat = mixed.T
    sel = out_ref.shape[0]
    for h in range(GROUP):
        out_ref[:, h * head_dim : (h + 1) * head_dim] = flat[h * sel : (h + 1) * sel, :].astype(
            bf16
        )
    pages = (my_pages_ref[...].astype(f32) + got_pages_ref[...].astype(f32)).T
    count = pages_ref.shape[0]
    pair = 2 * head_dim
    for u in range(PAGE):
        pages_ref[:, u * pair : (u + 1) * pair] = pages[u * count : (u + 1) * count, :].astype(
            bf16
        )


def shards(
    pool_kv, pool_slot, passage_order, passage_start, recompute_pos, page_table, fresh_q, fresh_kv
):
    seq_count = lax.axis_size("seq")
    chips = seq_count // 2
    me = lax.axis_index("seq")
    pages, width = pool_kv.shape
    sel = fresh_q.shape[0]
    head_dim = fresh_kv.shape[1] // 2
    tokens = pages * PAGE
    extra = round_up(-(-sel // PAGE), TILE)
    rows = pages + extra
    query_rows = sel * GROUP
    vmem = pl.BlockSpec(memory_space=pltpu.VMEM)
    smem = pl.BlockSpec(memory_space=pltpu.SMEM)
    params = pltpu.CompilerParams(vmem_limit_bytes=40 * 2**20)

    chunk, queries = pl.pallas_call(
        partial(prep_kernel, seq_count),
        out_shape=(
            jax.ShapeDtypeStruct((rows, width), bf16),
            jax.ShapeDtypeStruct((query_rows, head_dim), bf16),
        ),
        in_specs=[smem] * 3 + [vmem] * 5,
        out_specs=(vmem, vmem),
        scratch_shapes=[
            pltpu.VMEM((extra * PAGE, 2 * head_dim), f32),
            pltpu.VMEM((query_rows, head_dim), f32),
        ],
        compiler_params=params,
        name="prepare",
    )(
        pool_slot, passage_order, passage_start, jnp.asarray(frequencies(head_dim)),
        recompute_pos, pool_kv, fresh_q, fresh_kv,
    )

    passages = jnp.arange(seq_count, dtype=jnp.int32)
    spots = jnp.arange(tokens, dtype=jnp.int32)
    slots = jnp.sum(
        jnp.where(passage_order[:, None] == passages[None, :], pool_slot[None, :], 0), axis=1
    )
    replaced = jnp.any(recompute_pos[:, :, None] == spots[None, None, :], axis=1)
    natural = jnp.where(replaced, FAR, (passages[:, None] * tokens + spots[None, :]).astype(f32))
    by_slot = jnp.sum(
        jnp.where((slots[None, :] == passages[:, None])[:, :, None], natural[None], 0.0), axis=1
    )
    cached_place = by_slot.reshape(pages, seq_count, PAGE).transpose(2, 0, 1)
    fresh_place = jnp.pad(
        (recompute_pos + passages[:, None] * tokens).astype(f32),
        ((0, 0), (0, extra * PAGE - sel)),
        constant_values=FAR,
    )
    fresh_place = fresh_place.reshape(seq_count, PAGE, extra).transpose(1, 2, 0)
    meta = jnp.concatenate([cached_place, fresh_place], axis=1).reshape(PAGE * rows, seq_count)
    pair = jnp.stack([me, me ^ 1])
    limit = jnp.sum(
        jnp.where(
            pair[:, None, None] == passages[None, :, None],
            recompute_pos[None] + passages[None, :, None] * tokens,
            0,
        ),
        axis=1,
    ).astype(f32)
    limit = jnp.broadcast_to(limit[:, None, :], (2, GROUP, sel)).reshape(1, 2 * query_rows)
    page_ids = jnp.arange(pages, dtype=jnp.int32)
    request_pages = jnp.arange(page_table.shape[0], dtype=jnp.int32)
    owned = pair[:, None] * pages + page_ids[None, :]
    wanted = jnp.sum(
        jnp.where(page_table[None, None, :] == owned[:, :, None], request_pages[None, None, :], 0),
        axis=2,
    )
    wanted = wanted[:, None, :] * PAGE + jnp.arange(PAGE, dtype=jnp.int32)[None, :, None]
    wanted = wanted.astype(f32).reshape(1, 2 * tokens)

    swap = [(i, i ^ 1) for i in range(seq_count)]
    forward, backward = ring_pairs(chips, 1), ring_pairs(chips, -1)
    other_queries = lax.ppermute(queries, "seq", swap)

    state_shapes = (
        jax.ShapeDtypeStruct((head_dim + 8, 2 * query_rows), f32),
        jax.ShapeDtypeStruct((2 * head_dim, 2 * tokens), bf16),
    )
    last_shapes = (
        jax.ShapeDtypeStruct((head_dim + 8, query_rows), f32),
        jax.ShapeDtypeStruct((2 * head_dim, tokens), bf16),
    ) * 2

    def visit(state, arrivals, last=False):
        steps = [step for step, _ in arrivals]
        layout = [len(pieces) for _, pieces in arrivals]
        pieces = [piece for _, group in arrivals for piece in group]
        first = state is None
        operands = [*pieces, queries, other_queries, meta, limit, wanted]
        aliases = {}
        if not first:
            if not last:
                aliases = {len(operands): 0, len(operands) + 1: 1}
            operands += list(state)
        keys = PAGE * rows * len(steps)
        return pl.pallas_call(
            partial(visit_kernel, seq_count, steps, layout, first, last),
            out_shape=last_shapes if last else state_shapes,
            in_specs=[vmem] * len(operands),
            out_specs=(vmem,) * (4 if last else 2),
            input_output_aliases=aliases,
            compiler_params=params,
            cost_estimate=pl.CostEstimate(
                flops=4 * keys * head_dim * (2 * query_rows + 2 * tokens),
                bytes_accessed=4 * 2**20,
                transcendentals=keys * 2 * query_rows,
            ),
            name="visit",
        )(*operands)

    state = None
    ahead = behind = chunk
    arrivals = [(0, [chunk])]
    for step in range(1, chips // 2):
        ahead = lax.ppermute(ahead, "seq", forward)
        behind = lax.ppermute(behind, "seq", backward)
        state = visit(state, arrivals)
        arrivals = [(step, [ahead]), (-step, [behind])]
    cut = round_up(rows // 2, TILE)
    upper = lax.ppermute(ahead[:cut], "seq", forward)
    lower = lax.ppermute(behind[cut:], "seq", backward)
    state = visit(state, arrivals)
    mine, my_pages, theirs, their_pages = visit(state, [(chips // 2, [upper, lower])], last=True)
    got = lax.ppermute(theirs, "seq", swap)
    got_pages = lax.ppermute(their_pages, "seq", swap)
    return pl.pallas_call(
        join_kernel,
        out_shape=(
            jax.ShapeDtypeStruct((sel, GROUP * head_dim), bf16),
            jax.ShapeDtypeStruct((pages, width), bf16),
        ),
        in_specs=[vmem] * 4,
        out_specs=(vmem, vmem),
        compiler_params=params,
        name="join",
    )(mine, my_pages, got, got_pages)


def solution(mesh):
    placed = (
        P(("groups", "seq"), None),
        P("groups"),
        P("groups"),
        P("groups"),
        P("groups", None),
        P("groups"),
        P(("groups", "seq"), None),
        P(("groups", "seq"), None),
    )
    return jax.shard_map(
        shards,
        mesh=mesh,
        in_specs=placed,
        out_specs=(P(("groups", "seq"), None), P(("groups", "seq"), None)),
        check_vma=False,
    )
```

```python
from functools import partial

import jax
import jax.numpy as jnp
import numpy as np
from jax import lax
from jax.experimental import pallas as pl
from jax.experimental.pallas import tpu as pltpu
from jax.sharding import PartitionSpec as P

GROUP = 8
PAGE = 4
ROPE_BASE = 500000.0
FAR = float(2**23)
MASKED = -1e30
LOWEST = -1e29
TILE = 16
LANES = 128

QUARTER = (1.5703125, 253 * 2.0**-19, 170 * 2.0**-27, float(np.pi / 2 - 1.5703125 - 253 * 2.0**-19 - 170 * 2.0**-27))

f32 = jnp.float32
bf16 = jnp.bfloat16


def round_up(value, step):
    return -(-value // step) * step


def frequencies(head_dim):
    half = head_dim // 2
    index = np.arange(half, dtype=np.float32) * np.float32(2.0 / head_dim)
    one = np.power(np.float32(ROPE_BASE), -index).astype(np.float32)
    return np.concatenate([one, one])[None, :]


def ring_place(chip, chips):
    return jnp.where(chip % 2 == 0, chip // 2, chips - 1 - chip // 2)


def ring_chip(place, chips):
    return jnp.where(place < chips // 2, 2 * place, 2 * (chips - 1 - place) + 1)


def ring_order(chips):
    return list(range(0, chips, 2)) + list(range(chips - 1, 0, -2))


def ring_pairs(chips, shift):
    order = ring_order(chips)
    return [
        (order[p] * 2 + core, order[(p + shift) % chips] * 2 + core)
        for p in range(chips)
        for core in range(2)
    ]


def turned(vector, cosine, signed_sine):
    half = vector.shape[1] // 2
    return vector * cosine + pltpu.roll(vector, half, 1) * signed_sine


def cos_sin(angle):
    turns = jnp.round(angle * float(2 / np.pi))
    rest = angle
    for part in QUARTER:
        rest = rest - turns * part
    square = rest * rest
    sine = rest + rest * square * (
        -1.6666654611e-1 + square * (8.3321608736e-3 - square * 1.9515295891e-4)
    )
    cosine = (
        1.0
        - 0.5 * square
        + square
        * square
        * (4.166664568298827e-2 + square * (-1.388731625493765e-3 + square * 2.443315711809948e-5))
    )
    quadrant = turns.astype(jnp.int32) & 3
    odd = (quadrant & 1) == 1
    cos_value = jnp.where(odd, sine, cosine)
    sin_value = jnp.where(odd, cosine, sine)
    cos_value = jnp.where((quadrant == 1) | (quadrant == 2), -cos_value, cos_value)
    sin_value = jnp.where(quadrant >= 2, -sin_value, sin_value)
    return cos_value, sin_value


def rotation(angle):
    head_dim = angle.shape[1]
    cosine, sine = cos_sin(angle)
    lower = lax.broadcasted_iota(jnp.int32, angle.shape, 1) < head_dim // 2
    return cosine, jnp.where(lower, -sine, sine)


def fresh_rotation(row, start, frequency):
    sel = row.shape[1]
    wide = jnp.broadcast_to(row.astype(f32), (sel, sel))
    same = lax.broadcasted_iota(jnp.int32, (sel, sel), 0) == lax.broadcasted_iota(
        jnp.int32, (sel, sel), 1
    )
    picked = jnp.sum(jnp.where(same, wide, 0.0), axis=1, keepdims=True)
    return rotation((picked + start.astype(f32)) * frequency)


def fetch(sources, targets, sems):
    copies = [
        pltpu.make_async_copy(source, target, sems.at[i])
        for i, (source, target) in enumerate(zip(sources, targets))
    ]
    for copy in copies:
        copy.start()
    return copies


def prep_kernel(seq_count, *refs):
    sources, (chunk_ref,), targets = refs[:7], refs[7:8], refs[8:15]
    fresh_ref, sems = refs[15:]
    copies = fetch(sources, targets, sems)
    slot_ref, order_ref, start_ref, freq_ref, picked_ref, kv_ref, pool_ref = targets
    pages = pool_ref.shape[0]
    sel = kv_ref.shape[0]
    head_dim = freq_ref.shape[1]
    pair = 2 * head_dim
    extra = chunk_ref.shape[0] - pages
    me = lax.axis_index("seq")
    spot = lax.broadcasted_iota(jnp.int32, (pages, head_dim), 0) * seq_count + me
    for copy in copies[:-1]:
        copy.wait()

    def place(k, start):
        low = slot_ref[order_ref[k]] * pages
        return jnp.where(jnp.logical_and(spot >= low, spot < low + pages), start_ref[k], start)

    start = lax.fori_loop(0, seq_count, place, jnp.zeros((pages, head_dim), jnp.int32), unroll=16)
    cosine, sine = fresh_rotation(picked_ref[pl.ds(me, 1), :], start_ref[me], freq_ref[...])
    fresh_ref[sel:, :] = jnp.zeros((fresh_ref.shape[0] - sel, pair), f32)
    fresh_ref[:sel, :head_dim] = turned(kv_ref[:, :head_dim].astype(f32), cosine, sine)
    fresh_ref[:sel, head_dim:] = kv_ref[:, head_dim:].astype(f32)
    for u in range(PAGE):
        chunk_ref[pages:, u * pair : (u + 1) * pair] = fresh_ref[
            u * extra : (u + 1) * extra, :
        ].astype(bf16)

    cosine, sine = rotation(start.astype(f32) * freq_ref[...])
    copies[-1].wait()
    for u in range(PAGE):
        keys = slice(u * pair, u * pair + head_dim)
        values = slice(u * pair + head_dim, (u + 1) * pair)
        chunk_ref[:pages, keys] = turned(pool_ref[:, keys].astype(f32), cosine, sine).astype(bf16)
        chunk_ref[:pages, values] = pool_ref[:, values]


def plan_kernel(seq_count, tokens, *refs):
    sources, (queries_ref, facts_ref), targets = refs[:6], refs[6:8], refs[8:14]
    heads_ref, sems = refs[14:]
    for copy in fetch(sources, targets, sems):
        copy.wait()
    slot_ref, order_ref, start_ref, freq_ref, picked_ref, q_ref = targets
    me = lax.axis_index("seq")
    sel = q_ref.shape[0]
    head_dim = freq_ref.shape[1]

    row = picked_ref[pl.ds(me, 1), :]
    cosine, sine = fresh_rotation(row, start_ref[me], freq_ref[...])
    for h in range(GROUP):
        head = q_ref[:, h * head_dim : (h + 1) * head_dim].astype(f32)
        heads_ref[h * sel : (h + 1) * sel, :] = turned(head, cosine, sine)
    queries_ref[...] = heads_ref[...].astype(bf16)

    other = me + 1 - 2 * (me % 2)
    ours = (row + me * tokens).astype(f32)
    theirs = (picked_ref[pl.ds(other, 1), :] + other * tokens).astype(f32)
    both = jnp.concatenate([ours] * GROUP + [theirs] * GROUP, axis=1)
    at = put_rows(facts_ref, seq_count, both)

    shape = (seq_count, facts_ref.shape[1])
    lanes = lax.broadcasted_iota(jnp.int32, shape, 1)
    passages = lax.broadcasted_iota(jnp.int32, shape, 0)
    begin = ((passages + 1) * tokens).astype(f32)
    facts_ref[:seq_count, :] = jnp.where(lanes == shape[1] - 1, begin, FAR)
    facts_ref[:seq_count, :sel] = picked_ref[...].astype(f32)

    lanes = lax.broadcasted_iota(jnp.int32, (1, round_up(seq_count, shape[1])), 1)

    def slot(k, row):
        return jnp.where(lanes == k, slot_ref[order_ref[k]], row)

    slots = lax.fori_loop(0, seq_count, slot, jnp.zeros(lanes.shape, jnp.int32), unroll=16)
    put_rows(facts_ref, at, slots.astype(f32))


def put_rows(ref, at, row):
    width = ref.shape[1]
    for i in range(row.shape[1] // width):
        ref[at + i : at + i + 1, :] = row[:, i * width : (i + 1) * width]
    return at + row.shape[1] // width


def get_rows(ref, at, count):
    return jnp.concatenate([ref[at + i : at + i + 1, :] for i in range(count)], axis=1)


def fact_rows(seq_count, query_rows, width):
    return seq_count, 2 * query_rows // width, round_up(seq_count, width) // width


def chunk_rows(pieces):
    parts = []
    width = pieces[0].shape[1] // PAGE
    for u in range(PAGE):
        for piece in pieces:
            parts.append(piece[:, u * width : (u + 1) * width])
    return jnp.concatenate(parts, axis=0)


def chunk_places(source, facts_ref, slots, rows, tokens, shared):
    seq_count, width = slots.shape[1], facts_ref.shape[1]
    pages = tokens // PAGE
    extra = rows - pages
    if shared is None:
        spot = lax.broadcasted_iota(jnp.int32, (pages, seq_count), 0) * seq_count + source
        low = slots * pages
        held = jnp.where(jnp.logical_and(spot >= low, spot < low + pages), 1.0, 0.0)
        shared = jnp.dot(
            held, facts_ref[:seq_count, :], precision=lax.Precision.HIGHEST, preferred_element_type=f32
        )
    spot = lax.broadcasted_iota(jnp.int32, (pages, 1), 0) * seq_count + source
    spot = spot.astype(f32)
    page = spot - pages * jnp.floor((spot + 0.5) * (1.0 / pages))
    begin = shared[:, width - 1 :] - tokens + page * PAGE
    holder = jnp.floor(shared * (1.0 / PAGE))
    bits = jnp.where(holder == page, jnp.exp2(shared - PAGE * holder), 0.0)
    bits = jnp.sum(bits, axis=1, keepdims=True).astype(jnp.int32)
    row = jnp.broadcast_to(facts_ref[pl.ds(source, 1), :], (extra * PAGE, width))
    same = lax.broadcasted_iota(jnp.int32, row.shape, 0) == lax.broadcasted_iota(
        jnp.int32, row.shape, 1
    )
    fresh = jnp.sum(jnp.where(same, row, 0.0), axis=1, keepdims=True)
    fresh = fresh + (source * tokens).astype(f32)
    parts = []
    for u in range(PAGE):
        parts.append(jnp.where(((bits >> u) & 1) == 1, FAR, begin + u))
        parts.append(fresh[u * extra : (u + 1) * extra, :])
    return jnp.concatenate(parts, axis=0), shared


def visit_kernel(seq_count, tokens, steps, layout, first, last, *refs):
    piece_count = sum(layout)
    pieces = refs[:piece_count]
    own_q, other_q, facts_ref, wanted_ref = refs[piece_count : piece_count + 4]
    refs = refs[piece_count + 4 :]
    if not first:
        old_ref, old_pages_ref = refs[:2]
        refs = refs[2:]
    head_dim = own_q.shape[1]
    factor = float(head_dim**-0.5 * np.log2(np.e))
    chips = seq_count // 2
    pages = tokens // PAGE
    me = lax.axis_index("seq")
    core, here = me % 2, ring_place(me // 2, chips)
    table_rows, limit_rows, slot_rows = fact_rows(seq_count, own_q.shape[0], facts_ref.shape[1])
    limit = get_rows(facts_ref, table_rows, limit_rows)
    slots = get_rows(facts_ref, table_rows + limit_rows, slot_rows)[:, :seq_count].astype(jnp.int32)
    blocks, places, at, shared = [], [], 0, None
    for step, count in zip(steps, layout):
        source = ring_chip((here - step + chips) % chips, chips) * 2 + core
        group = pieces[at : at + count]
        at += count
        rows = sum(piece.shape[0] for piece in group)
        if pages % seq_count:
            shared = None
        found, shared = chunk_places(source, facts_ref, slots, rows, tokens, shared)
        places.append(found)
        blocks.append(chunk_rows(group))
    blended = jnp.concatenate(blocks, axis=0) if len(blocks) > 1 else blocks[0]
    place = jnp.concatenate(places, axis=0) if len(places) > 1 else places[0]
    queries = jnp.concatenate([own_q[...], other_q[...]], axis=0)
    flipped = blended.T

    scores = lax.dot_general(
        blended[:, :head_dim], queries, (((1,), (1,)), ((), ())), preferred_element_type=f32
    )
    scores = jnp.where(place <= limit, scores, MASKED)
    peak = jnp.max(scores, axis=0, keepdims=True)
    if first:
        new_peak = jnp.maximum(peak, LOWEST)
    else:
        old_peak = old_ref[head_dim : head_dim + 1, :]
        new_peak = jnp.maximum(peak, old_peak)
        fade = jnp.exp2((old_peak - new_peak) * factor)
    weights = jnp.exp2((scores - new_peak) * factor)
    total = jnp.sum(weights, axis=0, keepdims=True)
    mixed = jnp.dot(flipped[head_dim:, :], weights.astype(bf16), preferred_element_type=f32)
    chosen = jnp.where(place == wanted_ref[...], 1.0, 0.0).astype(bf16)
    picked = jnp.dot(flipped, chosen, preferred_element_type=f32)
    if not first:
        total = total + old_ref[head_dim + 1 : head_dim + 2, :] * fade
        mixed = mixed + old_ref[:head_dim, :] * fade
        picked = picked + old_pages_ref[...].astype(f32)
    picked = picked.astype(bf16)
    count = mixed.shape[1]
    tail = jnp.concatenate([new_peak, total, jnp.zeros((6, count), f32)], axis=0)
    if not last:
        new_ref, new_pages_ref = refs
        new_ref[:head_dim, :] = mixed
        new_ref[head_dim:, :] = tail
        new_pages_ref[...] = picked
    else:
        mine_ref, my_pages_ref, theirs_ref, their_pages_ref = refs
        half = count // 2
        mine_ref[:head_dim, :] = mixed[:, :half]
        mine_ref[head_dim:, :] = tail[:, :half]
        theirs_ref[:head_dim, :] = pltpu.roll(mixed, half, 1)[:, :half]
        theirs_ref[head_dim:, :] = pltpu.roll(tail, half, 1)[:, :half]
        wide = picked.shape[1] // 2
        my_pages_ref[...] = picked[:, :wide]
        their_pages_ref[...] = picked[:, wide:]


def join_kernel(mine_ref, my_pages_ref, got_ref, got_pages_ref, out_ref, pages_ref):
    head_dim = mine_ref.shape[0] - 8
    factor = float(head_dim**-0.5 * np.log2(np.e))
    peaks = [ref[head_dim : head_dim + 1, :] for ref in (mine_ref, got_ref)]
    top = jnp.maximum(peaks[0], peaks[1])
    fades = [jnp.exp2((peak - top) * factor) for peak in peaks]
    total = (
        mine_ref[head_dim + 1 : head_dim + 2, :] * fades[0]
        + got_ref[head_dim + 1 : head_dim + 2, :] * fades[1]
    )
    mixed = (mine_ref[:head_dim, :] * fades[0] + got_ref[:head_dim, :] * fades[1]) / total
    flat = mixed.T
    sel = out_ref.shape[0]
    for h in range(GROUP):
        out_ref[:, h * head_dim : (h + 1) * head_dim] = flat[h * sel : (h + 1) * sel, :].astype(
            bf16
        )
    pages = (my_pages_ref[...].astype(f32) + got_pages_ref[...].astype(f32)).T
    count = pages_ref.shape[0]
    pair = 2 * head_dim
    for u in range(PAGE):
        pages_ref[:, u * pair : (u + 1) * pair] = pages[u * count : (u + 1) * count, :].astype(
            bf16
        )


def shards(
    pool_kv, pool_slot, passage_order, passage_start, recompute_pos, page_table, fresh_q, fresh_kv
):
    seq_count = lax.axis_size("seq")
    chips = seq_count // 2
    me = lax.axis_index("seq")
    pages, width = pool_kv.shape
    sel = fresh_q.shape[0]
    head_dim = fresh_kv.shape[1] // 2
    tokens = pages * PAGE
    extra = round_up(-(-sel // PAGE), TILE)
    rows = pages + extra
    query_rows = sel * GROUP
    vmem = pl.BlockSpec(memory_space=pltpu.VMEM)
    params = pltpu.CompilerParams(vmem_limit_bytes=40 * 2**20)

    anywhere = pl.BlockSpec(memory_space=pltpu.HBM)
    frequency = jnp.asarray(frequencies(head_dim))

    def gathered(kernel, in_smem, in_vmem, out_shape, scratch, name):
        operands = [
            pltpu.with_memory_space_constraint(x, pltpu.HBM) for x in (*in_smem, *in_vmem)
        ]
        return pl.pallas_call(
            kernel,
            out_shape=out_shape,
            in_specs=[anywhere] * len(operands),
            out_specs=jax.tree.map(lambda _: vmem, out_shape),
            scratch_shapes=[
                *[pltpu.SMEM(x.shape, x.dtype) for x in in_smem],
                *[pltpu.VMEM(x.shape, x.dtype) for x in in_vmem],
                scratch,
                pltpu.SemaphoreType.DMA((len(operands),)),
            ],
            compiler_params=params,
            cost_estimate=pl.CostEstimate(
                flops=10**8, bytes_accessed=6 * 2**20, transcendentals=0
            ),
            name=name,
        )(*operands)

    chunk = gathered(
        partial(prep_kernel, seq_count),
        [pool_slot, passage_order, passage_start],
        [frequency, recompute_pos, fresh_kv, pool_kv],
        jax.ShapeDtypeStruct((rows, width), bf16),
        pltpu.VMEM((extra * PAGE, 2 * head_dim), f32),
        "prepare",
    )
    fact_width = round_up(sel + 1, LANES)
    fact_count = sum(fact_rows(seq_count, query_rows, fact_width))
    queries, facts = gathered(
        partial(plan_kernel, seq_count, tokens),
        [pool_slot, passage_order, passage_start],
        [frequency, recompute_pos, fresh_q],
        (
            jax.ShapeDtypeStruct((query_rows, head_dim), bf16),
            jax.ShapeDtypeStruct((round_up(fact_count, 8), fact_width), f32),
        ),
        pltpu.VMEM((query_rows, head_dim), f32),
        "plan",
    )

    pair = jnp.stack([me, me ^ 1])
    page_ids = jnp.arange(pages, dtype=jnp.int32)
    request_pages = jnp.arange(page_table.shape[0], dtype=jnp.int32)
    owned = pair[:, None] * pages + page_ids[None, :]
    wanted = jnp.sum(
        jnp.where(page_table[None, None, :] == owned[:, :, None], request_pages[None, None, :], 0),
        axis=2,
    )
    wanted = wanted[:, None, :] * PAGE + jnp.arange(PAGE, dtype=jnp.int32)[None, :, None]
    wanted = wanted.astype(f32).reshape(1, 2 * tokens)

    swap = [(i, i ^ 1) for i in range(seq_count)]
    forward, backward = ring_pairs(chips, 1), ring_pairs(chips, -1)
    other_queries = lax.ppermute(queries, "seq", swap)

    state_shapes = (
        jax.ShapeDtypeStruct((head_dim + 8, 2 * query_rows), f32),
        jax.ShapeDtypeStruct((2 * head_dim, 2 * tokens), bf16),
    )
    last_shapes = (
        jax.ShapeDtypeStruct((head_dim + 8, query_rows), f32),
        jax.ShapeDtypeStruct((2 * head_dim, tokens), bf16),
    ) * 2

    def visit(state, arrivals, last=False):
        steps = [step for step, _ in arrivals]
        layout = [len(pieces) for _, pieces in arrivals]
        pieces = [piece for _, group in arrivals for piece in group]
        first = state is None
        operands = [*pieces, queries, other_queries, facts, wanted]
        aliases = {}
        if not first:
            if not last:
                aliases = {len(operands): 0, len(operands) + 1: 1}
            operands += list(state)
        keys = PAGE * rows * len(steps)
        return pl.pallas_call(
            partial(visit_kernel, seq_count, tokens, steps, layout, first, last),
            out_shape=last_shapes if last else state_shapes,
            in_specs=[vmem] * len(operands),
            out_specs=(vmem,) * (4 if last else 2),
            input_output_aliases=aliases,
            compiler_params=params,
            cost_estimate=pl.CostEstimate(
                flops=4 * keys * head_dim * (2 * query_rows + 2 * tokens),
                bytes_accessed=4 * 2**20,
                transcendentals=keys * 2 * query_rows,
            ),
            name="visit",
        )(*operands)

    state = None
    ahead = behind = chunk
    arrivals = [(0, [chunk])]
    for step in range(1, chips // 2):
        ahead = lax.ppermute(ahead, "seq", forward)
        behind = lax.ppermute(behind, "seq", backward)
        state = visit(state, arrivals)
        ahead, state = lax.optimization_barrier((ahead, state))
        arrivals = [(step, [ahead]), (-step, [behind])]
    cut = round_up(rows // 2, TILE)
    upper = lax.ppermute(ahead[:cut], "seq", forward)
    lower = lax.ppermute(behind[cut:], "seq", backward)
    state = visit(state, arrivals)
    mine, my_pages, theirs, their_pages = visit(state, [(chips // 2, [upper, lower])], last=True)
    got = lax.ppermute(theirs, "seq", swap)
    got_pages = lax.ppermute(their_pages, "seq", swap)
    return pl.pallas_call(
        join_kernel,
        out_shape=(
            jax.ShapeDtypeStruct((sel, GROUP * head_dim), bf16),
            jax.ShapeDtypeStruct((pages, width), bf16),
        ),
        in_specs=[vmem] * 4,
        out_specs=(vmem, vmem),
        compiler_params=params,
        name="join",
    )(mine, my_pages, got, got_pages)


def solution(mesh):
    placed = (
        P(("groups", "seq"), None),
        P("groups"),
        P("groups"),
        P("groups"),
        P("groups", None),
        P("groups"),
        P(("groups", "seq"), None),
        P(("groups", "seq"), None),
    )
    return jax.shard_map(
        shards,
        mesh=mesh,
        in_specs=placed,
        out_specs=(P(("groups", "seq"), None), P(("groups", "seq"), None)),
        check_vma=False,
    )
```

```python
from functools import partial

import jax
import jax.numpy as jnp
import numpy as np
from jax import lax
from jax.experimental import pallas as pl
from jax.experimental.pallas import tpu as pltpu
from jax.sharding import PartitionSpec as P

GROUP = 8
PAGE = 4
ROPE_BASE = 500000.0
FAR = float(2**23)
MASKED = -1e30
LOWEST = -1e29
TILE = 16
LANES = 128

QUARTER = (1.5703125, 253 * 2.0**-19, 170 * 2.0**-27, float(np.pi / 2 - 1.5703125 - 253 * 2.0**-19 - 170 * 2.0**-27))

f32 = jnp.float32
bf16 = jnp.bfloat16


def round_up(value, step):
    return -(-value // step) * step


def frequencies(head_dim):
    half = head_dim // 2
    index = np.arange(half, dtype=np.float32) * np.float32(2.0 / head_dim)
    one = np.power(np.float32(ROPE_BASE), -index).astype(np.float32)
    return np.concatenate([one, one])[None, :]


def ring_place(chip, chips):
    return jnp.where(chip % 2 == 0, chip // 2, chips - 1 - chip // 2)


def ring_chip(place, chips):
    return jnp.where(place < chips // 2, 2 * place, 2 * (chips - 1 - place) + 1)


def ring_order(chips):
    return list(range(0, chips, 2)) + list(range(chips - 1, 0, -2))


def ring_pairs(chips, shift):
    order = ring_order(chips)
    return [
        (order[p] * 2 + core, order[(p + shift) % chips] * 2 + core)
        for p in range(chips)
        for core in range(2)
    ]


def turned(vector, cosine, signed_sine):
    half = vector.shape[1] // 2
    return vector * cosine + pltpu.roll(vector, half, 1) * signed_sine


def cos_sin(angle):
    turns = jnp.round(angle * float(2 / np.pi))
    rest = angle
    for part in QUARTER:
        rest = rest - turns * part
    square = rest * rest
    sine = rest + rest * square * (
        -1.6666654611e-1 + square * (8.3321608736e-3 - square * 1.9515295891e-4)
    )
    cosine = (
        1.0
        - 0.5 * square
        + square
        * square
        * (4.166664568298827e-2 + square * (-1.388731625493765e-3 + square * 2.443315711809948e-5))
    )
    quadrant = turns.astype(jnp.int32) & 3
    odd = (quadrant & 1) == 1
    cos_value = jnp.where(odd, sine, cosine)
    sin_value = jnp.where(odd, cosine, sine)
    cos_value = jnp.where((quadrant == 1) | (quadrant == 2), -cos_value, cos_value)
    sin_value = jnp.where(quadrant >= 2, -sin_value, sin_value)
    return cos_value, sin_value


def rotation(angle):
    head_dim = angle.shape[1]
    cosine, sine = cos_sin(angle)
    lower = lax.broadcasted_iota(jnp.int32, angle.shape, 1) < head_dim // 2
    return cosine, jnp.where(lower, -sine, sine)


def fresh_rotation(row, start, frequency):
    sel = row.shape[1]
    wide = jnp.broadcast_to(row.astype(f32), (sel, sel))
    same = lax.broadcasted_iota(jnp.int32, (sel, sel), 0) == lax.broadcasted_iota(
        jnp.int32, (sel, sel), 1
    )
    picked = jnp.sum(jnp.where(same, wide, 0.0), axis=1, keepdims=True)
    return rotation((picked + start.astype(f32)) * frequency)


def fetch(sources, targets, sems):
    copies = [
        pltpu.make_async_copy(source, target, sems.at[i])
        for i, (source, target) in enumerate(zip(sources, targets))
    ]
    for copy in copies:
        copy.start()
    return copies


def prep_kernel(seq_count, *refs):
    sources, (chunk_ref,), targets = refs[:7], refs[7:8], refs[8:15]
    fresh_ref, sems = refs[15:]
    copies = fetch(sources, targets, sems)
    slot_ref, order_ref, start_ref, freq_ref, picked_ref, kv_ref, pool_ref = targets
    pages = pool_ref.shape[0]
    sel = kv_ref.shape[0]
    head_dim = freq_ref.shape[1]
    pair = 2 * head_dim
    extra = chunk_ref.shape[0] - pages
    me = lax.axis_index("seq")
    spot = lax.broadcasted_iota(jnp.int32, (pages, head_dim), 0) * seq_count + me
    for copy in copies[:-1]:
        copy.wait()

    def place(k, start):
        low = slot_ref[order_ref[k]] * pages
        return jnp.where(jnp.logical_and(spot >= low, spot < low + pages), start_ref[k], start)

    start = lax.fori_loop(0, seq_count, place, jnp.zeros((pages, head_dim), jnp.int32), unroll=16)
    cosine, sine = fresh_rotation(picked_ref[pl.ds(me, 1), :], start_ref[me], freq_ref[...])
    fresh_ref[sel:, :] = jnp.zeros((fresh_ref.shape[0] - sel, pair), f32)
    fresh_ref[:sel, :head_dim] = turned(kv_ref[:, :head_dim].astype(f32), cosine, sine)
    fresh_ref[:sel, head_dim:] = kv_ref[:, head_dim:].astype(f32)
    for u in range(PAGE):
        chunk_ref[pages:, u * pair : (u + 1) * pair] = fresh_ref[
            u * extra : (u + 1) * extra, :
        ].astype(bf16)

    cosine, sine = rotation(start.astype(f32) * freq_ref[...])
    copies[-1].wait()
    for u in range(PAGE):
        keys = slice(u * pair, u * pair + head_dim)
        values = slice(u * pair + head_dim, (u + 1) * pair)
        chunk_ref[:pages, keys] = turned(pool_ref[:, keys].astype(f32), cosine, sine).astype(bf16)
        chunk_ref[:pages, values] = pool_ref[:, values]


def plan_kernel(seq_count, tokens, *refs):
    sources, (queries_ref, facts_ref), targets = refs[:6], refs[6:8], refs[8:14]
    heads_ref, sems = refs[14:]
    for copy in fetch(sources, targets, sems):
        copy.wait()
    slot_ref, order_ref, start_ref, freq_ref, picked_ref, q_ref = targets
    me = lax.axis_index("seq")
    sel = q_ref.shape[0]
    head_dim = freq_ref.shape[1]

    row = picked_ref[pl.ds(me, 1), :]
    cosine, sine = fresh_rotation(row, start_ref[me], freq_ref[...])
    for h in range(GROUP):
        head = q_ref[:, h * head_dim : (h + 1) * head_dim].astype(f32)
        heads_ref[h * sel : (h + 1) * sel, :] = turned(head, cosine, sine)
    queries_ref[...] = heads_ref[...].astype(bf16)

    other = me + 1 - 2 * (me % 2)
    ours = (row + me * tokens).astype(f32)
    theirs = (picked_ref[pl.ds(other, 1), :] + other * tokens).astype(f32)
    both = jnp.concatenate([ours] * GROUP + [theirs] * GROUP, axis=1)
    at = put_rows(facts_ref, seq_count, both)

    shape = (seq_count, facts_ref.shape[1])
    lanes = lax.broadcasted_iota(jnp.int32, shape, 1)
    passages = lax.broadcasted_iota(jnp.int32, shape, 0)
    begin = ((passages + 1) * tokens).astype(f32)
    facts_ref[:seq_count, :] = jnp.where(lanes == shape[1] - 1, begin, FAR)
    facts_ref[:seq_count, :sel] = picked_ref[...].astype(f32)

    lanes = lax.broadcasted_iota(jnp.int32, (1, round_up(seq_count, shape[1])), 1)

    def slot(k, row):
        return jnp.where(lanes == k, slot_ref[order_ref[k]], row)

    slots = lax.fori_loop(0, seq_count, slot, jnp.zeros(lanes.shape, jnp.int32), unroll=16)
    put_rows(facts_ref, at, slots.astype(f32))


def put_rows(ref, at, row):
    width = ref.shape[1]
    for i in range(row.shape[1] // width):
        ref[at + i : at + i + 1, :] = row[:, i * width : (i + 1) * width]
    return at + row.shape[1] // width


def get_rows(ref, at, count):
    return jnp.concatenate([ref[at + i : at + i + 1, :] for i in range(count)], axis=1)


def fact_rows(seq_count, query_rows, width):
    return seq_count, 2 * query_rows // width, round_up(seq_count, width) // width


def chunk_rows(pieces):
    parts = []
    width = pieces[0].shape[1] // PAGE
    for u in range(PAGE):
        for piece in pieces:
            parts.append(piece[:, u * width : (u + 1) * width])
    return jnp.concatenate(parts, axis=0)


def chunk_places(source, facts_ref, slots, rows, tokens, shared):
    seq_count, width = slots.shape[1], facts_ref.shape[1]
    pages = tokens // PAGE
    extra = rows - pages
    if shared is None:
        spot = lax.broadcasted_iota(jnp.int32, (pages, seq_count), 0) * seq_count + source
        low = slots * pages
        held = jnp.where(jnp.logical_and(spot >= low, spot < low + pages), 1.0, 0.0)
        shared = jnp.dot(
            held, facts_ref[:seq_count, :], precision=lax.Precision.HIGHEST, preferred_element_type=f32
        )
    spot = lax.broadcasted_iota(jnp.int32, (pages, 1), 0) * seq_count + source
    spot = spot.astype(f32)
    page = spot - pages * jnp.floor((spot + 0.5) * (1.0 / pages))
    begin = shared[:, width - 1 :] - tokens + page * PAGE
    holder = jnp.floor(shared * (1.0 / PAGE))
    bits = jnp.where(holder == page, jnp.exp2(shared - PAGE * holder), 0.0)
    bits = jnp.sum(bits, axis=1, keepdims=True).astype(jnp.int32)
    row = jnp.broadcast_to(facts_ref[pl.ds(source, 1), :], (extra * PAGE, width))
    same = lax.broadcasted_iota(jnp.int32, row.shape, 0) == lax.broadcasted_iota(
        jnp.int32, row.shape, 1
    )
    fresh = jnp.sum(jnp.where(same, row, 0.0), axis=1, keepdims=True)
    fresh = fresh + (source * tokens).astype(f32)
    parts = []
    for u in range(PAGE):
        parts.append(jnp.where(((bits >> u) & 1) == 1, FAR, begin + u))
        parts.append(fresh[u * extra : (u + 1) * extra, :])
    return jnp.concatenate(parts, axis=0), shared


def read_chunks(seq_count, tokens, arrivals, core, pieces, facts_ref, query_rows):
    chips = seq_count // 2
    here = ring_place(lax.axis_index("seq") // 2, chips)
    table_rows, limit_rows, slot_rows = fact_rows(seq_count, query_rows, facts_ref.shape[1])
    limit = get_rows(facts_ref, table_rows, limit_rows)
    slots = get_rows(facts_ref, table_rows + limit_rows, slot_rows)[:, :seq_count].astype(jnp.int32)
    blocks, places, at, shared = [], [], 0, None
    for step, count in arrivals:
        source = ring_chip((here - step + chips) % chips, chips) * 2 + core
        group = pieces[at : at + count]
        at += count
        rows = sum(piece.shape[0] for piece in group)
        if (tokens // PAGE) % seq_count:
            shared = None
        found, shared = chunk_places(source, facts_ref, slots, rows, tokens, shared)
        places.append(found)
        blocks.append(chunk_rows(group))
    blended = jnp.concatenate(blocks, axis=0) if len(blocks) > 1 else blocks[0]
    place = jnp.concatenate(places, axis=0) if len(places) > 1 else places[0]
    return blended, place, limit


def score_factor(head_dim):
    return float(head_dim**-0.5 * np.log2(np.e))


def attend(blended, place, queries, limit, wanted, old):
    head_dim = queries.shape[1]
    factor = score_factor(head_dim)
    flipped = blended.T
    scores = lax.dot_general(
        blended[:, :head_dim], queries, (((1,), (1,)), ((), ())), preferred_element_type=f32
    )
    scores = jnp.where(place <= limit, scores, MASKED)
    peak = jnp.maximum(jnp.max(scores, axis=0, keepdims=True), LOWEST if old is None else old[0])
    weights = jnp.exp2((scores - peak) * factor)
    total = jnp.sum(weights, axis=0, keepdims=True)
    mixed = jnp.dot(flipped[head_dim:, :], weights.astype(bf16), preferred_element_type=f32)
    chosen = jnp.where(place == wanted, 1.0, 0.0).astype(bf16)
    picked = jnp.dot(flipped, chosen, preferred_element_type=f32)
    if old is not None:
        fade = jnp.exp2((old[0] - peak) * factor)
        total = total + old[1] * fade
        mixed = mixed + old[2] * fade
        picked = picked + old[3]
    return peak, total, mixed, picked


def get_state(ref, pages_ref):
    head_dim = ref.shape[0] - 8
    peak = ref[head_dim : head_dim + 1, :]
    total = ref[head_dim + 1 : head_dim + 2, :]
    return peak, total, ref[:head_dim, :], pages_ref[...].astype(f32)


def put_state(state, half, ref, pages_ref):
    peak, total, mixed, picked = state
    head_dim = mixed.shape[0]
    tail = jnp.concatenate([peak, total, jnp.zeros((6, peak.shape[1]), f32)], axis=0)
    count, wide = ref.shape[1], pages_ref.shape[1]
    if half == 1:
        mixed, tail = pltpu.roll(mixed, count, 1), pltpu.roll(tail, count, 1)
        picked = picked[:, wide:]
    ref[:head_dim, :] = mixed[:, :count]
    ref[head_dim:, :] = tail[:, :count]
    pages_ref[...] = picked[:, :wide].astype(bf16)


def visit_kernel(seq_count, tokens, arrivals, first, last, *refs):
    piece_count = sum(count for _, count in arrivals)
    pieces = refs[:piece_count]
    own_q, other_q, facts_ref, wanted_ref = refs[piece_count : piece_count + 4]
    refs = refs[piece_count + 4 :]
    old = None
    if not first:
        old = get_state(*refs[:2])
        refs = refs[2:]
    core = lax.axis_index("seq") % 2
    blended, place, limit = read_chunks(
        seq_count, tokens, arrivals, core, pieces, facts_ref, own_q.shape[0]
    )
    queries = jnp.concatenate([own_q[...], other_q[...]], axis=0)
    state = attend(blended, place, queries, limit, wanted_ref[...], old)
    put_state(state, 0, *refs[:2])
    if last:
        put_state(state, 1, *refs[2:])


def merged(one, two, factor):
    peak = jnp.maximum(one[0], two[0])
    fades = [jnp.exp2((part[0] - peak) * factor) for part in (one, two)]
    return [peak] + [one[i] * fades[0] + two[i] * fades[1] for i in (1, 2)] + [one[3] + two[3]]


def close_kernel(seq_count, tokens, arrivals, *refs):
    pieces = refs[: len(refs) - 7]
    own_q, facts_ref, wanted_ref, mine, my_pages, new, new_pages = refs[-7:]
    core = lax.axis_index("seq") % 2
    query_rows = own_q.shape[0]
    blended, place, limit = read_chunks(
        seq_count, tokens, arrivals, core, pieces, facts_ref, query_rows
    )
    wanted = wanted_ref[:, :tokens]
    old = get_state(mine, my_pages)
    state = attend(blended, place, own_q[...], limit[:, :query_rows], wanted, old)
    put_state(state, 0, new, new_pages)


def finish_kernel(seq_count, tokens, arrivals, *refs):
    pieces = refs[: len(refs) - 9]
    own_q, facts_ref, wanted_ref, mine, my_pages, got, got_pages, out_ref, pages_ref = refs[-9:]
    core = 1 - lax.axis_index("seq") % 2
    query_rows, head_dim = own_q.shape
    blended, place, limit = read_chunks(
        seq_count, tokens, arrivals, core, pieces, facts_ref, query_rows
    )
    wanted = wanted_ref[:, :tokens]
    old = merged(get_state(mine, my_pages), get_state(got, got_pages), score_factor(head_dim))
    _, total, mixed, picked = attend(
        blended, place, own_q[...], limit[:, :query_rows], wanted, old
    )
    flat = (mixed / total).T
    sel = out_ref.shape[0]
    for h in range(GROUP):
        out_ref[:, h * head_dim : (h + 1) * head_dim] = flat[h * sel : (h + 1) * sel, :].astype(
            bf16
        )
    pages = picked.T
    count = pages_ref.shape[0]
    pair = 2 * head_dim
    for u in range(PAGE):
        pages_ref[:, u * pair : (u + 1) * pair] = pages[u * count : (u + 1) * count, :].astype(
            bf16
        )


def shards(
    pool_kv, pool_slot, passage_order, passage_start, recompute_pos, page_table, fresh_q, fresh_kv
):
    seq_count = lax.axis_size("seq")
    chips = seq_count // 2
    me = lax.axis_index("seq")
    pages, width = pool_kv.shape
    sel = fresh_q.shape[0]
    head_dim = fresh_kv.shape[1] // 2
    tokens = pages * PAGE
    extra = round_up(-(-sel // PAGE), TILE)
    rows = pages + extra
    query_rows = sel * GROUP
    vmem = pl.BlockSpec(memory_space=pltpu.VMEM)
    params = pltpu.CompilerParams(vmem_limit_bytes=40 * 2**20)

    anywhere = pl.BlockSpec(memory_space=pltpu.HBM)
    frequency = jnp.asarray(frequencies(head_dim))

    def gathered(kernel, in_smem, in_vmem, out_shape, scratch, name):
        operands = [
            pltpu.with_memory_space_constraint(x, pltpu.HBM) for x in (*in_smem, *in_vmem)
        ]
        return pl.pallas_call(
            kernel,
            out_shape=out_shape,
            in_specs=[anywhere] * len(operands),
            out_specs=jax.tree.map(lambda _: vmem, out_shape),
            scratch_shapes=[
                *[pltpu.SMEM(x.shape, x.dtype) for x in in_smem],
                *[pltpu.VMEM(x.shape, x.dtype) for x in in_vmem],
                scratch,
                pltpu.SemaphoreType.DMA((len(operands),)),
            ],
            compiler_params=params,
            cost_estimate=pl.CostEstimate(
                flops=10**8, bytes_accessed=6 * 2**20, transcendentals=0
            ),
            name=name,
        )(*operands)

    chunk = gathered(
        partial(prep_kernel, seq_count),
        [pool_slot, passage_order, passage_start],
        [frequency, recompute_pos, fresh_kv, pool_kv],
        jax.ShapeDtypeStruct((rows, width), bf16),
        pltpu.VMEM((extra * PAGE, 2 * head_dim), f32),
        "prepare",
    )
    fact_width = round_up(sel + 1, LANES)
    fact_count = sum(fact_rows(seq_count, query_rows, fact_width))
    queries, facts = gathered(
        partial(plan_kernel, seq_count, tokens),
        [pool_slot, passage_order, passage_start],
        [frequency, recompute_pos, fresh_q],
        (
            jax.ShapeDtypeStruct((query_rows, head_dim), bf16),
            jax.ShapeDtypeStruct((round_up(fact_count, 8), fact_width), f32),
        ),
        pltpu.VMEM((query_rows, head_dim), f32),
        "plan",
    )

    pair = jnp.stack([me, me ^ 1])
    page_ids = jnp.arange(pages, dtype=jnp.int32)
    request_pages = jnp.arange(page_table.shape[0], dtype=jnp.int32)
    owned = pair[:, None] * pages + page_ids[None, :]
    wanted = jnp.sum(
        jnp.where(page_table[None, None, :] == owned[:, :, None], request_pages[None, None, :], 0),
        axis=2,
    )
    wanted = wanted[:, None, :] * PAGE + jnp.arange(PAGE, dtype=jnp.int32)[None, :, None]
    wanted = wanted.astype(f32).reshape(1, 2 * tokens)

    swap = [(i, i ^ 1) for i in range(seq_count)]
    forward, backward = ring_pairs(chips, 1), ring_pairs(chips, -1)
    other_queries = lax.ppermute(queries, "seq", swap)

    state_shapes = (
        jax.ShapeDtypeStruct((head_dim + 8, 2 * query_rows), f32),
        jax.ShapeDtypeStruct((2 * head_dim, 2 * tokens), bf16),
    )
    half_shapes = (
        jax.ShapeDtypeStruct((head_dim + 8, query_rows), f32),
        jax.ShapeDtypeStruct((2 * head_dim, tokens), bf16),
    )
    out_shapes = (
        jax.ShapeDtypeStruct((sel, GROUP * head_dim), bf16),
        jax.ShapeDtypeStruct((pages, width), bf16),
    )

    def run(kernel, arrivals, operands, out_shape, name, aliases=(), weight=1):
        layout = [(step, len(pieces)) for step, pieces in arrivals]
        operands = [piece for _, pieces in arrivals for piece in pieces] + list(operands)
        pairs = PAGE * rows * len(layout) * (query_rows + tokens)
        return pl.pallas_call(
            partial(kernel, seq_count, tokens, layout),
            out_shape=out_shape,
            in_specs=[vmem] * len(operands),
            out_specs=(vmem,) * len(out_shape),
            input_output_aliases={len(operands) - 2 + i: i for i in aliases},
            compiler_params=params,
            cost_estimate=pl.CostEstimate(
                flops=8 * pairs * head_dim * weight,
                bytes_accessed=4 * 2**20 * weight,
                transcendentals=2 * pairs * weight,
            ),
            name=name,
        )(*operands)

    def visit(state, arrivals, last=False):
        operands = [queries, other_queries, facts, wanted]
        first = state is None
        kernel = lambda count, size, layout, *refs: visit_kernel(
            count, size, layout, first, last, *refs
        )
        if not first:
            operands += list(state)
        out_shape = half_shapes * 2 if last else state_shapes
        aliases = () if first or last else (0, 1)
        return run(kernel, arrivals, operands, out_shape, "visit", aliases)

    state = None
    ahead = behind = chunk
    arrivals = [(0, [chunk])]
    for step in range(1, chips // 2):
        ahead = lax.ppermute(ahead, "seq", forward)
        behind = lax.ppermute(behind, "seq", backward)
        state = visit(state, arrivals)
        ahead, state = lax.optimization_barrier((ahead, state))
        arrivals = [(step, [ahead]), (-step, [behind])]
    cut = round_up(rows // 2, TILE)
    upper = lax.ppermute(ahead[:cut], "seq", forward)
    lower = lax.ppermute(behind[cut:], "seq", backward)
    mine, my_pages, theirs, their_pages = visit(state, arrivals, last=True)
    got = lax.ppermute(theirs, "seq", swap)
    got_pages = lax.ppermute(their_pages, "seq", swap)
    farthest = [(chips // 2, [upper, lower])]
    other_farthest = [(chips // 2, [lax.ppermute(piece, "seq", swap) for piece in (upper, lower)])]
    operands = [queries, facts, wanted, mine, my_pages]
    state = run(close_kernel, farthest, operands, half_shapes, "close", weight=10)
    operands = [queries, facts, wanted, *state, got, got_pages]
    return run(finish_kernel, other_farthest, operands, out_shapes, "finish")


def solution(mesh):
    placed = (
        P(("groups", "seq"), None),
        P("groups"),
        P("groups"),
        P("groups"),
        P("groups", None),
        P("groups"),
        P(("groups", "seq"), None),
        P(("groups", "seq"), None),
    )
    return jax.shard_map(
        shards,
        mesh=mesh,
        in_specs=placed,
        out_specs=(P(("groups", "seq"), None), P(("groups", "seq"), None)),
        check_vma=False,
    )
```

```python
from functools import partial

import jax
import jax.numpy as jnp
import numpy as np
from jax import lax
from jax.experimental import pallas as pl
from jax.experimental.pallas import tpu as pltpu
from jax.sharding import PartitionSpec as P

GROUP = 8
PAGE = 4
ROPE_BASE = 500000.0
FAR = float(2**23)
MASKED = -1e30
LOWEST = -1e29
TILE = 16
LANES = 128

QUARTER = (1.5703125, 253 * 2.0**-19, 170 * 2.0**-27, float(np.pi / 2 - 1.5703125 - 253 * 2.0**-19 - 170 * 2.0**-27))

f32 = jnp.float32
bf16 = jnp.bfloat16


def round_up(value, step):
    return -(-value // step) * step


def frequencies(head_dim):
    half = head_dim // 2
    index = np.arange(half, dtype=np.float32) * np.float32(2.0 / head_dim)
    one = np.power(np.float32(ROPE_BASE), -index).astype(np.float32)
    return np.concatenate([one, one])[None, :]


def ring_place(chip, chips):
    return jnp.where(chip % 2 == 0, chip // 2, chips - 1 - chip // 2)


def ring_chip(place, chips):
    return jnp.where(place < chips // 2, 2 * place, 2 * (chips - 1 - place) + 1)


def ring_order(chips):
    return list(range(0, chips, 2)) + list(range(chips - 1, 0, -2))


def ring_pairs(chips, shift):
    order = ring_order(chips)
    return [
        (order[p] * 2 + core, order[(p + shift) % chips] * 2 + core)
        for p in range(chips)
        for core in range(2)
    ]


def turned(vector, cosine, signed_sine):
    half = vector.shape[1] // 2
    return vector * cosine + pltpu.roll(vector, half, 1) * signed_sine


def cos_sin(angle):
    turns = jnp.round(angle * float(2 / np.pi))
    rest = angle
    for part in QUARTER:
        rest = rest - turns * part
    square = rest * rest
    sine = rest + rest * square * (
        -1.6666654611e-1 + square * (8.3321608736e-3 - square * 1.9515295891e-4)
    )
    cosine = (
        1.0
        - 0.5 * square
        + square
        * square
        * (4.166664568298827e-2 + square * (-1.388731625493765e-3 + square * 2.443315711809948e-5))
    )
    quadrant = turns.astype(jnp.int32) & 3
    odd = (quadrant & 1) == 1
    cos_value = jnp.where(odd, sine, cosine)
    sin_value = jnp.where(odd, cosine, sine)
    cos_value = jnp.where((quadrant == 1) | (quadrant == 2), -cos_value, cos_value)
    sin_value = jnp.where(quadrant >= 2, -sin_value, sin_value)
    return cos_value, sin_value


def rotation(angle):
    head_dim = angle.shape[1]
    cosine, sine = cos_sin(angle)
    lower = lax.broadcasted_iota(jnp.int32, angle.shape, 1) < head_dim // 2
    return cosine, jnp.where(lower, -sine, sine)


def fresh_rotation(row, start, frequency):
    sel = row.shape[1]
    wide = jnp.broadcast_to(row.astype(f32), (sel, sel))
    same = lax.broadcasted_iota(jnp.int32, (sel, sel), 0) == lax.broadcasted_iota(
        jnp.int32, (sel, sel), 1
    )
    picked = jnp.sum(jnp.where(same, wide, 0.0), axis=1, keepdims=True)
    return rotation((picked + start.astype(f32)) * frequency)


def fetch(sources, targets, sems):
    copies = [
        pltpu.make_async_copy(source, target, sems.at[i])
        for i, (source, target) in enumerate(zip(sources, targets))
    ]
    for copy in copies:
        copy.start()
    return copies


def prep_kernel(seq_count, *refs):
    sources, (chunk_ref,), targets = refs[:7], refs[7:8], refs[8:15]
    fresh_ref, sems = refs[15:]
    copies = fetch(sources, targets, sems)
    slot_ref, order_ref, start_ref, freq_ref, picked_ref, kv_ref, pool_ref = targets
    pages = pool_ref.shape[0]
    sel = kv_ref.shape[0]
    head_dim = freq_ref.shape[1]
    pair = 2 * head_dim
    extra = chunk_ref.shape[0] - pages
    me = lax.axis_index("seq")
    spot = lax.broadcasted_iota(jnp.int32, (pages, head_dim), 0) * seq_count + me
    for copy in copies[:-1]:
        copy.wait()

    def place(k, start):
        low = slot_ref[order_ref[k]] * pages
        return jnp.where(jnp.logical_and(spot >= low, spot < low + pages), start_ref[k], start)

    start = lax.fori_loop(0, seq_count, place, jnp.zeros((pages, head_dim), jnp.int32), unroll=16)
    cosine, sine = fresh_rotation(picked_ref[pl.ds(me, 1), :], start_ref[me], freq_ref[...])
    fresh_ref[sel:, :] = jnp.zeros((fresh_ref.shape[0] - sel, pair), f32)
    fresh_ref[:sel, :head_dim] = turned(kv_ref[:, :head_dim].astype(f32), cosine, sine)
    fresh_ref[:sel, head_dim:] = kv_ref[:, head_dim:].astype(f32)
    for u in range(PAGE):
        chunk_ref[pages:, u * pair : (u + 1) * pair] = fresh_ref[
            u * extra : (u + 1) * extra, :
        ].astype(bf16)

    cosine, sine = rotation(start.astype(f32) * freq_ref[...])
    copies[-1].wait()
    for u in range(PAGE):
        keys = slice(u * pair, u * pair + head_dim)
        values = slice(u * pair + head_dim, (u + 1) * pair)
        chunk_ref[:pages, keys] = turned(pool_ref[:, keys].astype(f32), cosine, sine).astype(bf16)
        chunk_ref[:pages, values] = pool_ref[:, values]


def plan_kernel(seq_count, tokens, *refs):
    sources, (queries_ref, facts_ref), targets = refs[:6], refs[6:8], refs[8:14]
    heads_ref, sems = refs[14:]
    for copy in fetch(sources, targets, sems):
        copy.wait()
    slot_ref, order_ref, start_ref, freq_ref, picked_ref, q_ref = targets
    me = lax.axis_index("seq")
    sel = q_ref.shape[0]
    head_dim = freq_ref.shape[1]

    row = picked_ref[pl.ds(me, 1), :]
    cosine, sine = fresh_rotation(row, start_ref[me], freq_ref[...])
    for h in range(GROUP):
        head = q_ref[:, h * head_dim : (h + 1) * head_dim].astype(f32)
        heads_ref[h * sel : (h + 1) * sel, :] = turned(head, cosine, sine)
    queries_ref[...] = heads_ref[...].astype(bf16)

    other = me + 1 - 2 * (me % 2)
    ours = (row + me * tokens).astype(f32)
    theirs = (picked_ref[pl.ds(other, 1), :] + other * tokens).astype(f32)
    both = jnp.concatenate([ours] * GROUP + [theirs] * GROUP, axis=1)
    at = put_rows(facts_ref, seq_count, both)

    shape = (seq_count, facts_ref.shape[1])
    lanes = lax.broadcasted_iota(jnp.int32, shape, 1)
    passages = lax.broadcasted_iota(jnp.int32, shape, 0)
    begin = ((passages + 1) * tokens).astype(f32)
    facts_ref[:seq_count, :] = jnp.where(lanes == shape[1] - 1, begin, FAR)
    facts_ref[:seq_count, :sel] = picked_ref[...].astype(f32)

    lanes = lax.broadcasted_iota(jnp.int32, (1, round_up(seq_count, shape[1])), 1)

    def slot(k, row):
        return jnp.where(lanes == k, slot_ref[order_ref[k]], row)

    slots = lax.fori_loop(0, seq_count, slot, jnp.zeros(lanes.shape, jnp.int32), unroll=16)
    put_rows(facts_ref, at, slots.astype(f32))


def put_rows(ref, at, row):
    width = ref.shape[1]
    for i in range(row.shape[1] // width):
        ref[at + i : at + i + 1, :] = row[:, i * width : (i + 1) * width]
    return at + row.shape[1] // width


def get_rows(ref, at, count):
    return jnp.concatenate([ref[at + i : at + i + 1, :] for i in range(count)], axis=1)


def fact_rows(seq_count, query_rows, width):
    return seq_count, 2 * query_rows // width, round_up(seq_count, width) // width


def chunk_rows(pieces):
    parts = []
    width = pieces[0].shape[1] // PAGE
    for u in range(PAGE):
        for piece in pieces:
            parts.append(piece[:, u * width : (u + 1) * width])
    return jnp.concatenate(parts, axis=0)


def chunk_places(source, facts_ref, slots, rows, tokens, shared):
    seq_count, width = slots.shape[1], facts_ref.shape[1]
    pages = tokens // PAGE
    extra = rows - pages
    if shared is None:
        spot = lax.broadcasted_iota(jnp.int32, (pages, seq_count), 0) * seq_count + source
        low = slots * pages
        held = jnp.where(jnp.logical_and(spot >= low, spot < low + pages), 1.0, 0.0)
        shared = jnp.dot(
            held, facts_ref[:seq_count, :], precision=lax.Precision.HIGHEST, preferred_element_type=f32
        )
    spot = lax.broadcasted_iota(jnp.int32, (pages, 1), 0) * seq_count + source
    spot = spot.astype(f32)
    page = spot - pages * jnp.floor((spot + 0.5) * (1.0 / pages))
    begin = shared[:, width - 1 :] - tokens + page * PAGE
    holder = jnp.floor(shared * (1.0 / PAGE))
    bits = jnp.where(holder == page, jnp.exp2(shared - PAGE * holder), 0.0)
    bits = jnp.sum(bits, axis=1, keepdims=True).astype(jnp.int32)
    row = jnp.broadcast_to(facts_ref[pl.ds(source, 1), :], (extra * PAGE, width))
    same = lax.broadcasted_iota(jnp.int32, row.shape, 0) == lax.broadcasted_iota(
        jnp.int32, row.shape, 1
    )
    fresh = jnp.sum(jnp.where(same, row, 0.0), axis=1, keepdims=True)
    fresh = fresh + (source * tokens).astype(f32)
    parts = []
    for u in range(PAGE):
        parts.append(jnp.where(((bits >> u) & 1) == 1, FAR, begin + u))
        parts.append(fresh[u * extra : (u + 1) * extra, :])
    return jnp.concatenate(parts, axis=0), shared


def read_chunks(seq_count, tokens, arrivals, core, pieces, facts_ref, query_rows):
    chips = seq_count // 2
    here = ring_place(lax.axis_index("seq") // 2, chips)
    table_rows, limit_rows, slot_rows = fact_rows(seq_count, query_rows, facts_ref.shape[1])
    limit = get_rows(facts_ref, table_rows, limit_rows)
    slots = get_rows(facts_ref, table_rows + limit_rows, slot_rows)[:, :seq_count].astype(jnp.int32)
    blocks, places, at, shared = [], [], 0, None
    for step, count in arrivals:
        source = ring_chip((here - step + chips) % chips, chips) * 2 + core
        group = pieces[at : at + count]
        at += count
        rows = sum(piece.shape[0] for piece in group)
        if (tokens // PAGE) % seq_count:
            shared = None
        found, shared = chunk_places(source, facts_ref, slots, rows, tokens, shared)
        places.append(found)
        blocks.append(chunk_rows(group))
    blended = jnp.concatenate(blocks, axis=0) if len(blocks) > 1 else blocks[0]
    place = jnp.concatenate(places, axis=0) if len(places) > 1 else places[0]
    return blended, place, limit


def score_factor(head_dim):
    return float(head_dim**-0.5 * np.log2(np.e))


def attend(blended, place, queries, limit, wanted, old):
    head_dim = queries.shape[1]
    factor = score_factor(head_dim)
    flipped = blended.T
    scores = lax.dot_general(
        blended[:, :head_dim], queries, (((1,), (1,)), ((), ())), preferred_element_type=f32
    )
    scores = jnp.where(place <= limit, scores, MASKED)
    peak = jnp.maximum(jnp.max(scores, axis=0, keepdims=True), LOWEST if old is None else old[0])
    weights = jnp.exp2((scores - peak) * factor)
    total = jnp.sum(weights, axis=0, keepdims=True)
    mixed = jnp.dot(flipped[head_dim:, :], weights.astype(bf16), preferred_element_type=f32)
    chosen = jnp.where(place == wanted, 1.0, 0.0).astype(bf16)
    picked = jnp.dot(flipped, chosen, preferred_element_type=f32)
    if old is not None:
        fade = jnp.exp2((old[0] - peak) * factor)
        total = total + old[1] * fade
        mixed = mixed + old[2] * fade
        picked = picked + old[3]
    return peak, total, mixed, picked


def get_state(ref, pages_ref):
    head_dim = ref.shape[0] - 8
    peak = ref[head_dim : head_dim + 1, :]
    total = ref[head_dim + 1 : head_dim + 2, :]
    return peak, total, ref[:head_dim, :], pages_ref[...].astype(f32)


def put_state(state, half, ref, pages_ref):
    peak, total, mixed, picked = state
    head_dim = mixed.shape[0]
    tail = jnp.concatenate([peak, total, jnp.zeros((6, peak.shape[1]), f32)], axis=0)
    count, wide = ref.shape[1], pages_ref.shape[1]
    if half == 1:
        mixed, tail = pltpu.roll(mixed, count, 1), pltpu.roll(tail, count, 1)
        picked = picked[:, wide:]
    ref[:head_dim, :] = mixed[:, :count]
    ref[head_dim:, :] = tail[:, :count]
    pages_ref[...] = picked[:, :wide].astype(bf16)


def visit_kernel(seq_count, tokens, arrivals, first, last, *refs):
    piece_count = sum(count for _, count in arrivals)
    pieces = refs[:piece_count]
    own_q, other_q, facts_ref, wanted_ref = refs[piece_count : piece_count + 4]
    refs = refs[piece_count + 4 :]
    old = None
    if not first:
        old = get_state(*refs[:2])
        refs = refs[2:]
    core = lax.axis_index("seq") % 2
    blended, place, limit = read_chunks(
        seq_count, tokens, arrivals, core, pieces, facts_ref, own_q.shape[0]
    )
    queries = jnp.concatenate([own_q[...], other_q[...]], axis=0)
    state = attend(blended, place, queries, limit, wanted_ref[...], old)
    put_state(state, 0, *refs[:2])
    if last:
        put_state(state, 1, *refs[2:])


def merged(one, two, factor):
    peak = jnp.maximum(one[0], two[0])
    fades = [jnp.exp2((part[0] - peak) * factor) for part in (one, two)]
    return [peak] + [one[i] * fades[0] + two[i] * fades[1] for i in (1, 2)] + [one[3] + two[3]]


def close_kernel(seq_count, tokens, arrivals, *refs):
    pieces = refs[: len(refs) - 7]
    own_q, facts_ref, wanted_ref, mine, my_pages, new, new_pages = refs[-7:]
    core = lax.axis_index("seq") % 2
    query_rows = own_q.shape[0]
    blended, place, limit = read_chunks(
        seq_count, tokens, arrivals, core, pieces, facts_ref, query_rows
    )
    wanted = wanted_ref[:, :tokens]
    old = get_state(mine, my_pages)
    state = attend(blended, place, own_q[...], limit[:, :query_rows], wanted, old)
    put_state(state, 0, new, new_pages)


def finish_kernel(seq_count, tokens, arrivals, *refs):
    pieces = refs[: len(refs) - 9]
    own_q, facts_ref, wanted_ref, mine, my_pages, got, got_pages, out_ref, pages_ref = refs[-9:]
    core = 1 - lax.axis_index("seq") % 2
    query_rows, head_dim = own_q.shape
    blended, place, limit = read_chunks(
        seq_count, tokens, arrivals, core, pieces, facts_ref, query_rows
    )
    wanted = wanted_ref[:, :tokens]
    old = merged(get_state(mine, my_pages), get_state(got, got_pages), score_factor(head_dim))
    _, total, mixed, picked = attend(
        blended, place, own_q[...], limit[:, :query_rows], wanted, old
    )
    flat = (mixed / total).T
    sel = out_ref.shape[0]
    for h in range(GROUP):
        out_ref[:, h * head_dim : (h + 1) * head_dim] = flat[h * sel : (h + 1) * sel, :].astype(
            bf16
        )
    pages = picked.T
    count = pages_ref.shape[0]
    pair = 2 * head_dim
    for u in range(PAGE):
        pages_ref[:, u * pair : (u + 1) * pair] = pages[u * count : (u + 1) * count, :].astype(
            bf16
        )


def shards(
    pool_kv, pool_slot, passage_order, passage_start, recompute_pos, page_table, fresh_q, fresh_kv
):
    seq_count = lax.axis_size("seq")
    chips = seq_count // 2
    me = lax.axis_index("seq")
    pages, width = pool_kv.shape
    sel = fresh_q.shape[0]
    head_dim = fresh_kv.shape[1] // 2
    tokens = pages * PAGE
    extra = round_up(-(-sel // PAGE), TILE)
    rows = pages + extra
    query_rows = sel * GROUP
    vmem = pl.BlockSpec(memory_space=pltpu.VMEM)
    params = pltpu.CompilerParams(vmem_limit_bytes=40 * 2**20)

    anywhere = pl.BlockSpec(memory_space=pltpu.HBM)
    frequency = jnp.asarray(frequencies(head_dim))

    def gathered(kernel, in_smem, in_vmem, out_shape, scratch, name):
        operands = [
            pltpu.with_memory_space_constraint(x, pltpu.HBM) for x in (*in_smem, *in_vmem)
        ]
        return pl.pallas_call(
            kernel,
            out_shape=out_shape,
            in_specs=[anywhere] * len(operands),
            out_specs=jax.tree.map(lambda _: vmem, out_shape),
            scratch_shapes=[
                *[pltpu.SMEM(x.shape, x.dtype) for x in in_smem],
                *[pltpu.VMEM(x.shape, x.dtype) for x in in_vmem],
                scratch,
                pltpu.SemaphoreType.DMA((len(operands),)),
            ],
            compiler_params=params,
            cost_estimate=pl.CostEstimate(
                flops=10**8, bytes_accessed=6 * 2**20, transcendentals=0
            ),
            name=name,
        )(*operands)

    chunk = gathered(
        partial(prep_kernel, seq_count),
        [pool_slot, passage_order, passage_start],
        [frequency, recompute_pos, fresh_kv, pool_kv],
        jax.ShapeDtypeStruct((rows, width), bf16),
        pltpu.VMEM((extra * PAGE, 2 * head_dim), f32),
        "prepare",
    )
    fact_width = round_up(sel + 1, LANES)
    fact_count = sum(fact_rows(seq_count, query_rows, fact_width))
    queries, facts = gathered(
        partial(plan_kernel, seq_count, tokens),
        [pool_slot, passage_order, passage_start],
        [frequency, recompute_pos, fresh_q],
        (
            jax.ShapeDtypeStruct((query_rows, head_dim), bf16),
            jax.ShapeDtypeStruct((round_up(fact_count, 8), fact_width), f32),
        ),
        pltpu.VMEM((query_rows, head_dim), f32),
        "plan",
    )

    pair = jnp.stack([me, me ^ 1])
    page_ids = jnp.arange(pages, dtype=jnp.int32)
    request_pages = jnp.arange(page_table.shape[0], dtype=jnp.int32)
    owned = pair[:, None] * pages + page_ids[None, :]
    wanted = jnp.sum(
        jnp.where(page_table[None, None, :] == owned[:, :, None], request_pages[None, None, :], 0),
        axis=2,
    )
    wanted = wanted[:, None, :] * PAGE + jnp.arange(PAGE, dtype=jnp.int32)[None, :, None]
    wanted = wanted.astype(f32).reshape(1, 2 * tokens)

    swap = [(i, i ^ 1) for i in range(seq_count)]
    forward, backward = ring_pairs(chips, 1), ring_pairs(chips, -1)
    other_queries = lax.ppermute(queries, "seq", swap)

    state_shapes = (
        jax.ShapeDtypeStruct((head_dim + 8, 2 * query_rows), f32),
        jax.ShapeDtypeStruct((2 * head_dim, 2 * tokens), bf16),
    )
    half_shapes = (
        jax.ShapeDtypeStruct((head_dim + 8, query_rows), f32),
        jax.ShapeDtypeStruct((2 * head_dim, tokens), bf16),
    )
    out_shapes = (
        jax.ShapeDtypeStruct((sel, GROUP * head_dim), bf16),
        jax.ShapeDtypeStruct((pages, width), bf16),
    )

    def run(kernel, arrivals, operands, out_shape, name, aliases=(), weight=1):
        layout = [(step, len(pieces)) for step, pieces in arrivals]
        operands = [piece for _, pieces in arrivals for piece in pieces] + list(operands)
        pairs = PAGE * rows * len(layout) * (query_rows + tokens)
        return pl.pallas_call(
            partial(kernel, seq_count, tokens, layout),
            out_shape=out_shape,
            in_specs=[vmem] * len(operands),
            out_specs=(vmem,) * len(out_shape),
            input_output_aliases={len(operands) - 2 + i: i for i in aliases},
            compiler_params=params,
            cost_estimate=pl.CostEstimate(
                flops=8 * pairs * head_dim * weight,
                bytes_accessed=4 * 2**20 * weight,
                transcendentals=2 * pairs * weight,
            ),
            name=name,
        )(*operands)

    def visit(state, arrivals, last=False):
        operands = [queries, other_queries, facts, wanted]
        first = state is None
        kernel = lambda count, size, layout, *refs: visit_kernel(
            count, size, layout, first, last, *refs
        )
        if not first:
            operands += list(state)
        out_shape = half_shapes * 2 if last else state_shapes
        aliases = () if first or last else (0, 1)
        return run(kernel, arrivals, operands, out_shape, "visit", aliases)

    state = None
    ahead = behind = chunk
    arrivals = [(0, [chunk])]
    for step in range(1, chips // 2):
        ahead = lax.ppermute(ahead, "seq", forward)
        behind = lax.ppermute(behind, "seq", backward)
        state = visit(state, arrivals)
        ahead, state = lax.optimization_barrier((ahead, state))
        arrivals = [(step, [ahead]), (-step, [behind])]
    farthest = lax.ppermute(ahead, "seq", forward)
    mine, my_pages, theirs, their_pages = visit(state, arrivals, last=True)
    got = lax.ppermute(theirs, "seq", swap)
    got_pages = lax.ppermute(their_pages, "seq", swap)
    other_farthest = lax.ppermute(farthest, "seq", swap)
    operands = [queries, facts, wanted, mine, my_pages]
    state = run(close_kernel, [(chips // 2, [farthest])], operands, half_shapes, "close", weight=10)
    operands = [queries, facts, wanted, *state, got, got_pages]
    return run(finish_kernel, [(chips // 2, [other_farthest])], operands, out_shapes, "finish")


def solution(mesh):
    placed = (
        P(("groups", "seq"), None),
        P("groups"),
        P("groups"),
        P("groups"),
        P("groups", None),
        P("groups"),
        P(("groups", "seq"), None),
        P(("groups", "seq"), None),
    )
    return jax.shard_map(
        shards,
        mesh=mesh,
        in_specs=placed,
        out_specs=(P(("groups", "seq"), None), P(("groups", "seq"), None)),
        check_vma=False,
    )
```

```python
from functools import partial

import jax
import jax.numpy as jnp
import numpy as np
from jax import lax
from jax.experimental import pallas as pl
from jax.experimental.pallas import tpu as pltpu
from jax.sharding import PartitionSpec as P

GROUP = 8
PAGE = 4
ROPE_BASE = 500000.0
FAR = float(2**23)
MASKED = -1e30
LOWEST = -1e29
TILE = 16
LANES = 128

QUARTER = (1.5703125, 253 * 2.0**-19, 170 * 2.0**-27, float(np.pi / 2 - 1.5703125 - 253 * 2.0**-19 - 170 * 2.0**-27))

f32 = jnp.float32
bf16 = jnp.bfloat16


def round_up(value, step):
    return -(-value // step) * step


def frequencies(head_dim):
    half = head_dim // 2
    index = np.arange(half, dtype=np.float32) * np.float32(2.0 / head_dim)
    one = np.power(np.float32(ROPE_BASE), -index).astype(np.float32)
    return np.concatenate([one, one])[None, :]


def ring_place(chip, chips):
    return jnp.where(chip % 2 == 0, chip // 2, chips - 1 - chip // 2)


def ring_chip(place, chips):
    return jnp.where(place < chips // 2, 2 * place, 2 * (chips - 1 - place) + 1)


def ring_order(chips):
    return list(range(0, chips, 2)) + list(range(chips - 1, 0, -2))


def ring_pairs(chips, shift):
    order = ring_order(chips)
    return [
        (order[p] * 2 + core, order[(p + shift) % chips] * 2 + core)
        for p in range(chips)
        for core in range(2)
    ]


def turned(vector, cosine, signed_sine):
    half = vector.shape[1] // 2
    return vector * cosine + pltpu.roll(vector, half, 1) * signed_sine


def cos_sin(angle):
    turns = jnp.round(angle * float(2 / np.pi))
    rest = angle
    for part in QUARTER:
        rest = rest - turns * part
    square = rest * rest
    sine = rest + rest * square * (
        -1.6666654611e-1 + square * (8.3321608736e-3 - square * 1.9515295891e-4)
    )
    cosine = (
        1.0
        - 0.5 * square
        + square
        * square
        * (4.166664568298827e-2 + square * (-1.388731625493765e-3 + square * 2.443315711809948e-5))
    )
    quadrant = turns.astype(jnp.int32) & 3
    odd = (quadrant & 1) == 1
    cos_value = jnp.where(odd, sine, cosine)
    sin_value = jnp.where(odd, cosine, sine)
    cos_value = jnp.where((quadrant == 1) | (quadrant == 2), -cos_value, cos_value)
    sin_value = jnp.where(quadrant >= 2, -sin_value, sin_value)
    return cos_value, sin_value


def rotation(angle):
    head_dim = angle.shape[1]
    cosine, sine = cos_sin(angle)
    lower = lax.broadcasted_iota(jnp.int32, angle.shape, 1) < head_dim // 2
    return cosine, jnp.where(lower, -sine, sine)


def fresh_rotation(row, start, frequency):
    sel = row.shape[1]
    wide = jnp.broadcast_to(row.astype(f32), (sel, sel))
    same = lax.broadcasted_iota(jnp.int32, (sel, sel), 0) == lax.broadcasted_iota(
        jnp.int32, (sel, sel), 1
    )
    picked = jnp.sum(jnp.where(same, wide, 0.0), axis=1, keepdims=True)
    return rotation((picked + start.astype(f32)) * frequency)


def fetch(sources, targets, sems):
    copies = [
        pltpu.make_async_copy(source, target, sems.at[i])
        for i, (source, target) in enumerate(zip(sources, targets))
    ]
    for copy in copies:
        copy.start()
    return copies


def prep_kernel(seq_count, *refs):
    sources, (chunk_ref,), targets = refs[:7], refs[7:8], refs[8:15]
    fresh_ref, sems = refs[15:]
    copies = fetch(sources, targets, sems)
    slot_ref, order_ref, start_ref, freq_ref, picked_ref, kv_ref, pool_ref = targets
    pages = pool_ref.shape[0]
    sel = kv_ref.shape[0]
    head_dim = freq_ref.shape[1]
    pair = 2 * head_dim
    extra = chunk_ref.shape[0] - pages
    me = lax.axis_index("seq")
    spot = lax.broadcasted_iota(jnp.int32, (pages, head_dim), 0) * seq_count + me
    for copy in copies[:-1]:
        copy.wait()

    def place(k, start):
        low = slot_ref[order_ref[k]] * pages
        return jnp.where(jnp.logical_and(spot >= low, spot < low + pages), start_ref[k], start)

    start = lax.fori_loop(0, seq_count, place, jnp.zeros((pages, head_dim), jnp.int32), unroll=16)
    cosine, sine = fresh_rotation(picked_ref[pl.ds(me, 1), :], start_ref[me], freq_ref[...])
    fresh_ref[sel:, :] = jnp.zeros((fresh_ref.shape[0] - sel, pair), f32)
    fresh_ref[:sel, :head_dim] = turned(kv_ref[:, :head_dim].astype(f32), cosine, sine)
    fresh_ref[:sel, head_dim:] = kv_ref[:, head_dim:].astype(f32)
    for u in range(PAGE):
        chunk_ref[pages:, u * pair : (u + 1) * pair] = fresh_ref[
            u * extra : (u + 1) * extra, :
        ].astype(bf16)

    cosine, sine = rotation(start.astype(f32) * freq_ref[...])
    copies[-1].wait()
    for u in range(PAGE):
        keys = slice(u * pair, u * pair + head_dim)
        values = slice(u * pair + head_dim, (u + 1) * pair)
        chunk_ref[:pages, keys] = turned(pool_ref[:, keys].astype(f32), cosine, sine).astype(bf16)
        chunk_ref[:pages, values] = pool_ref[:, values]


def plan_kernel(seq_count, tokens, *refs):
    sources, (queries_ref, facts_ref), targets = refs[:6], refs[6:8], refs[8:14]
    heads_ref, sems = refs[14:]
    for copy in fetch(sources, targets, sems):
        copy.wait()
    slot_ref, order_ref, start_ref, freq_ref, picked_ref, q_ref = targets
    me = lax.axis_index("seq")
    sel = q_ref.shape[0]
    head_dim = freq_ref.shape[1]

    row = picked_ref[pl.ds(me, 1), :]
    cosine, sine = fresh_rotation(row, start_ref[me], freq_ref[...])
    for h in range(GROUP):
        head = q_ref[:, h * head_dim : (h + 1) * head_dim].astype(f32)
        heads_ref[h * sel : (h + 1) * sel, :] = turned(head, cosine, sine)
    queries_ref[...] = heads_ref[...].astype(bf16)

    other = me + 1 - 2 * (me % 2)
    ours = (row + me * tokens).astype(f32)
    theirs = (picked_ref[pl.ds(other, 1), :] + other * tokens).astype(f32)
    both = jnp.concatenate([ours] * GROUP + [theirs] * GROUP, axis=1)
    at = put_rows(facts_ref, seq_count, both)

    shape = (seq_count, facts_ref.shape[1])
    lanes = lax.broadcasted_iota(jnp.int32, shape, 1)
    passages = lax.broadcasted_iota(jnp.int32, shape, 0)
    begin = ((passages + 1) * tokens).astype(f32)
    facts_ref[:seq_count, :] = jnp.where(lanes == shape[1] - 1, begin, FAR)
    facts_ref[:seq_count, :sel] = picked_ref[...].astype(f32)

    lanes = lax.broadcasted_iota(jnp.int32, (1, round_up(seq_count, shape[1])), 1)

    def slot(k, row):
        return jnp.where(lanes == k, slot_ref[order_ref[k]], row)

    slots = lax.fori_loop(0, seq_count, slot, jnp.zeros(lanes.shape, jnp.int32), unroll=16)
    put_rows(facts_ref, at, slots.astype(f32))


def put_rows(ref, at, row):
    width = ref.shape[1]
    for i in range(row.shape[1] // width):
        ref[at + i : at + i + 1, :] = row[:, i * width : (i + 1) * width]
    return at + row.shape[1] // width


def get_rows(ref, at, count):
    return jnp.concatenate([ref[at + i : at + i + 1, :] for i in range(count)], axis=1)


def fact_rows(seq_count, query_rows, width):
    return seq_count, 2 * query_rows // width, round_up(seq_count, width) // width


def chunk_rows(pieces):
    parts = []
    width = pieces[0].shape[1] // PAGE
    for u in range(PAGE):
        for piece in pieces:
            parts.append(piece[:, u * width : (u + 1) * width])
    return jnp.concatenate(parts, axis=0)


def chunk_places(source, facts_ref, slots, rows, tokens, shared):
    seq_count, width = slots.shape[1], facts_ref.shape[1]
    pages = tokens // PAGE
    extra = rows - pages
    if shared is None:
        spot = lax.broadcasted_iota(jnp.int32, (pages, seq_count), 0) * seq_count + source
        low = slots * pages
        held = jnp.where(jnp.logical_and(spot >= low, spot < low + pages), 1.0, 0.0)
        shared = jnp.dot(
            held, facts_ref[:seq_count, :], precision=lax.Precision.HIGHEST, preferred_element_type=f32
        )
    spot = lax.broadcasted_iota(jnp.int32, (pages, 1), 0) * seq_count + source
    spot = spot.astype(f32)
    page = spot - pages * jnp.floor((spot + 0.5) * (1.0 / pages))
    begin = shared[:, width - 1 :] - tokens + page * PAGE
    holder = jnp.floor(shared * (1.0 / PAGE))
    bits = jnp.where(holder == page, jnp.exp2(shared - PAGE * holder), 0.0)
    bits = jnp.sum(bits, axis=1, keepdims=True).astype(jnp.int32)
    row = jnp.broadcast_to(facts_ref[pl.ds(source, 1), :], (extra * PAGE, width))
    same = lax.broadcasted_iota(jnp.int32, row.shape, 0) == lax.broadcasted_iota(
        jnp.int32, row.shape, 1
    )
    fresh = jnp.sum(jnp.where(same, row, 0.0), axis=1, keepdims=True)
    fresh = fresh + (source * tokens).astype(f32)
    parts = []
    for u in range(PAGE):
        parts.append(jnp.where(((bits >> u) & 1) == 1, FAR, begin + u))
        parts.append(fresh[u * extra : (u + 1) * extra, :])
    return jnp.concatenate(parts, axis=0), shared


def read_chunks(seq_count, tokens, arrivals, core, pieces, facts_ref, query_rows):
    chips = seq_count // 2
    here = ring_place(lax.axis_index("seq") // 2, chips)
    table_rows, limit_rows, slot_rows = fact_rows(seq_count, query_rows, facts_ref.shape[1])
    limit = get_rows(facts_ref, table_rows, limit_rows)
    slots = get_rows(facts_ref, table_rows + limit_rows, slot_rows)[:, :seq_count].astype(jnp.int32)
    blocks, places, at, shared = [], [], 0, None
    for step, count in arrivals:
        source = ring_chip((here - step + chips) % chips, chips) * 2 + core
        group = pieces[at : at + count]
        at += count
        rows = sum(piece.shape[0] for piece in group)
        if (tokens // PAGE) % seq_count:
            shared = None
        found, shared = chunk_places(source, facts_ref, slots, rows, tokens, shared)
        places.append(found)
        blocks.append(chunk_rows(group))
    blended = jnp.concatenate(blocks, axis=0) if len(blocks) > 1 else blocks[0]
    place = jnp.concatenate(places, axis=0) if len(places) > 1 else places[0]
    return blended, place, limit


def score_factor(head_dim):
    return float(head_dim**-0.5 * np.log2(np.e))


def attend(blended, flipped, place, queries, limit, old):
    head_dim = queries.shape[1]
    factor = score_factor(head_dim)
    scores = lax.dot_general(
        blended[:, :head_dim], queries, (((1,), (1,)), ((), ())), preferred_element_type=f32
    )
    scores = jnp.where(place <= limit, scores, MASKED)
    peak = jnp.maximum(jnp.max(scores, axis=0, keepdims=True), LOWEST if old is None else old[0])
    weights = jnp.exp2((scores - peak) * factor)
    total = jnp.sum(weights, axis=0, keepdims=True)
    mixed = jnp.dot(flipped, weights.astype(bf16), preferred_element_type=f32)
    if old is not None:
        fade = jnp.exp2((old[0] - peak) * factor)
        total = total + old[1] * fade
        mixed = mixed + old[2] * fade
    return peak, total, mixed


def chosen(place, wanted):
    return jnp.where(place == wanted, 1.0, 0.0).astype(bf16)


def get_state(ref):
    head_dim = ref.shape[0] - 8
    peak = ref[head_dim : head_dim + 1, :]
    total = ref[head_dim + 1 : head_dim + 2, :]
    return peak, total, ref[:head_dim, :]


def put_state(state, half, ref):
    peak, total, mixed = state
    head_dim = mixed.shape[0]
    tail = jnp.concatenate([peak, total, jnp.zeros((6, peak.shape[1]), f32)], axis=0)
    count = ref.shape[1]
    if half == 1:
        mixed, tail = pltpu.roll(mixed, count, 1), pltpu.roll(tail, count, 1)
    ref[:head_dim, :] = mixed[:, :count]
    ref[head_dim:, :] = tail[:, :count]


def put_pages(picked, ref, *others):
    count = ref.shape[0]
    pair = picked.shape[1]
    for u in range(PAGE):
        part = picked[u * count : (u + 1) * count, :]
        for other in others:
            part = part + other[:, u * pair : (u + 1) * pair].astype(f32)
        ref[:, u * pair : (u + 1) * pair] = part.astype(bf16)


def visit_kernel(seq_count, tokens, arrivals, first, last, *refs):
    piece_count = sum(count for _, count in arrivals)
    pieces = refs[:piece_count]
    own_q, other_q, facts_ref, wanted_ref = refs[piece_count : piece_count + 4]
    refs = refs[piece_count + 4 :]
    old = None
    if not first:
        old, old_pages = get_state(refs[0]), refs[1]
        refs = refs[2:]
    core = lax.axis_index("seq") % 2
    blended, place, limit = read_chunks(
        seq_count, tokens, arrivals, core, pieces, facts_ref, own_q.shape[0]
    )
    queries = jnp.concatenate([own_q[...], other_q[...]], axis=0)
    flipped = blended.T
    state = attend(blended, flipped[own_q.shape[1] :, :], place, queries, limit, old)
    picked = jnp.dot(flipped, chosen(place, wanted_ref[...]), preferred_element_type=f32)
    if not first:
        picked = picked + old_pages[...].astype(f32)
    if not last:
        put_state(state, 0, refs[0])
        refs[1][...] = picked.astype(bf16)
    else:
        turned_pages = picked.T
        for half in (0, 1):
            put_state(state, half, refs[2 * half])
            put_pages(turned_pages[half * tokens : (half + 1) * tokens, :], refs[2 * half + 1])


def close_kernel(seq_count, tokens, arrivals, *refs):
    chunk, own_q, facts_ref, wanted_ref, mine, my_pages = refs[:6]
    new, new_pages, next_place, next_chosen = refs[6:]
    core = lax.axis_index("seq") % 2
    query_rows, head_dim = own_q.shape
    blended, place, limit = read_chunks(
        seq_count, tokens, arrivals, core, [chunk], facts_ref, query_rows
    )
    wanted = wanted_ref[:, :tokens]
    state = attend(
        blended, blended[:, head_dim:].T, place, own_q[...], limit[:, :query_rows], get_state(mine)
    )
    put_state(state, 0, new)
    picked = jnp.dot(chosen(place, wanted).T, blended, preferred_element_type=f32)
    put_pages(picked, new_pages, my_pages)

    _, place, _ = read_chunks(
        seq_count, tokens, arrivals, 1 - core, [chunk], facts_ref, query_rows
    )
    next_place[...] = jnp.broadcast_to(place, next_place.shape)
    next_chosen[...] = chosen(place, wanted).T


def finish_kernel(seq_count, tokens, arrivals, *refs):
    chunk, own_q, facts_ref, mine, my_pages, place_ref, chosen_ref, got, got_pages = refs[:9]
    out_ref, pages_ref, out_scratch, pages_scratch, sems = refs[9:]
    query_rows, head_dim = own_q.shape
    table_rows, limit_rows, _ = fact_rows(seq_count, query_rows, facts_ref.shape[1])
    limit = get_rows(facts_ref, table_rows, limit_rows)[:, :query_rows]
    blended = chunk_rows([chunk])
    picked = jnp.dot(chosen_ref[...], blended, preferred_element_type=f32)
    put_pages(picked, pages_scratch, my_pages, got_pages)
    pages_copy = pltpu.make_async_copy(pages_scratch, pages_ref, sems.at[0])
    pages_copy.start()
    one, two = get_state(mine), get_state(got)
    peak = jnp.maximum(one[0], two[0])
    fades = [jnp.exp2((part[0] - peak) * score_factor(head_dim)) for part in (one, two)]
    old = [peak] + [one[i] * fades[0] + two[i] * fades[1] for i in (1, 2)]
    _, total, mixed = attend(
        blended, blended[:, head_dim:].T, place_ref[:, :1], own_q[...], limit, old
    )
    flat = (mixed * (1.0 / total)).T
    sel = out_ref.shape[0]
    for h in range(GROUP):
        out_scratch[:, h * head_dim : (h + 1) * head_dim] = flat[
            h * sel : (h + 1) * sel, :
        ].astype(bf16)
    out_copy = pltpu.make_async_copy(out_scratch, out_ref, sems.at[1])
    out_copy.start()
    pages_copy.wait()
    out_copy.wait()


def shards(
    pool_kv, pool_slot, passage_order, passage_start, recompute_pos, page_table, fresh_q, fresh_kv
):
    seq_count = lax.axis_size("seq")
    chips = seq_count // 2
    me = lax.axis_index("seq")
    pages, width = pool_kv.shape
    sel = fresh_q.shape[0]
    head_dim = fresh_kv.shape[1] // 2
    tokens = pages * PAGE
    extra = round_up(-(-sel // PAGE), TILE)
    rows = pages + extra
    query_rows = sel * GROUP
    vmem = pl.BlockSpec(memory_space=pltpu.VMEM)
    params = pltpu.CompilerParams(vmem_limit_bytes=40 * 2**20)

    anywhere = pl.BlockSpec(memory_space=pltpu.HBM)
    frequency = jnp.asarray(frequencies(head_dim))

    def gathered(kernel, in_smem, in_vmem, out_shape, scratch, name):
        operands = [
            pltpu.with_memory_space_constraint(x, pltpu.HBM) for x in (*in_smem, *in_vmem)
        ]
        return pl.pallas_call(
            kernel,
            out_shape=out_shape,
            in_specs=[anywhere] * len(operands),
            out_specs=jax.tree.map(lambda _: vmem, out_shape),
            scratch_shapes=[
                *[pltpu.SMEM(x.shape, x.dtype) for x in in_smem],
                *[pltpu.VMEM(x.shape, x.dtype) for x in in_vmem],
                scratch,
                pltpu.SemaphoreType.DMA((len(operands),)),
            ],
            compiler_params=params,
            cost_estimate=pl.CostEstimate(
                flops=10**8, bytes_accessed=6 * 2**20, transcendentals=0
            ),
            name=name,
        )(*operands)

    chunk = gathered(
        partial(prep_kernel, seq_count),
        [pool_slot, passage_order, passage_start],
        [frequency, recompute_pos, fresh_kv, pool_kv],
        jax.ShapeDtypeStruct((rows, width), bf16),
        pltpu.VMEM((extra * PAGE, 2 * head_dim), f32),
        "prepare",
    )
    fact_width = round_up(sel + 1, LANES)
    fact_count = sum(fact_rows(seq_count, query_rows, fact_width))
    queries, facts = gathered(
        partial(plan_kernel, seq_count, tokens),
        [pool_slot, passage_order, passage_start],
        [frequency, recompute_pos, fresh_q],
        (
            jax.ShapeDtypeStruct((query_rows, head_dim), bf16),
            jax.ShapeDtypeStruct((round_up(fact_count, 8), fact_width), f32),
        ),
        pltpu.VMEM((query_rows, head_dim), f32),
        "plan",
    )

    pair = jnp.stack([me, me ^ 1])
    page_ids = jnp.arange(pages, dtype=jnp.int32)
    request_pages = jnp.arange(page_table.shape[0], dtype=jnp.int32)
    owned = pair[:, None] * pages + page_ids[None, :]
    wanted = jnp.sum(
        jnp.where(page_table[None, None, :] == owned[:, :, None], request_pages[None, None, :], 0),
        axis=2,
    )
    wanted = wanted[:, None, :] * PAGE + jnp.arange(PAGE, dtype=jnp.int32)[None, :, None]
    wanted = wanted.astype(f32).reshape(1, 2 * tokens)

    swap = [(i, i ^ 1) for i in range(seq_count)]
    forward, backward = ring_pairs(chips, 1), ring_pairs(chips, -1)
    other_queries = lax.ppermute(queries, "seq", swap)

    state_shapes = (
        jax.ShapeDtypeStruct((head_dim + 8, 2 * query_rows), f32),
        jax.ShapeDtypeStruct((2 * head_dim, 2 * tokens), bf16),
    )
    half_shapes = (
        jax.ShapeDtypeStruct((head_dim + 8, query_rows), f32),
        jax.ShapeDtypeStruct((pages, width), bf16),
    )
    close_shapes = half_shapes + (
        jax.ShapeDtypeStruct((PAGE * rows, LANES), f32),
        jax.ShapeDtypeStruct((tokens, PAGE * rows), bf16),
    )
    out_shapes = (
        jax.ShapeDtypeStruct((sel, GROUP * head_dim), bf16),
        jax.ShapeDtypeStruct((pages, width), bf16),
    )

    def run(kernel, arrivals, operands, out_shape, name, aliases=(), weight=1, scratch=()):
        layout = [(step, len(pieces)) for step, pieces in arrivals]
        operands = [piece for _, pieces in arrivals for piece in pieces] + list(operands)
        pairs = PAGE * rows * len(layout) * (query_rows + tokens)
        return pl.pallas_call(
            partial(kernel, seq_count, tokens, layout),
            out_shape=out_shape,
            in_specs=[vmem] * len(operands),
            out_specs=(anywhere if scratch else vmem,) * len(out_shape),
            scratch_shapes=scratch,
            input_output_aliases={len(operands) - 2 + i: i for i in aliases},
            compiler_params=params,
            cost_estimate=pl.CostEstimate(
                flops=8 * pairs * head_dim * weight,
                bytes_accessed=4 * 2**20 * weight,
                transcendentals=2 * pairs * weight,
            ),
            name=name,
        )(*operands)

    def visit(state, arrivals, last=False):
        operands = [queries, other_queries, facts, wanted]
        first = state is None
        kernel = lambda count, size, layout, *refs: visit_kernel(
            count, size, layout, first, last, *refs
        )
        if not first:
            operands += list(state)
        out_shape = half_shapes * 2 if last else state_shapes
        aliases = () if first or last else (0, 1)
        return run(kernel, arrivals, operands, out_shape, "visit", aliases)

    state = None
    ahead = behind = chunk
    arrivals = [(0, [chunk])]
    for step in range(1, chips // 2):
        ahead = lax.ppermute(ahead, "seq", forward)
        behind = lax.ppermute(behind, "seq", backward)
        state = visit(state, arrivals)
        ahead, state = lax.optimization_barrier((ahead, state))
        arrivals = [(step, [ahead]), (-step, [behind])]
    farthest = lax.ppermute(ahead, "seq", forward)
    mine, my_pages, theirs, their_pages = visit(state, arrivals, last=True)
    got = lax.ppermute(theirs, "seq", swap)
    got_pages = lax.ppermute(their_pages, "seq", swap)
    other_farthest = lax.ppermute(farthest, "seq", swap)
    operands = [queries, facts, wanted, mine, my_pages]
    *state, place, choice = run(
        close_kernel, [(chips // 2, [farthest])], operands, close_shapes, "close", weight=10
    )
    scratch = [pltpu.VMEM(x.shape, x.dtype) for x in out_shapes]
    scratch.append(pltpu.SemaphoreType.DMA((2,)))
    operands = [queries, facts, *state, place, choice, got, got_pages]
    return run(
        finish_kernel, [(chips // 2, [other_farthest])], operands, out_shapes, "finish",
        scratch=scratch,
    )


def solution(mesh):
    placed = (
        P(("groups", "seq"), None),
        P("groups"),
        P("groups"),
        P("groups"),
        P("groups", None),
        P("groups"),
        P(("groups", "seq"), None),
        P(("groups", "seq"), None),
    )
    return jax.shard_map(
        shards,
        mesh=mesh,
        in_specs=placed,
        out_specs=(P(("groups", "seq"), None), P(("groups", "seq"), None)),
        check_vma=False,
    )
```

```python
from functools import partial

import jax
import jax.numpy as jnp
import numpy as np
from jax import lax
from jax.experimental import pallas as pl
from jax.experimental.pallas import tpu as pltpu
from jax.sharding import PartitionSpec as P

GROUP = 8
PAGE = 4
ROPE_BASE = 500000.0
FAR = float(2**23)
MASKED = -1e30
LOWEST = -1e29
TILE = 16
LANES = 128

QUARTER = (1.5703125, 253 * 2.0**-19, 170 * 2.0**-27, float(np.pi / 2 - 1.5703125 - 253 * 2.0**-19 - 170 * 2.0**-27))

f32 = jnp.float32
bf16 = jnp.bfloat16


def round_up(value, step):
    return -(-value // step) * step


def frequencies(head_dim):
    half = head_dim // 2
    index = np.arange(half, dtype=np.float32) * np.float32(2.0 / head_dim)
    one = np.power(np.float32(ROPE_BASE), -index).astype(np.float32)
    return np.concatenate([one, one])[None, :]


def ring_place(chip, chips):
    return jnp.where(chip % 2 == 0, chip // 2, chips - 1 - chip // 2)


def ring_chip(place, chips):
    return jnp.where(place < chips // 2, 2 * place, 2 * (chips - 1 - place) + 1)


def ring_order(chips):
    return list(range(0, chips, 2)) + list(range(chips - 1, 0, -2))


def ring_pairs(chips, shift):
    order = ring_order(chips)
    return [
        (order[p] * 2 + core, order[(p + shift) % chips] * 2 + core)
        for p in range(chips)
        for core in range(2)
    ]


def turned(vector, cosine, signed_sine):
    half = vector.shape[1] // 2
    return vector * cosine + pltpu.roll(vector, half, 1) * signed_sine


def cos_sin(angle):
    turns = jnp.round(angle * float(2 / np.pi))
    rest = angle
    for part in QUARTER:
        rest = rest - turns * part
    square = rest * rest
    sine = rest + rest * square * (
        -1.6666654611e-1 + square * (8.3321608736e-3 - square * 1.9515295891e-4)
    )
    cosine = (
        1.0
        - 0.5 * square
        + square
        * square
        * (4.166664568298827e-2 + square * (-1.388731625493765e-3 + square * 2.443315711809948e-5))
    )
    quadrant = turns.astype(jnp.int32) & 3
    odd = (quadrant & 1) == 1
    cos_value = jnp.where(odd, sine, cosine)
    sin_value = jnp.where(odd, cosine, sine)
    cos_value = jnp.where((quadrant == 1) | (quadrant == 2), -cos_value, cos_value)
    sin_value = jnp.where(quadrant >= 2, -sin_value, sin_value)
    return cos_value, sin_value


def rotation(angle):
    head_dim = angle.shape[1]
    cosine, sine = cos_sin(angle)
    lower = lax.broadcasted_iota(jnp.int32, angle.shape, 1) < head_dim // 2
    return cosine, jnp.where(lower, -sine, sine)


def fresh_rotation(row, start, frequency):
    sel = row.shape[1]
    wide = jnp.broadcast_to(row.astype(f32), (sel, sel))
    same = lax.broadcasted_iota(jnp.int32, (sel, sel), 0) == lax.broadcasted_iota(
        jnp.int32, (sel, sel), 1
    )
    picked = jnp.sum(jnp.where(same, wide, 0.0), axis=1, keepdims=True)
    return rotation((picked + start.astype(f32)) * frequency)


def fetch(sources, targets, sems):
    copies = [
        pltpu.make_async_copy(source, target, sems.at[i])
        for i, (source, target) in enumerate(zip(sources, targets))
    ]
    for copy in copies:
        copy.start()
    return copies


def pack_pool(chunk_ref, pool_ref, angles):
    pages = pool_ref.shape[0]
    pair = pool_ref.shape[1] // PAGE
    half = pair // 2
    for u in range(PAGE):
        keys = slice(u * pair, u * pair + half)
        values = slice(u * pair + half, (u + 1) * pair)
        chunk_ref[:pages, keys] = turned(pool_ref[:, keys].astype(f32), *angles).astype(bf16)
        chunk_ref[:pages, values] = pool_ref[:, values]


def pack_fresh(chunk_ref, fresh_ref, kv_ref, angles):
    sel, pair = kv_ref.shape
    half = pair // 2
    extra = fresh_ref.shape[0] // PAGE
    pages = chunk_ref.shape[0] - extra
    fresh_ref[sel:, :] = jnp.zeros((fresh_ref.shape[0] - sel, pair), f32)
    fresh_ref[:sel, :half] = turned(kv_ref[:, :half].astype(f32), *angles)
    fresh_ref[:sel, half:] = kv_ref[:, half:].astype(f32)
    for u in range(PAGE):
        chunk_ref[pages:, u * pair : (u + 1) * pair] = fresh_ref[
            u * extra : (u + 1) * extra, :
        ].astype(bf16)


def holding(facts_ref, slots, source, pages):
    seq_count = slots.shape[1]
    spot = lax.broadcasted_iota(jnp.int32, (pages, seq_count), 0) * seq_count + source
    low = slots * pages
    held = jnp.where(jnp.logical_and(spot >= low, spot < low + pages), 1.0, 0.0)
    return jnp.dot(
        held,
        facts_ref[:seq_count, :],
        precision=lax.Precision.HIGHEST,
        preferred_element_type=f32,
    )


def pool_rotation(facts_ref, seq_count, query_rows, source, pages):
    table, limit, slot, _ = fact_rows(seq_count, query_rows, facts_ref.shape[1])
    slots = get_rows(facts_ref, table + limit, slot)[:, :seq_count].astype(jnp.int32)
    frequency = get_rows(facts_ref, table + limit + slot, 1)
    facts = holding(facts_ref, slots, source, pages)
    at = facts.shape[1] - 2
    return rotation((facts[:, at : at + 1] - pages * PAGE) * frequency)


def plan_kernel(seq_count, tokens, *refs):
    sources, outputs, targets = refs[:9], refs[9:14], refs[14:22]
    fresh_ref, heads_ref, sems = refs[22:]
    queries_ref, facts_ref, angles_ref, chunk_ref, page_table_ref = outputs
    for copy in fetch(sources, (*targets, page_table_ref), sems):
        copy.wait()
    slot_ref, order_ref, start_ref, freq_ref, picked_ref, kv_ref, q_ref, pool_ref = targets
    me = lax.axis_index("seq")
    sel = q_ref.shape[0]
    head_dim = freq_ref.shape[1]
    pages = pool_ref.shape[0]

    row = picked_ref[pl.ds(me, 1), :]
    fresh_angles = fresh_rotation(row, start_ref[me], freq_ref[...])
    for h in range(GROUP):
        head = q_ref[:, h * head_dim : (h + 1) * head_dim].astype(f32)
        heads_ref[h * sel : (h + 1) * sel, :] = turned(head, *fresh_angles)
    queries_ref[...] = heads_ref[...].astype(bf16)

    other = me + 1 - 2 * (me % 2)
    ours = (row + me * tokens).astype(f32)
    theirs = (picked_ref[pl.ds(other, 1), :] + other * tokens).astype(f32)
    both = jnp.concatenate([ours] * GROUP + [theirs] * GROUP, axis=1)
    at = put_rows(facts_ref, seq_count, both)

    shape = (seq_count, facts_ref.shape[1])
    lanes = lax.broadcasted_iota(jnp.int32, shape, 1)
    passages = lax.broadcasted_iota(jnp.int32, shape, 0)

    def start(k, rows):
        return jnp.where(passages == k, start_ref[k] + tokens, rows)

    starts = lax.fori_loop(0, seq_count, start, jnp.zeros(shape, jnp.int32), unroll=16)
    last = jnp.where(lanes == shape[1] - 1, (passages + 1) * tokens, starts).astype(f32)
    facts_ref[:seq_count, :] = jnp.where(lanes >= shape[1] - 2, last, FAR)
    facts_ref[:seq_count, :sel] = picked_ref[...].astype(f32)

    lanes = lax.broadcasted_iota(jnp.int32, (1, round_up(seq_count, shape[1])), 1)

    def slot(k, row):
        return jnp.where(lanes == k, slot_ref[order_ref[k]], row)

    slots = lax.fori_loop(0, seq_count, slot, jnp.zeros(lanes.shape, jnp.int32), unroll=16)
    at = put_rows(facts_ref, at, slots.astype(f32))
    put_rows(facts_ref, at, freq_ref[...])

    cosine, sine = pool_rotation(facts_ref, seq_count, queries_ref.shape[0], me, pages)
    angles_ref[:pages, :] = cosine
    angles_ref[pages:, :] = sine
    pack_pool(chunk_ref, pool_ref, (cosine, sine))
    pack_fresh(chunk_ref, fresh_ref, kv_ref, fresh_angles)


def merge_kernel(seq_count, query_rows, step, pool_ref, block_ref, facts_ref, angles_ref, chunk_ref):
    pages = pool_ref.shape[0]
    if pages % seq_count:
        me = lax.axis_index("seq")
        here = ring_place(me // 2, seq_count // 2)
        source = chunk_source(here, step, seq_count, me % 2)
        angles = pool_rotation(facts_ref, seq_count, query_rows, source, pages)
    else:
        angles = angles_ref[:pages, :], angles_ref[pages:, :]
    pack_pool(chunk_ref, pool_ref, angles)
    chunk_ref[pages:, :] = block_ref[...]


def chunk_source(here, step, seq_count, core):
    chips = seq_count // 2
    return ring_chip((here - step + chips) % chips, chips) * 2 + core


def put_rows(ref, at, row):
    width = ref.shape[1]
    for i in range(row.shape[1] // width):
        ref[at + i : at + i + 1, :] = row[:, i * width : (i + 1) * width]
    return at + row.shape[1] // width


def get_rows(ref, at, count):
    return jnp.concatenate([ref[at + i : at + i + 1, :] for i in range(count)], axis=1)


def fact_rows(seq_count, query_rows, width):
    return seq_count, 2 * query_rows // width, round_up(seq_count, width) // width, 1


def fresh_places(facts_ref, source, extra, tokens):
    row = jnp.broadcast_to(facts_ref[pl.ds(source, 1), :], (extra * PAGE, facts_ref.shape[1]))
    same = lax.broadcasted_iota(jnp.int32, row.shape, 0) == lax.broadcasted_iota(
        jnp.int32, row.shape, 1
    )
    fresh = jnp.sum(jnp.where(same, row, 0.0), axis=1, keepdims=True)
    return fresh + (source * tokens).astype(f32)


def cached_places(source, shared, seq_count, pages):
    spot = lax.broadcasted_iota(jnp.int32, (pages, 1), 0) * seq_count + source
    spot = spot.astype(f32)
    page = spot - pages * jnp.floor((spot + 0.5) * (1.0 / pages))
    begin = shared[:, shared.shape[1] - 1 :] - pages * PAGE + page * PAGE
    holder = jnp.floor(shared * (1.0 / PAGE))
    bits = jnp.where(holder == page, jnp.exp2(shared - PAGE * holder), 0.0)
    bits = jnp.sum(bits, axis=1, keepdims=True).astype(jnp.int32)
    return [jnp.where(((bits >> u) & 1) == 1, FAR, begin + u) for u in range(PAGE)]


def read_places(seq_count, tokens, arrivals, core, extra, facts_ref, query_rows):
    pages = tokens // PAGE
    here = ring_place(lax.axis_index("seq") // 2, seq_count // 2)
    table_rows, limit_rows, slot_rows, _ = fact_rows(seq_count, query_rows, facts_ref.shape[1])
    slots = get_rows(facts_ref, table_rows + limit_rows, slot_rows)[:, :seq_count].astype(jnp.int32)
    parts, shared = [], None
    for pool_step, fresh_steps in arrivals:
        groups = []
        if pool_step is not None:
            source = chunk_source(here, pool_step, seq_count, core)
            if shared is None or pages % seq_count:
                shared = holding(facts_ref, slots, source, pages)
            groups.append(cached_places(source, shared, seq_count, pages))
        for step in fresh_steps:
            if step is None:
                groups.append([jnp.full((extra, 1), FAR, f32)] * PAGE)
            else:
                source = chunk_source(here, step, seq_count, core)
                fresh = fresh_places(facts_ref, source, extra, tokens)
                groups.append([fresh[u * extra : (u + 1) * extra, :] for u in range(PAGE)])
        for u in range(PAGE):
            parts += [group[u] for group in groups]
    return jnp.concatenate(parts, axis=0)


def read_rows(pieces):
    parts = []
    for piece in pieces:
        width = piece.shape[1] // PAGE
        parts += [piece[:, u * width : (u + 1) * width] for u in range(PAGE)]
    return jnp.concatenate(parts, axis=0)


def read_limit(facts_ref, seq_count, query_rows):
    table_rows, limit_rows, _, _ = fact_rows(seq_count, query_rows, facts_ref.shape[1])
    return get_rows(facts_ref, table_rows, limit_rows)


def score_factor(head_dim):
    return float(head_dim**-0.5 * np.log2(np.e))


def attend(blended, flipped, place, queries, limit, old):
    head_dim = queries.shape[1]
    factor = score_factor(head_dim)
    scores = lax.dot_general(
        blended[:, :head_dim], queries, (((1,), (1,)), ((), ())), preferred_element_type=f32
    )
    scores = jnp.where(place <= limit, scores, MASKED)
    peak = jnp.maximum(jnp.max(scores, axis=0, keepdims=True), LOWEST if old is None else old[0])
    weights = jnp.exp2((scores - peak) * factor)
    total = jnp.sum(weights, axis=0, keepdims=True)
    mixed = jnp.dot(flipped, weights.astype(bf16), preferred_element_type=f32)
    if old is not None:
        fade = jnp.exp2((old[0] - peak) * factor)
        total = total + old[1] * fade
        mixed = mixed + old[2] * fade
    return peak, total, mixed


def chosen(place, wanted):
    return jnp.where(place == wanted, 1.0, 0.0).astype(bf16)


def get_state(ref):
    head_dim = ref.shape[0] - 8
    peak = ref[head_dim : head_dim + 1, :]
    total = ref[head_dim + 1 : head_dim + 2, :]
    return peak, total, ref[:head_dim, :]


def put_state(state, half, ref):
    peak, total, mixed = state
    head_dim = mixed.shape[0]
    tail = jnp.concatenate([peak, total, jnp.zeros((6, peak.shape[1]), f32)], axis=0)
    count = ref.shape[1]
    if half == 1:
        mixed, tail = pltpu.roll(mixed, count, 1), pltpu.roll(tail, count, 1)
    ref[:head_dim, :] = mixed[:, :count]
    ref[head_dim:, :] = tail[:, :count]


def put_pages(picked, ref, *others):
    count = ref.shape[0]
    pair = picked.shape[1]
    for u in range(PAGE):
        part = picked[u * count : (u + 1) * count, :]
        for other in others:
            part = part + other[:, u * pair : (u + 1) * pair].astype(f32)
        ref[:, u * pair : (u + 1) * pair] = part.astype(bf16)


def visit_kernel(seq_count, tokens, extra, arrivals, first, last, *refs):
    pieces, refs = refs[: len(arrivals)], refs[len(arrivals) :]
    own_q, other_q, facts_ref, wanted_ref = refs[:4]
    refs = refs[4:]
    old = None
    if not first:
        old, old_pages = get_state(refs[0]), refs[1]
        refs = refs[2:]
    core = lax.axis_index("seq") % 2
    query_rows = own_q.shape[0]
    place = read_places(seq_count, tokens, arrivals, core, extra, facts_ref, query_rows)
    blended = read_rows(pieces)
    limit = read_limit(facts_ref, seq_count, query_rows)
    queries = jnp.concatenate([own_q[...], other_q[...]], axis=0)
    flipped = blended.T
    state = attend(blended, flipped[own_q.shape[1] :, :], place, queries, limit, old)
    picked = jnp.dot(flipped, chosen(place, wanted_ref[...]), preferred_element_type=f32)
    if not first:
        picked = picked + old_pages[...].astype(f32)
    if not last:
        put_state(state, 0, refs[0])
        refs[1][...] = picked.astype(bf16)
    else:
        turned_pages = picked.T
        for half in (0, 1):
            put_state(state, half, refs[2 * half])
            put_pages(turned_pages[half * tokens : (half + 1) * tokens, :], refs[2 * half + 1])


def close_kernel(seq_count, tokens, extra, arrivals, *refs):
    pieces, refs = refs[: len(arrivals)], refs[len(arrivals) :]
    own_q, facts_ref, wanted_ref, mine, my_pages = refs[:5]
    new, new_pages, next_place, next_chosen = refs[5:]
    core = lax.axis_index("seq") % 2
    query_rows, head_dim = own_q.shape
    place = read_places(seq_count, tokens, arrivals, core, extra, facts_ref, query_rows)
    blended = read_rows(pieces)
    limit = read_limit(facts_ref, seq_count, query_rows)[:, :query_rows]
    wanted = wanted_ref[:, :tokens]
    state = attend(
        blended, blended[:, head_dim:].T, place, own_q[...], limit, get_state(mine)
    )
    put_state(state, 0, new)
    picked = jnp.dot(chosen(place, wanted).T, blended, preferred_element_type=f32)
    put_pages(picked, new_pages, my_pages)

    place = read_places(seq_count, tokens, arrivals, 1 - core, extra, facts_ref, query_rows)
    next_place[...] = jnp.broadcast_to(place, next_place.shape)
    next_chosen[...] = chosen(place, wanted).T


def finish_kernel(seq_count, tokens, extra, arrivals, *refs):
    pieces, refs = refs[: len(arrivals)], refs[len(arrivals) :]
    own_q, facts_ref, mine, my_pages, place_ref, chosen_ref, got, got_pages = refs[:8]
    out_ref, pages_ref, out_scratch, pages_scratch, sems = refs[8:]
    query_rows, head_dim = own_q.shape
    limit = read_limit(facts_ref, seq_count, query_rows)[:, :query_rows]
    blended = read_rows(pieces)
    picked = jnp.dot(chosen_ref[...], blended, preferred_element_type=f32)
    put_pages(picked, pages_scratch, my_pages, got_pages)
    pages_copy = pltpu.make_async_copy(pages_scratch, pages_ref, sems.at[0])
    pages_copy.start()
    one, two = get_state(mine), get_state(got)
    peak = jnp.maximum(one[0], two[0])
    fades = [jnp.exp2((part[0] - peak) * score_factor(head_dim)) for part in (one, two)]
    old = [peak] + [one[i] * fades[0] + two[i] * fades[1] for i in (1, 2)]
    _, total, mixed = attend(
        blended, blended[:, head_dim:].T, place_ref[:, :1], own_q[...], limit, old
    )
    flat = (mixed * (1.0 / total)).T
    sel = out_ref.shape[0]
    for h in range(GROUP):
        out_scratch[:, h * head_dim : (h + 1) * head_dim] = flat[
            h * sel : (h + 1) * sel, :
        ].astype(bf16)
    out_copy = pltpu.make_async_copy(out_scratch, out_ref, sems.at[1])
    out_copy.start()
    pages_copy.wait()
    out_copy.wait()


def shards(
    pool_kv, pool_slot, passage_order, passage_start, recompute_pos, page_table, fresh_q, fresh_kv
):
    seq_count = lax.axis_size("seq")
    chips = seq_count // 2
    me = lax.axis_index("seq")
    pages, width = pool_kv.shape
    sel = fresh_q.shape[0]
    head_dim = fresh_kv.shape[1] // 2
    tokens = pages * PAGE
    extra = round_up(-(-sel // PAGE), TILE)
    rows = pages + extra
    query_rows = sel * GROUP
    vmem = pl.BlockSpec(memory_space=pltpu.VMEM)
    params = pltpu.CompilerParams(vmem_limit_bytes=40 * 2**20)

    anywhere = pl.BlockSpec(memory_space=pltpu.HBM)
    frequency = jnp.asarray(frequencies(head_dim))

    swap = [(i, i ^ 1) for i in range(seq_count)]
    forward, backward = ring_pairs(chips, 1), ring_pairs(chips, -1)
    ahead = lax.ppermute(pool_kv, "seq", forward)
    behind = lax.ppermute(pool_kv, "seq", backward)

    fact_width = round_up(sel + 2, LANES)
    fact_count = round_up(sum(fact_rows(seq_count, query_rows, fact_width)), 8)
    chunk_shape = jax.ShapeDtypeStruct((rows, width), bf16)
    in_smem = [pool_slot, passage_order, passage_start]
    in_vmem = [frequency, recompute_pos, fresh_kv, fresh_q, pool_kv]
    in_all = [*in_smem, *in_vmem, page_table]
    queries, facts, angles, chunk, page_table = pl.pallas_call(
        partial(plan_kernel, seq_count, tokens),
        out_shape=(
            jax.ShapeDtypeStruct((query_rows, head_dim), bf16),
            jax.ShapeDtypeStruct((fact_count, fact_width), f32),
            jax.ShapeDtypeStruct((2 * pages, head_dim), f32),
            chunk_shape,
            jax.ShapeDtypeStruct(page_table.shape, page_table.dtype),
        ),
        in_specs=[anywhere] * 9,
        out_specs=(vmem,) * 5,
        scratch_shapes=[
            *[pltpu.SMEM(x.shape, x.dtype) for x in in_smem],
            *[pltpu.VMEM(x.shape, x.dtype) for x in in_vmem],
            pltpu.VMEM((extra * PAGE, 2 * head_dim), f32),
            pltpu.VMEM((query_rows, head_dim), f32),
            pltpu.SemaphoreType.DMA((9,)),
        ],
        compiler_params=params,
        cost_estimate=pl.CostEstimate(flops=10**8, bytes_accessed=6 * 2**20, transcendentals=0),
        name="plan",
    )(*[pltpu.with_memory_space_constraint(x, pltpu.HBM) for x in in_all])

    def merge(step, pool_part, block):
        return pl.pallas_call(
            partial(merge_kernel, seq_count, query_rows, step),
            out_shape=chunk_shape,
            in_specs=[vmem] * 4,
            out_specs=vmem,
            compiler_params=params,
            cost_estimate=pl.CostEstimate(flops=10**7, bytes_accessed=2**20, transcendentals=0),
            name="merge",
        )(pool_part, block, facts, angles)

    pair = jnp.stack([me, me ^ 1])
    page_ids = jnp.arange(pages, dtype=jnp.int32)
    request_pages = jnp.arange(page_table.shape[0], dtype=jnp.int32)
    owned = pair[:, None] * pages + page_ids[None, :]
    wanted = jnp.sum(
        jnp.where(page_table[None, None, :] == owned[:, :, None], request_pages[None, None, :], 0),
        axis=2,
    )
    wanted = wanted[:, None, :] * PAGE + jnp.arange(PAGE, dtype=jnp.int32)[None, :, None]
    wanted = wanted.astype(f32).reshape(1, 2 * tokens)

    other_queries = lax.ppermute(queries, "seq", swap)

    state_shapes = (
        jax.ShapeDtypeStruct((head_dim + 8, 2 * query_rows), f32),
        jax.ShapeDtypeStruct((2 * head_dim, 2 * tokens), bf16),
    )
    half_shapes = (
        jax.ShapeDtypeStruct((head_dim + 8, query_rows), f32),
        jax.ShapeDtypeStruct((pages, width), bf16),
    )
    close_shapes = half_shapes + (
        jax.ShapeDtypeStruct((PAGE * (rows + extra), LANES), f32),
        jax.ShapeDtypeStruct((tokens, PAGE * (rows + extra)), bf16),
    )
    out_shapes = (
        jax.ShapeDtypeStruct((sel, GROUP * head_dim), bf16),
        jax.ShapeDtypeStruct((pages, width), bf16),
    )

    def run(kernel, arrivals, operands, out_shape, name, aliases=(), weight=1, scratch=()):
        layout = [(pool_step, fresh_steps) for pool_step, fresh_steps, _ in arrivals]
        pieces = [piece for _, _, piece in arrivals]
        operands = pieces + list(operands)
        keys = PAGE * sum(piece.shape[0] for piece in pieces)
        pairs = keys * (query_rows + tokens)
        return pl.pallas_call(
            partial(kernel, seq_count, tokens, extra, layout),
            out_shape=out_shape,
            in_specs=[vmem] * len(operands),
            out_specs=(anywhere if scratch else vmem,) * len(out_shape),
            scratch_shapes=scratch,
            input_output_aliases={len(operands) - 2 + i: i for i in aliases},
            compiler_params=params,
            cost_estimate=pl.CostEstimate(
                flops=8 * pairs * head_dim * weight,
                bytes_accessed=4 * 2**20 * weight,
                transcendentals=2 * pairs * weight,
            ),
            name=name,
        )(*operands)

    def visit(state, arrivals, last=False):
        operands = [queries, other_queries, facts, wanted]
        first = state is None
        kernel = lambda count, size, more, layout, *refs: visit_kernel(
            count, size, more, layout, first, last, *refs
        )
        if not first:
            operands += list(state)
        out_shape = half_shapes * 2 if last else state_shapes
        aliases = () if first or last else (0, 1)
        return run(kernel, arrivals, operands, out_shape, "visit", aliases)

    half = chips // 2
    own_block = chunk[pages:]
    block = lax.ppermute(own_block, "seq", backward)
    ahead, behind = merge(1, ahead, own_block), merge(-1, behind, block)
    behind, other_queries = lax.optimization_barrier((behind, other_queries))
    state = visit(None, [(0, (0,), chunk)])
    arrivals = [(1, (None,), ahead), (-1, (-1,), behind)]
    for step in range(2, half):
        ahead = lax.ppermute(ahead, "seq", forward)
        behind = lax.ppermute(behind, "seq", backward)
        state = visit(state, arrivals)
        behind, state = lax.optimization_barrier((behind, state))
        arrivals = [(step, (step - 1,), ahead), (-step, (-step,), behind)]
    farthest = lax.ppermute(behind, "seq", backward)
    fresh_left = lax.ppermute(ahead[pages:], "seq", forward)
    mine, my_pages, theirs, their_pages = visit(state, arrivals, last=True)
    got = lax.ppermute(theirs, "seq", swap)
    got_pages = lax.ppermute(their_pages, "seq", swap)
    other_farthest = lax.ppermute(farthest, "seq", swap)
    other_fresh = lax.ppermute(fresh_left, "seq", swap)
    operands = [queries, facts, wanted, mine, my_pages]
    *state, place, choice = run(
        close_kernel, [(half, (half,), farthest), (None, (half - 1,), fresh_left)], operands, close_shapes, "close", weight=10
    )
    scratch = [pltpu.VMEM(x.shape, x.dtype) for x in out_shapes]
    scratch.append(pltpu.SemaphoreType.DMA((2,)))
    operands = [queries, facts, *state, place, choice, got, got_pages]
    return run(
        finish_kernel, [(half, (half,), other_farthest), (None, (half - 1,), other_fresh)], operands, out_shapes, "finish",
        scratch=scratch,
    )


def solution(mesh):
    placed = (
        P(("groups", "seq"), None),
        P("groups"),
        P("groups"),
        P("groups"),
        P("groups", None),
        P("groups"),
        P(("groups", "seq"), None),
        P(("groups", "seq"), None),
    )
    return jax.shard_map(
        shards,
        mesh=mesh,
        in_specs=placed,
        out_specs=(P(("groups", "seq"), None), P(("groups", "seq"), None)),
        check_vma=False,
    )
```

```python
from functools import partial

import jax
import jax.numpy as jnp
import numpy as np
from jax import lax
from jax.experimental import pallas as pl
from jax.experimental.pallas import tpu as pltpu
from jax.sharding import PartitionSpec as P

GROUP = 8
PAGE = 4
ROPE_BASE = 500000.0
FAR = float(2**23)
MASKED = -1e30
LOWEST = -1e29
TILE = 16
LANES = 128

QUARTER = (1.5703125, 253 * 2.0**-19, 170 * 2.0**-27, float(np.pi / 2 - 1.5703125 - 253 * 2.0**-19 - 170 * 2.0**-27))

f32 = jnp.float32
bf16 = jnp.bfloat16


def round_up(value, step):
    return -(-value // step) * step


def frequencies(head_dim):
    half = head_dim // 2
    index = np.arange(half, dtype=np.float32) * np.float32(2.0 / head_dim)
    one = np.power(np.float32(ROPE_BASE), -index).astype(np.float32)
    return np.concatenate([one, one])[None, :]


def ring_place(chip, chips):
    return jnp.where(chip % 2 == 0, chip // 2, chips - 1 - chip // 2)


def ring_chip(place, chips):
    return jnp.where(place < chips // 2, 2 * place, 2 * (chips - 1 - place) + 1)


def ring_order(chips):
    return list(range(0, chips, 2)) + list(range(chips - 1, 0, -2))


def ring_pairs(chips, shift):
    order = ring_order(chips)
    return [
        (order[p] * 2 + core, order[(p + shift) % chips] * 2 + core)
        for p in range(chips)
        for core in range(2)
    ]


def turned(vector, cosine, signed_sine):
    half = vector.shape[1] // 2
    return vector * cosine + pltpu.roll(vector, half, 1) * signed_sine


def cos_sin(angle):
    turns = jnp.round(angle * float(2 / np.pi))
    rest = angle
    for part in QUARTER:
        rest = rest - turns * part
    square = rest * rest
    sine = rest + rest * square * (
        -1.6666654611e-1 + square * (8.3321608736e-3 - square * 1.9515295891e-4)
    )
    cosine = (
        1.0
        - 0.5 * square
        + square
        * square
        * (4.166664568298827e-2 + square * (-1.388731625493765e-3 + square * 2.443315711809948e-5))
    )
    quadrant = turns.astype(jnp.int32) & 3
    odd = (quadrant & 1) == 1
    cos_value = jnp.where(odd, sine, cosine)
    sin_value = jnp.where(odd, cosine, sine)
    cos_value = jnp.where((quadrant == 1) | (quadrant == 2), -cos_value, cos_value)
    sin_value = jnp.where(quadrant >= 2, -sin_value, sin_value)
    return cos_value, sin_value


def rotation(angle):
    head_dim = angle.shape[1]
    cosine, sine = cos_sin(angle)
    lower = lax.broadcasted_iota(jnp.int32, angle.shape, 1) < head_dim // 2
    return cosine, jnp.where(lower, -sine, sine)


def fresh_rotation(row, start, frequency):
    sel = row.shape[1]
    wide = jnp.broadcast_to(row.astype(f32), (sel, sel))
    same = lax.broadcasted_iota(jnp.int32, (sel, sel), 0) == lax.broadcasted_iota(
        jnp.int32, (sel, sel), 1
    )
    picked = jnp.sum(jnp.where(same, wide, 0.0), axis=1, keepdims=True)
    return rotation((picked + start.astype(f32)) * frequency)


def fetch(sources, targets, sems):
    copies = [
        pltpu.make_async_copy(source, target, sems.at[i])
        for i, (source, target) in enumerate(zip(sources, targets))
    ]
    for copy in copies:
        copy.start()
    return copies


def pack_pool(chunk_ref, pool_ref, angles):
    pages = pool_ref.shape[0]
    pair = pool_ref.shape[1] // PAGE
    half = pair // 2
    for u in range(PAGE):
        keys = slice(u * pair, u * pair + half)
        values = slice(u * pair + half, (u + 1) * pair)
        chunk_ref[:pages, keys] = turned(pool_ref[:, keys].astype(f32), *angles).astype(bf16)
        chunk_ref[:pages, values] = pool_ref[:, values]


def pack_fresh(chunk_ref, fresh_ref, kv_ref, angles):
    sel, pair = kv_ref.shape
    half = pair // 2
    extra = fresh_ref.shape[0] // PAGE
    pages = chunk_ref.shape[0] - extra
    fresh_ref[sel:, :] = jnp.zeros((fresh_ref.shape[0] - sel, pair), f32)
    fresh_ref[:sel, :half] = turned(kv_ref[:, :half].astype(f32), *angles)
    fresh_ref[:sel, half:] = kv_ref[:, half:].astype(f32)
    for u in range(PAGE):
        chunk_ref[pages:, u * pair : (u + 1) * pair] = fresh_ref[
            u * extra : (u + 1) * extra, :
        ].astype(bf16)


def holding(facts_ref, slots, source, pages):
    seq_count = slots.shape[1]
    spot = lax.broadcasted_iota(jnp.int32, (pages, seq_count), 0) * seq_count + source
    low = slots * pages
    held = jnp.where(jnp.logical_and(spot >= low, spot < low + pages), 1.0, 0.0)
    return jnp.dot(
        held,
        facts_ref[:seq_count, :],
        precision=lax.Precision.HIGHEST,
        preferred_element_type=f32,
    )


def pool_rotation(facts_ref, seq_count, query_rows, source, pages):
    table, limit, slot, _ = fact_rows(seq_count, query_rows, facts_ref.shape[1])
    slots = get_rows(facts_ref, table + limit, slot)[:, :seq_count].astype(jnp.int32)
    frequency = get_rows(facts_ref, table + limit + slot, 1)
    facts = holding(facts_ref, slots, source, pages)
    at = facts.shape[1] - 2
    return rotation((facts[:, at : at + 1] - pages * PAGE) * frequency)


def plan_kernel(seq_count, tokens, *refs):
    sources, outputs, targets = refs[:9], refs[9:14], refs[14:22]
    fresh_ref, heads_ref, sems = refs[22:]
    queries_ref, facts_ref, angles_ref, chunk_ref, page_table_ref = outputs
    for copy in fetch(sources, (*targets, page_table_ref), sems):
        copy.wait()
    slot_ref, order_ref, start_ref, freq_ref, picked_ref, kv_ref, q_ref, pool_ref = targets
    me = lax.axis_index("seq")
    sel = q_ref.shape[0]
    head_dim = freq_ref.shape[1]
    pages = pool_ref.shape[0]

    row = picked_ref[pl.ds(me, 1), :]
    fresh_angles = fresh_rotation(row, start_ref[me], freq_ref[...])
    for h in range(GROUP):
        head = q_ref[:, h * head_dim : (h + 1) * head_dim].astype(f32)
        heads_ref[h * sel : (h + 1) * sel, :] = turned(head, *fresh_angles)
    queries_ref[...] = heads_ref[...].astype(bf16)

    other = me + 1 - 2 * (me % 2)
    ours = (row + me * tokens).astype(f32)
    theirs = (picked_ref[pl.ds(other, 1), :] + other * tokens).astype(f32)
    both = jnp.concatenate([ours] * GROUP + [theirs] * GROUP, axis=1)
    at = put_rows(facts_ref, seq_count, both)

    shape = (seq_count, facts_ref.shape[1])
    lanes = lax.broadcasted_iota(jnp.int32, shape, 1)
    passages = lax.broadcasted_iota(jnp.int32, shape, 0)

    def start(k, rows):
        return jnp.where(passages == k, start_ref[k] + tokens, rows)

    starts = lax.fori_loop(0, seq_count, start, jnp.zeros(shape, jnp.int32), unroll=16)
    last = jnp.where(lanes == shape[1] - 1, (passages + 1) * tokens, starts).astype(f32)
    facts_ref[:seq_count, :] = jnp.where(lanes >= shape[1] - 2, last, FAR)
    facts_ref[:seq_count, :sel] = picked_ref[...].astype(f32)

    lanes = lax.broadcasted_iota(jnp.int32, (1, round_up(seq_count, shape[1])), 1)

    def slot(k, row):
        return jnp.where(lanes == k, slot_ref[order_ref[k]], row)

    slots = lax.fori_loop(0, seq_count, slot, jnp.zeros(lanes.shape, jnp.int32), unroll=16)
    at = put_rows(facts_ref, at, slots.astype(f32))
    put_rows(facts_ref, at, freq_ref[...])

    cosine, sine = pool_rotation(facts_ref, seq_count, queries_ref.shape[0], me, pages)
    angles_ref[:pages, :] = cosine
    angles_ref[pages:, :] = sine
    pack_pool(chunk_ref, pool_ref, (cosine, sine))
    pack_fresh(chunk_ref, fresh_ref, kv_ref, fresh_angles)


def merge_kernel(seq_count, query_rows, step, pool_ref, block_ref, facts_ref, angles_ref, chunk_ref):
    pages = pool_ref.shape[0]
    if pages % seq_count:
        me = lax.axis_index("seq")
        here = ring_place(me // 2, seq_count // 2)
        source = chunk_source(here, step, seq_count, me % 2)
        angles = pool_rotation(facts_ref, seq_count, query_rows, source, pages)
    else:
        angles = angles_ref[:pages, :], angles_ref[pages:, :]
    pack_pool(chunk_ref, pool_ref, angles)
    chunk_ref[pages:, :] = block_ref[...]


def chunk_source(here, step, seq_count, core):
    chips = seq_count // 2
    return ring_chip((here - step + chips) % chips, chips) * 2 + core


def put_rows(ref, at, row):
    width = ref.shape[1]
    for i in range(row.shape[1] // width):
        ref[at + i : at + i + 1, :] = row[:, i * width : (i + 1) * width]
    return at + row.shape[1] // width


def get_rows(ref, at, count):
    return jnp.concatenate([ref[at + i : at + i + 1, :] for i in range(count)], axis=1)


def fact_rows(seq_count, query_rows, width):
    return seq_count, 2 * query_rows // width, round_up(seq_count, width) // width, 1


def fresh_places(facts_ref, source, extra, tokens):
    row = jnp.broadcast_to(facts_ref[pl.ds(source, 1), :], (extra * PAGE, facts_ref.shape[1]))
    same = lax.broadcasted_iota(jnp.int32, row.shape, 0) == lax.broadcasted_iota(
        jnp.int32, row.shape, 1
    )
    fresh = jnp.sum(jnp.where(same, row, 0.0), axis=1, keepdims=True)
    return fresh + (source * tokens).astype(f32)


def cached_places(source, shared, seq_count, pages):
    spot = lax.broadcasted_iota(jnp.int32, (pages, 1), 0) * seq_count + source
    spot = spot.astype(f32)
    page = spot - pages * jnp.floor((spot + 0.5) * (1.0 / pages))
    begin = shared[:, shared.shape[1] - 1 :] - pages * PAGE + page * PAGE
    holder = jnp.floor(shared * (1.0 / PAGE))
    bits = jnp.where(holder == page, jnp.exp2(shared - PAGE * holder), 0.0)
    bits = jnp.sum(bits, axis=1, keepdims=True).astype(jnp.int32)
    return [jnp.where(((bits >> u) & 1) == 1, FAR, begin + u) for u in range(PAGE)]


def read_places(seq_count, tokens, arrivals, core, extra, facts_ref, query_rows):
    pages = tokens // PAGE
    here = ring_place(lax.axis_index("seq") // 2, seq_count // 2)
    table_rows, limit_rows, slot_rows, _ = fact_rows(seq_count, query_rows, facts_ref.shape[1])
    slots = get_rows(facts_ref, table_rows + limit_rows, slot_rows)[:, :seq_count].astype(jnp.int32)
    parts, shared = [], None
    for pool_step, fresh_steps in arrivals:
        groups = []
        if pool_step is not None:
            source = chunk_source(here, pool_step, seq_count, core)
            if shared is None or pages % seq_count:
                shared = holding(facts_ref, slots, source, pages)
            groups.append(cached_places(source, shared, seq_count, pages))
        for step in fresh_steps:
            if step is None:
                groups.append([jnp.full((extra, 1), FAR, f32)] * PAGE)
            else:
                source = chunk_source(here, step, seq_count, core)
                fresh = fresh_places(facts_ref, source, extra, tokens)
                groups.append([fresh[u * extra : (u + 1) * extra, :] for u in range(PAGE)])
        for u in range(PAGE):
            parts += [group[u] for group in groups]
    return jnp.concatenate(parts, axis=0)


def read_rows(pieces):
    parts = []
    for piece in pieces:
        width = piece.shape[1] // PAGE
        parts += [piece[:, u * width : (u + 1) * width] for u in range(PAGE)]
    return jnp.concatenate(parts, axis=0)


def read_limit(facts_ref, seq_count, query_rows):
    table_rows, limit_rows, _, _ = fact_rows(seq_count, query_rows, facts_ref.shape[1])
    return get_rows(facts_ref, table_rows, limit_rows)


def score_factor(head_dim):
    return float(head_dim**-0.5 * np.log2(np.e))


def attend(blended, flipped, place, queries, limit, old):
    head_dim = queries.shape[1]
    factor = score_factor(head_dim)
    scores = lax.dot_general(
        blended[:, :head_dim], queries, (((1,), (1,)), ((), ())), preferred_element_type=f32
    )
    scores = jnp.where(place <= limit, scores, MASKED)
    peak = jnp.maximum(jnp.max(scores, axis=0, keepdims=True), LOWEST if old is None else old[0])
    weights = jnp.exp2((scores - peak) * factor)
    total = jnp.sum(weights, axis=0, keepdims=True)
    mixed = jnp.dot(flipped, weights.astype(bf16), preferred_element_type=f32)
    if old is not None:
        fade = jnp.exp2((old[0] - peak) * factor)
        total = total + old[1] * fade
        mixed = mixed + old[2] * fade
    return peak, total, mixed


def chosen(place, wanted):
    return jnp.where(place == wanted, 1.0, 0.0).astype(bf16)


def get_state(ref):
    head_dim = ref.shape[0] - 8
    peak = ref[head_dim : head_dim + 1, :]
    total = ref[head_dim + 1 : head_dim + 2, :]
    return peak, total, ref[:head_dim, :]


def put_state(state, half, ref):
    peak, total, mixed = state
    head_dim = mixed.shape[0]
    tail = jnp.concatenate([peak, total, jnp.zeros((6, peak.shape[1]), f32)], axis=0)
    count = ref.shape[1]
    if half == 1:
        mixed, tail = pltpu.roll(mixed, count, 1), pltpu.roll(tail, count, 1)
    ref[:head_dim, :] = mixed[:, :count]
    ref[head_dim:, :] = tail[:, :count]


def put_pages(picked, ref, *others):
    count = ref.shape[0]
    pair = picked.shape[1]
    for u in range(PAGE):
        part = picked[u * count : (u + 1) * count, :]
        for other in others:
            part = part + other[:, u * pair : (u + 1) * pair].astype(f32)
        ref[:, u * pair : (u + 1) * pair] = part.astype(bf16)


def visit_kernel(seq_count, tokens, extra, arrivals, first, last, *refs):
    pieces, refs = refs[: len(arrivals)], refs[len(arrivals) :]
    own_q, other_q, facts_ref, wanted_ref = refs[:4]
    refs = refs[4:]
    old = None
    if not first:
        old, old_pages = get_state(refs[0]), refs[1]
        refs = refs[2:]
    core = lax.axis_index("seq") % 2
    query_rows = own_q.shape[0]
    place = read_places(seq_count, tokens, arrivals, core, extra, facts_ref, query_rows)
    blended = read_rows(pieces)
    limit = read_limit(facts_ref, seq_count, query_rows)
    queries = jnp.concatenate([own_q[...], other_q[...]], axis=0)
    flipped = blended.T
    state = attend(blended, flipped[own_q.shape[1] :, :], place, queries, limit, old)
    picked = jnp.dot(flipped, chosen(place, wanted_ref[...]), preferred_element_type=f32)
    if not first:
        picked = picked + old_pages[...].astype(f32)
    if not last:
        put_state(state, 0, refs[0])
        refs[1][...] = picked.astype(bf16)
    else:
        turned_pages = picked.T
        for half in (0, 1):
            put_state(state, half, refs[2 * half])
            put_pages(turned_pages[half * tokens : (half + 1) * tokens, :], refs[2 * half + 1])


def close_kernel(seq_count, tokens, extra, arrivals, *refs):
    pieces, refs = refs[: len(arrivals)], refs[len(arrivals) :]
    own_q, facts_ref, wanted_ref, mine, my_pages = refs[:5]
    new, new_pages, next_place, next_chosen = refs[5:]
    core = lax.axis_index("seq") % 2
    query_rows, head_dim = own_q.shape
    place = read_places(seq_count, tokens, arrivals, core, extra, facts_ref, query_rows)
    blended = read_rows(pieces)
    limit = read_limit(facts_ref, seq_count, query_rows)[:, :query_rows]
    wanted = wanted_ref[:, :tokens]
    state = attend(
        blended, blended[:, head_dim:].T, place, own_q[...], limit, get_state(mine)
    )
    put_state(state, 0, new)
    picked = jnp.dot(chosen(place, wanted).T, blended, preferred_element_type=f32)
    put_pages(picked, new_pages, my_pages)

    place = read_places(seq_count, tokens, arrivals, 1 - core, extra, facts_ref, query_rows)
    next_place[...] = jnp.broadcast_to(place, next_place.shape)
    next_chosen[...] = chosen(place, wanted).T


def finish_kernel(seq_count, tokens, extra, arrivals, *refs):
    pieces, refs = refs[: len(arrivals)], refs[len(arrivals) :]
    own_q, facts_ref, mine, my_pages, place_ref, chosen_ref, got, got_pages = refs[:8]
    out_ref, pages_ref, out_scratch, pages_scratch, sems = refs[8:]
    query_rows, head_dim = own_q.shape
    limit = read_limit(facts_ref, seq_count, query_rows)[:, :query_rows]
    blended = read_rows(pieces)
    picked = jnp.dot(chosen_ref[...], blended, preferred_element_type=f32)
    put_pages(picked, pages_scratch, my_pages, got_pages)
    pages_copy = pltpu.make_async_copy(pages_scratch, pages_ref, sems.at[0])
    pages_copy.start()
    one, two = get_state(mine), get_state(got)
    peak = jnp.maximum(one[0], two[0])
    fades = [jnp.exp2((part[0] - peak) * score_factor(head_dim)) for part in (one, two)]
    old = [peak] + [one[i] * fades[0] + two[i] * fades[1] for i in (1, 2)]
    _, total, mixed = attend(
        blended, blended[:, head_dim:].T, place_ref[:, :1], own_q[...], limit, old
    )
    flat = (mixed * (1.0 / total)).T
    sel = out_ref.shape[0]
    for h in range(GROUP):
        out_scratch[:, h * head_dim : (h + 1) * head_dim] = flat[
            h * sel : (h + 1) * sel, :
        ].astype(bf16)
    out_copy = pltpu.make_async_copy(out_scratch, out_ref, sems.at[1])
    out_copy.start()
    pages_copy.wait()
    out_copy.wait()


def shards(
    pool_kv, pool_slot, passage_order, passage_start, recompute_pos, page_table, fresh_q, fresh_kv
):
    seq_count = lax.axis_size("seq")
    chips = seq_count // 2
    me = lax.axis_index("seq")
    pages, width = pool_kv.shape
    sel = fresh_q.shape[0]
    head_dim = fresh_kv.shape[1] // 2
    tokens = pages * PAGE
    extra = round_up(-(-sel // PAGE), TILE)
    rows = pages + extra
    query_rows = sel * GROUP
    vmem = pl.BlockSpec(memory_space=pltpu.VMEM)
    params = pltpu.CompilerParams(vmem_limit_bytes=40 * 2**20)

    anywhere = pl.BlockSpec(memory_space=pltpu.HBM)
    frequency = jnp.asarray(frequencies(head_dim))

    swap = [(i, i ^ 1) for i in range(seq_count)]
    forward, backward = ring_pairs(chips, 1), ring_pairs(chips, -1)
    ahead = lax.ppermute(pool_kv, "seq", forward)
    behind = lax.ppermute(pool_kv, "seq", backward)

    fact_width = round_up(sel + 2, LANES)
    fact_count = round_up(sum(fact_rows(seq_count, query_rows, fact_width)), 8)
    chunk_shape = jax.ShapeDtypeStruct((rows, width), bf16)
    in_smem = [pool_slot, passage_order, passage_start]
    in_vmem = [frequency, recompute_pos, fresh_kv, fresh_q, pool_kv]
    in_all = [*in_smem, *in_vmem, page_table]
    queries, facts, angles, chunk, page_table = pl.pallas_call(
        partial(plan_kernel, seq_count, tokens),
        out_shape=(
            jax.ShapeDtypeStruct((query_rows, head_dim), bf16),
            jax.ShapeDtypeStruct((fact_count, fact_width), f32),
            jax.ShapeDtypeStruct((2 * pages, head_dim), f32),
            chunk_shape,
            jax.ShapeDtypeStruct(page_table.shape, page_table.dtype),
        ),
        in_specs=[anywhere] * 9,
        out_specs=(vmem,) * 5,
        scratch_shapes=[
            *[pltpu.SMEM(x.shape, x.dtype) for x in in_smem],
            *[pltpu.VMEM(x.shape, x.dtype) for x in in_vmem],
            pltpu.VMEM((extra * PAGE, 2 * head_dim), f32),
            pltpu.VMEM((query_rows, head_dim), f32),
            pltpu.SemaphoreType.DMA((9,)),
        ],
        compiler_params=params,
        cost_estimate=pl.CostEstimate(flops=10**8, bytes_accessed=6 * 2**20, transcendentals=0),
        name="plan",
    )(*[pltpu.with_memory_space_constraint(x, pltpu.HBM) for x in in_all])

    def merge(step, pool_part, block):
        return pl.pallas_call(
            partial(merge_kernel, seq_count, query_rows, step),
            out_shape=chunk_shape,
            in_specs=[vmem] * 4,
            out_specs=vmem,
            compiler_params=params,
            cost_estimate=pl.CostEstimate(flops=10**7, bytes_accessed=2**20, transcendentals=0),
            name="merge",
        )(pool_part, block, facts, angles)

    pair = jnp.stack([me, me ^ 1])
    page_ids = jnp.arange(pages, dtype=jnp.int32)
    request_pages = jnp.arange(page_table.shape[0], dtype=jnp.int32)
    owned = pair[:, None] * pages + page_ids[None, :]
    wanted = jnp.sum(
        jnp.where(page_table[None, None, :] == owned[:, :, None], request_pages[None, None, :], 0),
        axis=2,
    )
    wanted = wanted[:, None, :] * PAGE + jnp.arange(PAGE, dtype=jnp.int32)[None, :, None]
    wanted = wanted.astype(f32).reshape(1, 2 * tokens)

    other_queries = lax.ppermute(queries, "seq", swap)

    state_shapes = (
        jax.ShapeDtypeStruct((head_dim + 8, 2 * query_rows), f32),
        jax.ShapeDtypeStruct((2 * head_dim, 2 * tokens), bf16),
    )
    half_shapes = (
        jax.ShapeDtypeStruct((head_dim + 8, query_rows), f32),
        jax.ShapeDtypeStruct((pages, width), bf16),
    )
    close_shapes = half_shapes + (
        jax.ShapeDtypeStruct((PAGE * (rows + extra), LANES), f32),
        jax.ShapeDtypeStruct((tokens, PAGE * (rows + extra)), bf16),
    )
    out_shapes = (
        jax.ShapeDtypeStruct((sel, GROUP * head_dim), bf16),
        jax.ShapeDtypeStruct((pages, width), bf16),
    )

    def run(kernel, arrivals, operands, out_shape, name, aliases=(), weight=1, scratch=()):
        layout = [(pool_step, fresh_steps) for pool_step, fresh_steps, _ in arrivals]
        pieces = [piece for _, _, piece in arrivals]
        operands = pieces + list(operands)
        keys = PAGE * sum(piece.shape[0] for piece in pieces)
        pairs = keys * (query_rows + tokens)
        return pl.pallas_call(
            partial(kernel, seq_count, tokens, extra, layout),
            out_shape=out_shape,
            in_specs=[vmem] * len(operands),
            out_specs=(anywhere if scratch else vmem,) * len(out_shape),
            scratch_shapes=scratch,
            input_output_aliases={len(operands) - 2 + i: i for i in aliases},
            compiler_params=params,
            cost_estimate=pl.CostEstimate(
                flops=8 * pairs * head_dim * weight,
                bytes_accessed=4 * 2**20 * weight,
                transcendentals=2 * pairs * weight,
            ),
            name=name,
        )(*operands)

    def visit(state, arrivals, last=False):
        operands = [queries, other_queries, facts, wanted]
        first = state is None
        kernel = lambda count, size, more, layout, *refs: visit_kernel(
            count, size, more, layout, first, last, *refs
        )
        if not first:
            operands += list(state)
        out_shape = half_shapes * 2 if last else state_shapes
        aliases = () if first or last else (0, 1)
        return run(kernel, arrivals, operands, out_shape, "visit", aliases)

    half = chips // 2
    own_block = chunk[pages:]
    block = lax.ppermute(own_block, "seq", backward)
    ahead, behind = merge(1, ahead, own_block), merge(-1, behind, block)
    ahead, other_queries = lax.optimization_barrier((ahead, other_queries))
    behind, other_queries = lax.optimization_barrier((behind, other_queries))
    state = visit(None, [(0, (0,), chunk)])
    arrivals = [(1, (None,), ahead), (-1, (-1,), behind)]
    for step in range(2, half):
        ahead = lax.ppermute(ahead, "seq", forward)
        behind = lax.ppermute(behind, "seq", backward)
        state = visit(state, arrivals)
        ahead, state = lax.optimization_barrier((ahead, state))
        arrivals = [(step, (step - 1,), ahead), (-step, (-step,), behind)]
    farthest = lax.ppermute(ahead, "seq", forward)
    fresh_farthest = lax.ppermute(behind[pages:], "seq", backward)
    mine, my_pages, theirs, their_pages = visit(state, arrivals, last=True)
    got = lax.ppermute(theirs, "seq", swap)
    got_pages = lax.ppermute(their_pages, "seq", swap)
    other_farthest = lax.ppermute(farthest, "seq", swap)
    other_fresh = lax.ppermute(fresh_farthest, "seq", swap)
    operands = [queries, facts, wanted, mine, my_pages]
    *state, place, choice = run(
        close_kernel, [(half, (half - 1,), farthest), (None, (half,), fresh_farthest)], operands, close_shapes, "close", weight=10
    )
    scratch = [pltpu.VMEM(x.shape, x.dtype) for x in out_shapes]
    scratch.append(pltpu.SemaphoreType.DMA((2,)))
    operands = [queries, facts, *state, place, choice, got, got_pages]
    return run(
        finish_kernel, [(half, (half - 1,), other_farthest), (None, (half,), other_fresh)], operands, out_shapes, "finish",
        scratch=scratch,
    )


def solution(mesh):
    placed = (
        P(("groups", "seq"), None),
        P("groups"),
        P("groups"),
        P("groups"),
        P("groups", None),
        P("groups"),
        P(("groups", "seq"), None),
        P(("groups", "seq"), None),
    )
    return jax.shard_map(
        shards,
        mesh=mesh,
        in_specs=placed,
        out_specs=(P(("groups", "seq"), None), P(("groups", "seq"), None)),
        check_vma=False,
    )
```

```python
from functools import partial

import jax
import jax.numpy as jnp
import numpy as np
from jax import lax
from jax.experimental import pallas as pl
from jax.experimental.pallas import tpu as pltpu
from jax.sharding import PartitionSpec as P

GROUP = 8
PAGE = 4
ROPE_BASE = 500000.0
FAR = float(2**23)
MASKED = -1e30
LOWEST = -1e29
TILE = 16
LANES = 128

QUARTER = (1.5703125, 253 * 2.0**-19, 170 * 2.0**-27, float(np.pi / 2 - 1.5703125 - 253 * 2.0**-19 - 170 * 2.0**-27))

f32 = jnp.float32
bf16 = jnp.bfloat16


def round_up(value, step):
    return -(-value // step) * step


def frequencies(head_dim):
    half = head_dim // 2
    index = np.arange(half, dtype=np.float32) * np.float32(2.0 / head_dim)
    one = np.power(np.float32(ROPE_BASE), -index).astype(np.float32)
    return np.concatenate([one, one])[None, :]


def ring_place(chip, chips):
    return jnp.where(chip % 2 == 0, chip // 2, chips - 1 - chip // 2)


def ring_chip(place, chips):
    return jnp.where(place < chips // 2, 2 * place, 2 * (chips - 1 - place) + 1)


def ring_order(chips):
    return list(range(0, chips, 2)) + list(range(chips - 1, 0, -2))


def ring_pairs(chips, shift):
    order = ring_order(chips)
    return [
        (order[p] * 2 + core, order[(p + shift) % chips] * 2 + core)
        for p in range(chips)
        for core in range(2)
    ]


def turned(vector, cosine, signed_sine):
    half = vector.shape[1] // 2
    return vector * cosine + pltpu.roll(vector, half, 1) * signed_sine


def cos_sin(angle):
    turns = jnp.round(angle * float(2 / np.pi))
    rest = angle
    for part in QUARTER:
        rest = rest - turns * part
    square = rest * rest
    sine = rest + rest * square * (
        -1.6666654611e-1 + square * (8.3321608736e-3 - square * 1.9515295891e-4)
    )
    cosine = (
        1.0
        - 0.5 * square
        + square
        * square
        * (4.166664568298827e-2 + square * (-1.388731625493765e-3 + square * 2.443315711809948e-5))
    )
    quadrant = turns.astype(jnp.int32) & 3
    odd = (quadrant & 1) == 1
    cos_value = jnp.where(odd, sine, cosine)
    sin_value = jnp.where(odd, cosine, sine)
    cos_value = jnp.where((quadrant == 1) | (quadrant == 2), -cos_value, cos_value)
    sin_value = jnp.where(quadrant >= 2, -sin_value, sin_value)
    return cos_value, sin_value


def rotation(angle):
    head_dim = angle.shape[1]
    cosine, sine = cos_sin(angle)
    lower = lax.broadcasted_iota(jnp.int32, angle.shape, 1) < head_dim // 2
    return cosine, jnp.where(lower, -sine, sine)


def fresh_rotation(row, start, frequency):
    sel = row.shape[1]
    wide = jnp.broadcast_to(row.astype(f32), (sel, sel))
    same = lax.broadcasted_iota(jnp.int32, (sel, sel), 0) == lax.broadcasted_iota(
        jnp.int32, (sel, sel), 1
    )
    picked = jnp.sum(jnp.where(same, wide, 0.0), axis=1, keepdims=True)
    return rotation((picked + start.astype(f32)) * frequency)


def fetch(sources, targets, sems):
    copies = [
        pltpu.make_async_copy(source, target, sems.at[i])
        for i, (source, target) in enumerate(zip(sources, targets))
    ]
    for copy in copies:
        copy.start()
    return copies


def pack_pool(chunk_ref, pool_ref, angles):
    pages = pool_ref.shape[0]
    pair = pool_ref.shape[1] // PAGE
    half = pair // 2
    for u in range(PAGE):
        keys = slice(u * pair, u * pair + half)
        values = slice(u * pair + half, (u + 1) * pair)
        chunk_ref[:pages, keys] = turned(pool_ref[:, keys].astype(f32), *angles).astype(bf16)
        chunk_ref[:pages, values] = pool_ref[:, values]


def pack_fresh(chunk_ref, fresh_ref, kv_ref, angles):
    sel, pair = kv_ref.shape
    half = pair // 2
    extra = fresh_ref.shape[0] // PAGE
    pages = chunk_ref.shape[0] - extra
    fresh_ref[sel:, :] = jnp.zeros((fresh_ref.shape[0] - sel, pair), f32)
    fresh_ref[:sel, :half] = turned(kv_ref[:, :half].astype(f32), *angles)
    fresh_ref[:sel, half:] = kv_ref[:, half:].astype(f32)
    for u in range(PAGE):
        chunk_ref[pages:, u * pair : (u + 1) * pair] = fresh_ref[
            u * extra : (u + 1) * extra, :
        ].astype(bf16)


def holding(facts_ref, slots, source, pages):
    seq_count = slots.shape[1]
    spot = lax.broadcasted_iota(jnp.int32, (pages, seq_count), 0) * seq_count + source
    low = slots * pages
    held = jnp.where(jnp.logical_and(spot >= low, spot < low + pages), 1.0, 0.0)
    return jnp.dot(
        held,
        facts_ref[:seq_count, :],
        precision=lax.Precision.HIGHEST,
        preferred_element_type=f32,
    )


def pool_rotation(facts_ref, seq_count, query_rows, source, pages):
    table, limit, slot, _ = fact_rows(seq_count, query_rows, facts_ref.shape[1])
    slots = get_rows(facts_ref, table + limit, slot)[:, :seq_count].astype(jnp.int32)
    frequency = get_rows(facts_ref, table + limit + slot, 1)
    facts = holding(facts_ref, slots, source, pages)
    at = facts.shape[1] - 2
    return rotation((facts[:, at : at + 1] - pages * PAGE) * frequency)


def plan_kernel(seq_count, tokens, *refs):
    sources, outputs, targets = refs[:9], refs[9:14], refs[14:22]
    fresh_ref, heads_ref, sems = refs[22:]
    queries_ref, facts_ref, angles_ref, chunk_ref, page_table_ref = outputs
    for copy in fetch(sources, (*targets, page_table_ref), sems):
        copy.wait()
    slot_ref, order_ref, start_ref, freq_ref, picked_ref, kv_ref, q_ref, pool_ref = targets
    me = lax.axis_index("seq")
    sel = q_ref.shape[0]
    head_dim = freq_ref.shape[1]
    pages = pool_ref.shape[0]

    row = picked_ref[pl.ds(me, 1), :]
    fresh_angles = fresh_rotation(row, start_ref[me], freq_ref[...])
    for h in range(GROUP):
        head = q_ref[:, h * head_dim : (h + 1) * head_dim].astype(f32)
        heads_ref[h * sel : (h + 1) * sel, :] = turned(head, *fresh_angles)
    queries_ref[...] = heads_ref[...].astype(bf16)

    other = me + 1 - 2 * (me % 2)
    ours = (row + me * tokens).astype(f32)
    theirs = (picked_ref[pl.ds(other, 1), :] + other * tokens).astype(f32)
    both = jnp.concatenate([ours] * GROUP + [theirs] * GROUP, axis=1)
    at = put_rows(facts_ref, seq_count, both)

    shape = (seq_count, facts_ref.shape[1])
    lanes = lax.broadcasted_iota(jnp.int32, shape, 1)
    passages = lax.broadcasted_iota(jnp.int32, shape, 0)

    def start(k, rows):
        return jnp.where(passages == k, start_ref[k] + tokens, rows)

    starts = lax.fori_loop(0, seq_count, start, jnp.zeros(shape, jnp.int32), unroll=16)
    last = jnp.where(lanes == shape[1] - 1, (passages + 1) * tokens, starts).astype(f32)
    facts_ref[:seq_count, :] = jnp.where(lanes >= shape[1] - 2, last, FAR)
    facts_ref[:seq_count, :sel] = picked_ref[...].astype(f32)

    lanes = lax.broadcasted_iota(jnp.int32, (1, round_up(seq_count, shape[1])), 1)

    def slot(k, row):
        return jnp.where(lanes == k, slot_ref[order_ref[k]], row)

    slots = lax.fori_loop(0, seq_count, slot, jnp.zeros(lanes.shape, jnp.int32), unroll=16)
    at = put_rows(facts_ref, at, slots.astype(f32))
    put_rows(facts_ref, at, freq_ref[...])

    cosine, sine = pool_rotation(facts_ref, seq_count, queries_ref.shape[0], me, pages)
    angles_ref[:pages, :] = cosine
    angles_ref[pages:, :] = sine
    pack_pool(chunk_ref, pool_ref, (cosine, sine))
    pack_fresh(chunk_ref, fresh_ref, kv_ref, fresh_angles)


def merge_kernel(seq_count, query_rows, step, pool_ref, block_ref, facts_ref, angles_ref, chunk_ref):
    pages = pool_ref.shape[0]
    if pages % seq_count:
        me = lax.axis_index("seq")
        here = ring_place(me // 2, seq_count // 2)
        source = chunk_source(here, step, seq_count, me % 2)
        angles = pool_rotation(facts_ref, seq_count, query_rows, source, pages)
    else:
        angles = angles_ref[:pages, :], angles_ref[pages:, :]
    pack_pool(chunk_ref, pool_ref, angles)
    chunk_ref[pages:, :] = block_ref[...]


def chunk_source(here, step, seq_count, core):
    chips = seq_count // 2
    return ring_chip((here - step + chips) % chips, chips) * 2 + core


def put_rows(ref, at, row):
    width = ref.shape[1]
    for i in range(row.shape[1] // width):
        ref[at + i : at + i + 1, :] = row[:, i * width : (i + 1) * width]
    return at + row.shape[1] // width


def get_rows(ref, at, count):
    return jnp.concatenate([ref[at + i : at + i + 1, :] for i in range(count)], axis=1)


def fact_rows(seq_count, query_rows, width):
    return seq_count, 2 * query_rows // width, round_up(seq_count, width) // width, 1


def fresh_places(facts_ref, source, extra, tokens):
    row = jnp.broadcast_to(facts_ref[pl.ds(source, 1), :], (extra * PAGE, facts_ref.shape[1]))
    same = lax.broadcasted_iota(jnp.int32, row.shape, 0) == lax.broadcasted_iota(
        jnp.int32, row.shape, 1
    )
    fresh = jnp.sum(jnp.where(same, row, 0.0), axis=1, keepdims=True)
    return fresh + (source * tokens).astype(f32)


def cached_places(source, shared, seq_count, pages):
    spot = lax.broadcasted_iota(jnp.int32, (pages, 1), 0) * seq_count + source
    spot = spot.astype(f32)
    page = spot - pages * jnp.floor((spot + 0.5) * (1.0 / pages))
    begin = shared[:, shared.shape[1] - 1 :] - pages * PAGE + page * PAGE
    holder = jnp.floor(shared * (1.0 / PAGE))
    bits = jnp.where(holder == page, jnp.exp2(shared - PAGE * holder), 0.0)
    bits = jnp.sum(bits, axis=1, keepdims=True).astype(jnp.int32)
    return [jnp.where(((bits >> u) & 1) == 1, FAR, begin + u) for u in range(PAGE)]


def read_places(seq_count, tokens, arrivals, core, extra, facts_ref, query_rows):
    pages = tokens // PAGE
    here = ring_place(lax.axis_index("seq") // 2, seq_count // 2)
    table_rows, limit_rows, slot_rows, _ = fact_rows(seq_count, query_rows, facts_ref.shape[1])
    slots = get_rows(facts_ref, table_rows + limit_rows, slot_rows)[:, :seq_count].astype(jnp.int32)
    parts, shared = [], None
    for pool_step, fresh_steps in arrivals:
        groups = []
        if pool_step is not None:
            source = chunk_source(here, pool_step, seq_count, core)
            if shared is None or pages % seq_count:
                shared = holding(facts_ref, slots, source, pages)
            groups.append(cached_places(source, shared, seq_count, pages))
        for step in fresh_steps:
            if step is None:
                groups.append([jnp.full((extra, 1), FAR, f32)] * PAGE)
            else:
                source = chunk_source(here, step, seq_count, core)
                fresh = fresh_places(facts_ref, source, extra, tokens)
                groups.append([fresh[u * extra : (u + 1) * extra, :] for u in range(PAGE)])
        for u in range(PAGE):
            parts += [group[u] for group in groups]
    return jnp.concatenate(parts, axis=0)


def read_rows(pieces):
    parts = []
    for piece in pieces:
        width = piece.shape[1] // PAGE
        parts += [piece[:, u * width : (u + 1) * width] for u in range(PAGE)]
    return jnp.concatenate(parts, axis=0)


def read_limit(facts_ref, seq_count, query_rows):
    table_rows, limit_rows, _, _ = fact_rows(seq_count, query_rows, facts_ref.shape[1])
    return get_rows(facts_ref, table_rows, limit_rows)


def score_factor(head_dim):
    return float(head_dim**-0.5 * np.log2(np.e))


def attend(blended, flipped, place, queries, limit, old):
    head_dim = queries.shape[1]
    factor = score_factor(head_dim)
    scores = lax.dot_general(
        blended[:, :head_dim], queries, (((1,), (1,)), ((), ())), preferred_element_type=f32
    )
    scores = jnp.where(place <= limit, scores, MASKED)
    peak = jnp.maximum(jnp.max(scores, axis=0, keepdims=True), LOWEST if old is None else old[0])
    weights = jnp.exp2((scores - peak) * factor)
    total = jnp.sum(weights, axis=0, keepdims=True)
    mixed = jnp.dot(flipped, weights.astype(bf16), preferred_element_type=f32)
    if old is not None:
        fade = jnp.exp2((old[0] - peak) * factor)
        total = total + old[1] * fade
        mixed = mixed + old[2] * fade
    return peak, total, mixed


def chosen(place, wanted):
    return jnp.where(place == wanted, 1.0, 0.0).astype(bf16)


def get_state(ref):
    head_dim = ref.shape[0] - 8
    peak = ref[head_dim : head_dim + 1, :]
    total = ref[head_dim + 1 : head_dim + 2, :]
    return peak, total, ref[:head_dim, :]


def put_state(state, half, ref):
    peak, total, mixed = state
    head_dim = mixed.shape[0]
    tail = jnp.concatenate([peak, total, jnp.zeros((6, peak.shape[1]), f32)], axis=0)
    count = ref.shape[1]
    if half == 1:
        mixed, tail = pltpu.roll(mixed, count, 1), pltpu.roll(tail, count, 1)
    ref[:head_dim, :] = mixed[:, :count]
    ref[head_dim:, :] = tail[:, :count]


def put_pages(picked, ref, *others):
    count = ref.shape[0]
    pair = picked.shape[1]
    for u in range(PAGE):
        part = picked[u * count : (u + 1) * count, :]
        for other in others:
            part = part + other[:, u * pair : (u + 1) * pair].astype(f32)
        ref[:, u * pair : (u + 1) * pair] = part.astype(bf16)


def visit_kernel(seq_count, tokens, extra, arrivals, first, last, *refs):
    pieces, refs = refs[: len(arrivals)], refs[len(arrivals) :]
    own_q, other_q, facts_ref, wanted_ref = refs[:4]
    refs = refs[4:]
    old = None
    if not first:
        old, old_pages = get_state(refs[0]), refs[1]
        refs = refs[2:]
    core = lax.axis_index("seq") % 2
    query_rows = own_q.shape[0]
    place = read_places(seq_count, tokens, arrivals, core, extra, facts_ref, query_rows)
    blended = read_rows(pieces)
    limit = read_limit(facts_ref, seq_count, query_rows)
    queries = jnp.concatenate([own_q[...], other_q[...]], axis=0)
    flipped = blended.T
    state = attend(blended, flipped[own_q.shape[1] :, :], place, queries, limit, old)
    picked = jnp.dot(flipped, chosen(place, wanted_ref[...]), preferred_element_type=f32)
    if not first:
        picked = picked + old_pages[...].astype(f32)
    if not last:
        put_state(state, 0, refs[0])
        refs[1][...] = picked.astype(bf16)
    else:
        turned_pages = picked.T
        for half in (0, 1):
            put_state(state, half, refs[2 * half])
            put_pages(turned_pages[half * tokens : (half + 1) * tokens, :], refs[2 * half + 1])


def places_kernel(seq_count, tokens, extra, arrivals, query_rows, facts_ref, wanted_ref, *outputs):
    core = lax.axis_index("seq") % 2
    wanted = wanted_ref[:, :tokens]
    for side in range(2):
        at = core + side * (1 - 2 * core)
        place = read_places(seq_count, tokens, arrivals, at, extra, facts_ref, query_rows)
        place_ref, chosen_ref = outputs[2 * side : 2 * side + 2]
        place_ref[...] = jnp.broadcast_to(place, place_ref.shape)
        chosen_ref[...] = chosen(place, wanted).T


def close_kernel(seq_count, tokens, extra, arrivals, *refs):
    pieces, refs = refs[: len(arrivals)], refs[len(arrivals) :]
    own_q, facts_ref, place_ref, chosen_ref, mine, my_pages, new, new_pages = refs
    query_rows, head_dim = own_q.shape
    blended = read_rows(pieces)
    limit = read_limit(facts_ref, seq_count, query_rows)[:, :query_rows]
    state = attend(
        blended, blended[:, head_dim:].T, place_ref[:, :1], own_q[...], limit, get_state(mine)
    )
    put_state(state, 0, new)
    picked = jnp.dot(chosen_ref[...], blended, preferred_element_type=f32)
    put_pages(picked, new_pages, my_pages)


def finish_kernel(seq_count, tokens, extra, arrivals, *refs):
    pieces, refs = refs[: len(arrivals)], refs[len(arrivals) :]
    own_q, facts_ref, mine, my_pages, place_ref, chosen_ref, got, got_pages = refs[:8]
    out_ref, pages_ref, out_scratch, pages_scratch, sems = refs[8:]
    query_rows, head_dim = own_q.shape
    limit = read_limit(facts_ref, seq_count, query_rows)[:, :query_rows]
    blended = read_rows(pieces)
    picked = jnp.dot(chosen_ref[...], blended, preferred_element_type=f32)
    put_pages(picked, pages_scratch, my_pages, got_pages)
    pages_copy = pltpu.make_async_copy(pages_scratch, pages_ref, sems.at[0])
    pages_copy.start()
    one, two = get_state(mine), get_state(got)
    peak = jnp.maximum(one[0], two[0])
    fades = [jnp.exp2((part[0] - peak) * score_factor(head_dim)) for part in (one, two)]
    old = [peak] + [one[i] * fades[0] + two[i] * fades[1] for i in (1, 2)]
    flat = []
    cut = round_up(query_rows // 2, LANES)
    for columns in (slice(0, cut), slice(cut, query_rows)):
        _, total, mixed = attend(
            blended, blended[:, head_dim:].T, place_ref[:, :1], own_q[columns, :],
            limit[:, columns], [part[:, columns] for part in old],
        )
        flat.append((mixed * (1.0 / total)).T)
    flat = jnp.concatenate(flat, axis=0)
    sel = out_ref.shape[0]
    for h in range(GROUP):
        out_scratch[:, h * head_dim : (h + 1) * head_dim] = flat[
            h * sel : (h + 1) * sel, :
        ].astype(bf16)
    out_copy = pltpu.make_async_copy(out_scratch, out_ref, sems.at[1])
    out_copy.start()
    pages_copy.wait()
    out_copy.wait()


def shards(
    pool_kv, pool_slot, passage_order, passage_start, recompute_pos, page_table, fresh_q, fresh_kv
):
    seq_count = lax.axis_size("seq")
    chips = seq_count // 2
    me = lax.axis_index("seq")
    pages, width = pool_kv.shape
    sel = fresh_q.shape[0]
    head_dim = fresh_kv.shape[1] // 2
    tokens = pages * PAGE
    extra = round_up(-(-sel // PAGE), TILE)
    rows = pages + extra
    query_rows = sel * GROUP
    vmem = pl.BlockSpec(memory_space=pltpu.VMEM)
    params = pltpu.CompilerParams(vmem_limit_bytes=40 * 2**20)

    anywhere = pl.BlockSpec(memory_space=pltpu.HBM)
    frequency = jnp.asarray(frequencies(head_dim))

    swap = [(i, i ^ 1) for i in range(seq_count)]
    forward, backward = ring_pairs(chips, 1), ring_pairs(chips, -1)
    ahead = lax.ppermute(pool_kv, "seq", forward)
    behind = lax.ppermute(pool_kv, "seq", backward)

    fact_width = round_up(sel + 2, LANES)
    fact_count = round_up(sum(fact_rows(seq_count, query_rows, fact_width)), 8)
    chunk_shape = jax.ShapeDtypeStruct((rows, width), bf16)
    in_smem = [pool_slot, passage_order, passage_start]
    in_vmem = [frequency, recompute_pos, fresh_kv, fresh_q, pool_kv]
    in_all = [*in_smem, *in_vmem, page_table]
    queries, facts, angles, chunk, page_table = pl.pallas_call(
        partial(plan_kernel, seq_count, tokens),
        out_shape=(
            jax.ShapeDtypeStruct((query_rows, head_dim), bf16),
            jax.ShapeDtypeStruct((fact_count, fact_width), f32),
            jax.ShapeDtypeStruct((2 * pages, head_dim), f32),
            chunk_shape,
            jax.ShapeDtypeStruct(page_table.shape, page_table.dtype),
        ),
        in_specs=[anywhere] * 9,
        out_specs=(vmem,) * 5,
        scratch_shapes=[
            *[pltpu.SMEM(x.shape, x.dtype) for x in in_smem],
            *[pltpu.VMEM(x.shape, x.dtype) for x in in_vmem],
            pltpu.VMEM((extra * PAGE, 2 * head_dim), f32),
            pltpu.VMEM((query_rows, head_dim), f32),
            pltpu.SemaphoreType.DMA((9,)),
        ],
        compiler_params=params,
        cost_estimate=pl.CostEstimate(flops=10**8, bytes_accessed=6 * 2**20, transcendentals=0),
        name="plan",
    )(*[pltpu.with_memory_space_constraint(x, pltpu.HBM) for x in in_all])

    def merge(step, pool_part, block):
        return pl.pallas_call(
            partial(merge_kernel, seq_count, query_rows, step),
            out_shape=chunk_shape,
            in_specs=[vmem] * 4,
            out_specs=vmem,
            compiler_params=params,
            cost_estimate=pl.CostEstimate(flops=10**7, bytes_accessed=2**20, transcendentals=0),
            name="merge",
        )(pool_part, block, facts, angles)

    pair = jnp.stack([me, me ^ 1])
    page_ids = jnp.arange(pages, dtype=jnp.int32)
    request_pages = jnp.arange(page_table.shape[0], dtype=jnp.int32)
    owned = pair[:, None] * pages + page_ids[None, :]
    wanted = jnp.sum(
        jnp.where(page_table[None, None, :] == owned[:, :, None], request_pages[None, None, :], 0),
        axis=2,
    )
    wanted = wanted[:, None, :] * PAGE + jnp.arange(PAGE, dtype=jnp.int32)[None, :, None]
    wanted = wanted.astype(f32).reshape(1, 2 * tokens)

    other_queries = lax.ppermute(queries, "seq", swap)

    state_shapes = (
        jax.ShapeDtypeStruct((head_dim + 8, 2 * query_rows), f32),
        jax.ShapeDtypeStruct((2 * head_dim, 2 * tokens), bf16),
    )
    half_shapes = (
        jax.ShapeDtypeStruct((head_dim + 8, query_rows), f32),
        jax.ShapeDtypeStruct((pages, width), bf16),
    )
    place_shapes = (
        jax.ShapeDtypeStruct((PAGE * (rows + extra), LANES), f32),
        jax.ShapeDtypeStruct((tokens, PAGE * (rows + extra)), bf16),
    ) * 2
    out_shapes = (
        jax.ShapeDtypeStruct((sel, GROUP * head_dim), bf16),
        jax.ShapeDtypeStruct((pages, width), bf16),
    )

    def run(kernel, arrivals, operands, out_shape, name, aliases=(), weight=1, scratch=()):
        layout = [(pool_step, fresh_steps) for pool_step, fresh_steps, _ in arrivals]
        pieces = [piece for _, _, piece in arrivals]
        operands = pieces + list(operands)
        keys = PAGE * sum(piece.shape[0] for piece in pieces)
        pairs = keys * (query_rows + tokens)
        return pl.pallas_call(
            partial(kernel, seq_count, tokens, extra, layout),
            out_shape=out_shape,
            in_specs=[vmem] * len(operands),
            out_specs=(anywhere if scratch else vmem,) * len(out_shape),
            scratch_shapes=scratch,
            input_output_aliases={len(operands) - 2 + i: i for i in aliases},
            compiler_params=params,
            cost_estimate=pl.CostEstimate(
                flops=8 * pairs * head_dim * weight,
                bytes_accessed=4 * 2**20 * weight,
                transcendentals=2 * pairs * weight,
            ),
            name=name,
        )(*operands)

    def visit(state, arrivals, last=False):
        operands = [queries, other_queries, facts, wanted]
        first = state is None
        kernel = lambda count, size, more, layout, *refs: visit_kernel(
            count, size, more, layout, first, last, *refs
        )
        if not first:
            operands += list(state)
        out_shape = half_shapes * 2 if last else state_shapes
        aliases = () if first or last else (0, 1)
        return run(kernel, arrivals, operands, out_shape, "visit", aliases)

    half = chips // 2
    last_steps = [(half, (half - 1,)), (None, (half,))]
    own_block = chunk[pages:]
    block = lax.ppermute(own_block, "seq", backward)
    ahead, behind = merge(1, ahead, own_block), merge(-1, behind, block)
    ahead, other_queries = lax.optimization_barrier((ahead, other_queries))
    behind, other_queries = lax.optimization_barrier((behind, other_queries))
    state = visit(None, [(0, (0,), chunk)])
    arrivals = [(1, (None,), ahead), (-1, (-1,), behind)]
    for step in range(2, half):
        ahead = lax.ppermute(ahead, "seq", forward)
        behind = lax.ppermute(behind, "seq", backward)
        state = visit(state, arrivals)
        if step == half - 1:
            found = pl.pallas_call(
                partial(places_kernel, seq_count, tokens, extra, last_steps, query_rows),
                out_shape=place_shapes,
                in_specs=[vmem] * 2,
                out_specs=(vmem,) * 4,
                compiler_params=params,
                cost_estimate=pl.CostEstimate(
                    flops=10**8, bytes_accessed=2**21, transcendentals=0
                ),
                name="places",
            )(facts, wanted)
            ahead, state, found = lax.optimization_barrier((ahead, state, found))
        else:
            ahead, state = lax.optimization_barrier((ahead, state))
        arrivals = [(step, (step - 1,), ahead), (-step, (-step,), behind)]
    farthest = lax.ppermute(ahead, "seq", forward)
    fresh_farthest = lax.ppermute(behind[pages:], "seq", backward)
    mine, my_pages, theirs, their_pages = visit(state, arrivals, last=True)
    got = lax.ppermute(theirs, "seq", swap)
    got_pages = lax.ppermute(their_pages, "seq", swap)
    other_farthest = lax.ppermute(farthest, "seq", swap)
    other_fresh = lax.ppermute(fresh_farthest, "seq", swap)
    state = run(
        close_kernel, [(half, (half - 1,), farthest), (None, (half,), fresh_farthest)],
        [queries, facts, *found[:2], mine, my_pages], half_shapes, "close", weight=10,
    )
    scratch = [pltpu.VMEM(x.shape, x.dtype) for x in out_shapes]
    scratch.append(pltpu.SemaphoreType.DMA((2,)))
    operands = [queries, facts, *state, *found[2:], got, got_pages]
    return run(
        finish_kernel, [(half, (half - 1,), other_farthest), (None, (half,), other_fresh)], operands, out_shapes, "finish",
        scratch=scratch,
    )


def solution(mesh):
    placed = (
        P(("groups", "seq"), None),
        P("groups"),
        P("groups"),
        P("groups"),
        P("groups", None),
        P("groups"),
        P(("groups", "seq"), None),
        P(("groups", "seq"), None),
    )
    return jax.shard_map(
        shards,
        mesh=mesh,
        in_specs=placed,
        out_specs=(P(("groups", "seq"), None), P(("groups", "seq"), None)),
        check_vma=False,
    )
```

```python
from functools import partial

import jax
import jax.numpy as jnp
import numpy as np
from jax import lax
from jax.experimental import pallas as pl
from jax.experimental.pallas import tpu as pltpu
from jax.sharding import PartitionSpec as P

GROUP = 8
PAGE = 4
ROPE_BASE = 500000.0
FAR = float(2**23)
MASKED = -1e30
LOWEST = -1e29
TILE = 16
LANES = 128

QUARTER = (1.5703125, 253 * 2.0**-19, 170 * 2.0**-27, float(np.pi / 2 - 1.5703125 - 253 * 2.0**-19 - 170 * 2.0**-27))

f32 = jnp.float32
bf16 = jnp.bfloat16


def round_up(value, step):
    return -(-value // step) * step


def frequencies(head_dim):
    half = head_dim // 2
    index = np.arange(half, dtype=np.float32) * np.float32(2.0 / head_dim)
    one = np.power(np.float32(ROPE_BASE), -index).astype(np.float32)
    return np.concatenate([one, one])[None, :]


def ring_place(chip, chips):
    return jnp.where(chip % 2 == 0, chip // 2, chips - 1 - chip // 2)


def ring_chip(place, chips):
    return jnp.where(place < chips // 2, 2 * place, 2 * (chips - 1 - place) + 1)


def ring_order(chips):
    return list(range(0, chips, 2)) + list(range(chips - 1, 0, -2))


def ring_pairs(chips, shift):
    order = ring_order(chips)
    return [
        (order[p] * 2 + core, order[(p + shift) % chips] * 2 + core)
        for p in range(chips)
        for core in range(2)
    ]


def turned(vector, cosine, signed_sine):
    half = vector.shape[1] // 2
    return vector * cosine + pltpu.roll(vector, half, 1) * signed_sine


def cos_sin(angle):
    turns = jnp.round(angle * float(2 / np.pi))
    rest = angle
    for part in QUARTER:
        rest = rest - turns * part
    square = rest * rest
    sine = rest + rest * square * (
        -1.6666654611e-1 + square * (8.3321608736e-3 - square * 1.9515295891e-4)
    )
    cosine = (
        1.0
        - 0.5 * square
        + square
        * square
        * (4.166664568298827e-2 + square * (-1.388731625493765e-3 + square * 2.443315711809948e-5))
    )
    quadrant = turns.astype(jnp.int32) & 3
    odd = (quadrant & 1) == 1
    cos_value = jnp.where(odd, sine, cosine)
    sin_value = jnp.where(odd, cosine, sine)
    cos_value = jnp.where((quadrant == 1) | (quadrant == 2), -cos_value, cos_value)
    sin_value = jnp.where(quadrant >= 2, -sin_value, sin_value)
    return cos_value, sin_value


def rotation(angle):
    head_dim = angle.shape[1]
    cosine, sine = cos_sin(angle)
    lower = lax.broadcasted_iota(jnp.int32, angle.shape, 1) < head_dim // 2
    return cosine, jnp.where(lower, -sine, sine)


def fresh_rotation(row, start, frequency):
    sel = row.shape[1]
    wide = jnp.broadcast_to(row.astype(f32), (sel, sel))
    same = lax.broadcasted_iota(jnp.int32, (sel, sel), 0) == lax.broadcasted_iota(
        jnp.int32, (sel, sel), 1
    )
    picked = jnp.sum(jnp.where(same, wide, 0.0), axis=1, keepdims=True)
    return rotation((picked + start.astype(f32)) * frequency)


def fetch(sources, targets, sems):
    copies = [
        pltpu.make_async_copy(source, target, sems.at[i])
        for i, (source, target) in enumerate(zip(sources, targets))
    ]
    for copy in copies:
        copy.start()
    return copies


def pack_pool(chunk_ref, pool_ref, angles):
    pages = pool_ref.shape[0]
    pair = pool_ref.shape[1] // PAGE
    half = pair // 2
    for u in range(PAGE):
        keys = slice(u * pair, u * pair + half)
        values = slice(u * pair + half, (u + 1) * pair)
        chunk_ref[:pages, keys] = turned(pool_ref[:, keys].astype(f32), *angles).astype(bf16)
        chunk_ref[:pages, values] = pool_ref[:, values]


def pack_fresh(chunk_ref, fresh_ref, kv_ref, angles):
    sel, pair = kv_ref.shape
    half = pair // 2
    extra = fresh_ref.shape[0] // PAGE
    pages = chunk_ref.shape[0] - extra
    fresh_ref[sel:, :] = jnp.zeros((fresh_ref.shape[0] - sel, pair), f32)
    fresh_ref[:sel, :half] = turned(kv_ref[:, :half].astype(f32), *angles)
    fresh_ref[:sel, half:] = kv_ref[:, half:].astype(f32)
    for u in range(PAGE):
        chunk_ref[pages:, u * pair : (u + 1) * pair] = fresh_ref[
            u * extra : (u + 1) * extra, :
        ].astype(bf16)


def holding(facts_ref, slots, source, pages):
    seq_count = slots.shape[1]
    spot = lax.broadcasted_iota(jnp.int32, (pages, seq_count), 0) * seq_count + source
    low = slots * pages
    held = jnp.where(jnp.logical_and(spot >= low, spot < low + pages), 1.0, 0.0)
    return jnp.dot(
        held,
        facts_ref[:seq_count, :],
        precision=lax.Precision.HIGHEST,
        preferred_element_type=f32,
    )


def pool_rotation(facts_ref, seq_count, query_rows, source, pages):
    table, limit, slot, _ = fact_rows(seq_count, query_rows, facts_ref.shape[1])
    slots = get_rows(facts_ref, table + limit, slot)[:, :seq_count].astype(jnp.int32)
    frequency = get_rows(facts_ref, table + limit + slot, 1)
    facts = holding(facts_ref, slots, source, pages)
    at = facts.shape[1] - 2
    return rotation((facts[:, at : at + 1] - pages * PAGE) * frequency)


def plan_kernel(seq_count, tokens, *refs):
    sources, outputs, targets = refs[:9], refs[9:14], refs[14:22]
    fresh_ref, heads_ref, sems = refs[22:]
    queries_ref, facts_ref, angles_ref, chunk_ref, page_table_ref = outputs
    for copy in fetch(sources, (*targets, page_table_ref), sems):
        copy.wait()
    slot_ref, order_ref, start_ref, freq_ref, picked_ref, kv_ref, q_ref, pool_ref = targets
    me = lax.axis_index("seq")
    sel = q_ref.shape[0]
    head_dim = freq_ref.shape[1]
    pages = pool_ref.shape[0]

    row = picked_ref[pl.ds(me, 1), :]
    fresh_angles = fresh_rotation(row, start_ref[me], freq_ref[...])
    for h in range(GROUP):
        head = q_ref[:, h * head_dim : (h + 1) * head_dim].astype(f32)
        heads_ref[h * sel : (h + 1) * sel, :] = turned(head, *fresh_angles)
    queries_ref[...] = heads_ref[...].astype(bf16)

    other = me + 1 - 2 * (me % 2)
    ours = (row + me * tokens).astype(f32)
    theirs = (picked_ref[pl.ds(other, 1), :] + other * tokens).astype(f32)
    both = jnp.concatenate([ours] * GROUP + [theirs] * GROUP, axis=1)
    at = put_rows(facts_ref, seq_count, both)

    shape = (seq_count, facts_ref.shape[1])
    lanes = lax.broadcasted_iota(jnp.int32, shape, 1)
    passages = lax.broadcasted_iota(jnp.int32, shape, 0)

    def start(k, rows):
        return jnp.where(passages == k, start_ref[k] + tokens, rows)

    starts = lax.fori_loop(0, seq_count, start, jnp.zeros(shape, jnp.int32), unroll=16)
    last = jnp.where(lanes == shape[1] - 1, (passages + 1) * tokens, starts).astype(f32)
    facts_ref[:seq_count, :] = jnp.where(lanes >= shape[1] - 2, last, FAR)
    facts_ref[:seq_count, :sel] = picked_ref[...].astype(f32)

    lanes = lax.broadcasted_iota(jnp.int32, (1, round_up(seq_count, shape[1])), 1)

    def slot(k, row):
        return jnp.where(lanes == k, slot_ref[order_ref[k]], row)

    slots = lax.fori_loop(0, seq_count, slot, jnp.zeros(lanes.shape, jnp.int32), unroll=16)
    at = put_rows(facts_ref, at, slots.astype(f32))
    put_rows(facts_ref, at, freq_ref[...])

    cosine, sine = pool_rotation(facts_ref, seq_count, queries_ref.shape[0], me, pages)
    angles_ref[:pages, :] = cosine
    angles_ref[pages:, :] = sine
    pack_pool(chunk_ref, pool_ref, (cosine, sine))
    pack_fresh(chunk_ref, fresh_ref, kv_ref, fresh_angles)


def merge_kernel(seq_count, query_rows, step, pool_ref, block_ref, facts_ref, angles_ref, chunk_ref):
    pages = pool_ref.shape[0]
    if pages % seq_count:
        me = lax.axis_index("seq")
        here = ring_place(me // 2, seq_count // 2)
        source = chunk_source(here, step, seq_count, me % 2)
        angles = pool_rotation(facts_ref, seq_count, query_rows, source, pages)
    else:
        angles = angles_ref[:pages, :], angles_ref[pages:, :]
    pack_pool(chunk_ref, pool_ref, angles)
    chunk_ref[pages:, :] = block_ref[...]


def chunk_source(here, step, seq_count, core):
    chips = seq_count // 2
    return ring_chip((here - step + chips) % chips, chips) * 2 + core


def put_rows(ref, at, row):
    width = ref.shape[1]
    for i in range(row.shape[1] // width):
        ref[at + i : at + i + 1, :] = row[:, i * width : (i + 1) * width]
    return at + row.shape[1] // width


def get_rows(ref, at, count):
    return jnp.concatenate([ref[at + i : at + i + 1, :] for i in range(count)], axis=1)


def fact_rows(seq_count, query_rows, width):
    return seq_count, 2 * query_rows // width, round_up(seq_count, width) // width, 1


def fresh_places(facts_ref, source, extra, tokens):
    row = jnp.broadcast_to(facts_ref[pl.ds(source, 1), :], (extra * PAGE, facts_ref.shape[1]))
    same = lax.broadcasted_iota(jnp.int32, row.shape, 0) == lax.broadcasted_iota(
        jnp.int32, row.shape, 1
    )
    fresh = jnp.sum(jnp.where(same, row, 0.0), axis=1, keepdims=True)
    return fresh + (source * tokens).astype(f32)


def cached_places(source, shared, seq_count, pages):
    spot = lax.broadcasted_iota(jnp.int32, (pages, 1), 0) * seq_count + source
    spot = spot.astype(f32)
    page = spot - pages * jnp.floor((spot + 0.5) * (1.0 / pages))
    begin = shared[:, shared.shape[1] - 1 :] - pages * PAGE + page * PAGE
    holder = jnp.floor(shared * (1.0 / PAGE))
    bits = jnp.where(holder == page, jnp.exp2(shared - PAGE * holder), 0.0)
    bits = jnp.sum(bits, axis=1, keepdims=True).astype(jnp.int32)
    return [jnp.where(((bits >> u) & 1) == 1, FAR, begin + u) for u in range(PAGE)]


def read_places(seq_count, tokens, arrivals, core, extra, facts_ref, query_rows):
    pages = tokens // PAGE
    here = ring_place(lax.axis_index("seq") // 2, seq_count // 2)
    table_rows, limit_rows, slot_rows, _ = fact_rows(seq_count, query_rows, facts_ref.shape[1])
    slots = get_rows(facts_ref, table_rows + limit_rows, slot_rows)[:, :seq_count].astype(jnp.int32)
    parts, shared = [], None
    for pool_step, fresh_steps in arrivals:
        groups = []
        if pool_step is not None:
            source = chunk_source(here, pool_step, seq_count, core)
            if shared is None or pages % seq_count:
                shared = holding(facts_ref, slots, source, pages)
            groups.append(cached_places(source, shared, seq_count, pages))
        for step in fresh_steps:
            if step is None:
                groups.append([jnp.full((extra, 1), FAR, f32)] * PAGE)
            else:
                source = chunk_source(here, step, seq_count, core)
                fresh = fresh_places(facts_ref, source, extra, tokens)
                groups.append([fresh[u * extra : (u + 1) * extra, :] for u in range(PAGE)])
        for u in range(PAGE):
            parts += [group[u] for group in groups]
    return jnp.concatenate(parts, axis=0)


def read_rows(pieces):
    parts = []
    for piece in pieces:
        width = piece.shape[1] // PAGE
        parts += [piece[:, u * width : (u + 1) * width] for u in range(PAGE)]
    return jnp.concatenate(parts, axis=0)


def read_limit(facts_ref, seq_count, query_rows):
    table_rows, limit_rows, _, _ = fact_rows(seq_count, query_rows, facts_ref.shape[1])
    return get_rows(facts_ref, table_rows, limit_rows)


def score_factor(head_dim):
    return float(head_dim**-0.5 * np.log2(np.e))


def attend(blended, flipped, place, queries, limit, old):
    head_dim = queries.shape[1]
    factor = score_factor(head_dim)
    scores = lax.dot_general(
        blended[:, :head_dim], queries, (((1,), (1,)), ((), ())), preferred_element_type=f32
    )
    scores = jnp.where(place <= limit, scores, MASKED)
    peak = jnp.maximum(jnp.max(scores, axis=0, keepdims=True), LOWEST if old is None else old[0])
    weights = jnp.exp2((scores - peak) * factor)
    total = jnp.sum(weights, axis=0, keepdims=True)
    mixed = jnp.dot(flipped, weights.astype(bf16), preferred_element_type=f32)
    if old is not None:
        fade = jnp.exp2((old[0] - peak) * factor)
        total = total + old[1] * fade
        mixed = mixed + old[2] * fade
    return peak, total, mixed


def chosen(place, wanted):
    return jnp.where(place == wanted, 1.0, 0.0).astype(bf16)


def get_state(ref):
    head_dim = ref.shape[0] - 8
    peak = ref[head_dim : head_dim + 1, :]
    total = ref[head_dim + 1 : head_dim + 2, :]
    return peak, total, ref[:head_dim, :]


def put_state(state, half, ref):
    peak, total, mixed = state
    head_dim = mixed.shape[0]
    tail = jnp.concatenate([peak, total, jnp.zeros((6, peak.shape[1]), f32)], axis=0)
    count = ref.shape[1]
    if half == 1:
        mixed, tail = pltpu.roll(mixed, count, 1), pltpu.roll(tail, count, 1)
    ref[:head_dim, :] = mixed[:, :count]
    ref[head_dim:, :] = tail[:, :count]


def put_pages(picked, ref, *others):
    count = ref.shape[0]
    pair = picked.shape[1]
    for u in range(PAGE):
        part = picked[u * count : (u + 1) * count, :]
        for other in others:
            part = part + other[:, u * pair : (u + 1) * pair].astype(f32)
        ref[:, u * pair : (u + 1) * pair] = part.astype(bf16)


def visit_kernel(seq_count, tokens, extra, arrivals, first, last, *refs):
    pieces, refs = refs[: len(arrivals)], refs[len(arrivals) :]
    own_q, other_q, facts_ref, wanted_ref = refs[:4]
    refs = refs[4:]
    old = None
    if not first:
        old, old_pages = get_state(refs[0]), refs[1]
        refs = refs[2:]
    core = lax.axis_index("seq") % 2
    query_rows = own_q.shape[0]
    place = read_places(seq_count, tokens, arrivals, core, extra, facts_ref, query_rows)
    blended = read_rows(pieces)
    limit = read_limit(facts_ref, seq_count, query_rows)
    queries = jnp.concatenate([own_q[...], other_q[...]], axis=0)
    flipped = blended.T
    state = attend(blended, flipped[own_q.shape[1] :, :], place, queries, limit, old)
    picked = jnp.dot(flipped, chosen(place, wanted_ref[...]), preferred_element_type=f32)
    if not first:
        picked = picked + old_pages[...].astype(f32)
    if not last:
        put_state(state, 0, refs[0])
        refs[1][...] = picked.astype(bf16)
    else:
        turned_pages = picked.T
        for half in (0, 1):
            put_state(state, half, refs[2 * half])
            put_pages(turned_pages[half * tokens : (half + 1) * tokens, :], refs[2 * half + 1])


def close_kernel(seq_count, tokens, extra, arrivals, *refs):
    pieces, refs = refs[: len(arrivals)], refs[len(arrivals) :]
    own_q, facts_ref, wanted_ref, mine, my_pages = refs[:5]
    new, new_pages, next_place, next_chosen = refs[5:]
    core = lax.axis_index("seq") % 2
    query_rows, head_dim = own_q.shape
    place = read_places(seq_count, tokens, arrivals, core, extra, facts_ref, query_rows)
    blended = read_rows(pieces)
    limit = read_limit(facts_ref, seq_count, query_rows)[:, :query_rows]
    wanted = wanted_ref[:, :tokens]
    state = attend(
        blended, blended[:, head_dim:].T, place, own_q[...], limit, get_state(mine)
    )
    put_state(state, 0, new)
    picked = jnp.dot(chosen(place, wanted).T, blended, preferred_element_type=f32)
    put_pages(picked, new_pages, my_pages)

    place = read_places(seq_count, tokens, arrivals, 1 - core, extra, facts_ref, query_rows)
    next_place[...] = jnp.broadcast_to(place, next_place.shape)
    next_chosen[...] = chosen(place, wanted).T


def finish_kernel(seq_count, tokens, extra, arrivals, *refs):
    pieces, refs = refs[: len(arrivals)], refs[len(arrivals) :]
    own_q, facts_ref, mine, my_pages, place_ref, chosen_ref, got, got_pages = refs[:8]
    out_ref, pages_ref, out_scratch, pages_scratch, sems = refs[8:]
    query_rows, head_dim = own_q.shape
    limit = read_limit(facts_ref, seq_count, query_rows)[:, :query_rows]
    blended = read_rows(pieces)
    picked = jnp.dot(chosen_ref[...], blended, preferred_element_type=f32)
    put_pages(picked, pages_scratch, my_pages, got_pages)
    pages_copy = pltpu.make_async_copy(pages_scratch, pages_ref, sems.at[0])
    pages_copy.start()
    one, two = get_state(mine), get_state(got)
    peak = jnp.maximum(one[0], two[0])
    fades = [jnp.exp2((part[0] - peak) * score_factor(head_dim)) for part in (one, two)]
    old = [peak] + [one[i] * fades[0] + two[i] * fades[1] for i in (1, 2)]
    flat, copies, done = None, [pages_copy], 0
    cut = round_up(query_rows // 2, LANES)
    sel = out_ref.shape[0]
    for columns in (slice(0, cut), slice(cut, query_rows)):
        _, total, mixed = attend(
            blended, blended[:, head_dim:].T, place_ref[:, :1], own_q[columns, :],
            limit[:, columns], [part[:, columns] for part in old],
        )
        rows = (mixed * (1.0 / total)).T
        flat = rows if flat is None else jnp.concatenate([flat, rows], axis=0)
        ready = flat.shape[0] // sel
        for h in range(done, ready):
            out_scratch[:, h * head_dim : (h + 1) * head_dim] = flat[
                h * sel : (h + 1) * sel, :
            ].astype(bf16)
        lanes = pl.ds(done * head_dim, (ready - done) * head_dim)
        copy = pltpu.make_async_copy(
            out_scratch.at[:, lanes], out_ref.at[:, lanes], sems.at[len(copies)]
        )
        copy.start()
        copies.append(copy)
        done = ready
    for copy in copies:
        copy.wait()


def shards(
    pool_kv, pool_slot, passage_order, passage_start, recompute_pos, page_table, fresh_q, fresh_kv
):
    seq_count = lax.axis_size("seq")
    chips = seq_count // 2
    me = lax.axis_index("seq")
    pages, width = pool_kv.shape
    sel = fresh_q.shape[0]
    head_dim = fresh_kv.shape[1] // 2
    tokens = pages * PAGE
    extra = round_up(-(-sel // PAGE), TILE)
    rows = pages + extra
    query_rows = sel * GROUP
    vmem = pl.BlockSpec(memory_space=pltpu.VMEM)
    params = pltpu.CompilerParams(vmem_limit_bytes=40 * 2**20)

    anywhere = pl.BlockSpec(memory_space=pltpu.HBM)
    frequency = jnp.asarray(frequencies(head_dim))

    swap = [(i, i ^ 1) for i in range(seq_count)]
    forward, backward = ring_pairs(chips, 1), ring_pairs(chips, -1)
    ahead = lax.ppermute(pool_kv, "seq", forward)
    behind = lax.ppermute(pool_kv, "seq", backward)

    fact_width = round_up(sel + 2, LANES)
    fact_count = round_up(sum(fact_rows(seq_count, query_rows, fact_width)), 8)
    chunk_shape = jax.ShapeDtypeStruct((rows, width), bf16)
    in_smem = [pool_slot, passage_order, passage_start]
    in_vmem = [frequency, recompute_pos, fresh_kv, fresh_q, pool_kv]
    in_all = [*in_smem, *in_vmem, page_table]
    queries, facts, angles, chunk, page_table = pl.pallas_call(
        partial(plan_kernel, seq_count, tokens),
        out_shape=(
            jax.ShapeDtypeStruct((query_rows, head_dim), bf16),
            jax.ShapeDtypeStruct((fact_count, fact_width), f32),
            jax.ShapeDtypeStruct((2 * pages, head_dim), f32),
            chunk_shape,
            jax.ShapeDtypeStruct(page_table.shape, page_table.dtype),
        ),
        in_specs=[anywhere] * 9,
        out_specs=(vmem,) * 5,
        scratch_shapes=[
            *[pltpu.SMEM(x.shape, x.dtype) for x in in_smem],
            *[pltpu.VMEM(x.shape, x.dtype) for x in in_vmem],
            pltpu.VMEM((extra * PAGE, 2 * head_dim), f32),
            pltpu.VMEM((query_rows, head_dim), f32),
            pltpu.SemaphoreType.DMA((9,)),
        ],
        compiler_params=params,
        cost_estimate=pl.CostEstimate(flops=10**8, bytes_accessed=6 * 2**20, transcendentals=0),
        name="plan",
    )(*[pltpu.with_memory_space_constraint(x, pltpu.HBM) for x in in_all])

    def merge(step, pool_part, block):
        return pl.pallas_call(
            partial(merge_kernel, seq_count, query_rows, step),
            out_shape=chunk_shape,
            in_specs=[vmem] * 4,
            out_specs=vmem,
            compiler_params=params,
            cost_estimate=pl.CostEstimate(flops=10**7, bytes_accessed=2**20, transcendentals=0),
            name="merge",
        )(pool_part, block, facts, angles)

    pair = jnp.stack([me, me ^ 1])
    page_ids = jnp.arange(pages, dtype=jnp.int32)
    request_pages = jnp.arange(page_table.shape[0], dtype=jnp.int32)
    owned = pair[:, None] * pages + page_ids[None, :]
    wanted = jnp.sum(
        jnp.where(page_table[None, None, :] == owned[:, :, None], request_pages[None, None, :], 0),
        axis=2,
    )
    wanted = wanted[:, None, :] * PAGE + jnp.arange(PAGE, dtype=jnp.int32)[None, :, None]
    wanted = wanted.astype(f32).reshape(1, 2 * tokens)

    other_queries = lax.ppermute(queries, "seq", swap)

    state_shapes = (
        jax.ShapeDtypeStruct((head_dim + 8, 2 * query_rows), f32),
        jax.ShapeDtypeStruct((2 * head_dim, 2 * tokens), bf16),
    )
    half_shapes = (
        jax.ShapeDtypeStruct((head_dim + 8, query_rows), f32),
        jax.ShapeDtypeStruct((pages, width), bf16),
    )
    close_shapes = half_shapes + (
        jax.ShapeDtypeStruct((PAGE * (rows + extra), LANES), f32),
        jax.ShapeDtypeStruct((tokens, PAGE * (rows + extra)), bf16),
    )
    out_shapes = (
        jax.ShapeDtypeStruct((sel, GROUP * head_dim), bf16),
        jax.ShapeDtypeStruct((pages, width), bf16),
    )

    def run(kernel, arrivals, operands, out_shape, name, aliases=(), weight=1, scratch=()):
        layout = [(pool_step, fresh_steps) for pool_step, fresh_steps, _ in arrivals]
        pieces = [piece for _, _, piece in arrivals]
        operands = pieces + list(operands)
        keys = PAGE * sum(piece.shape[0] for piece in pieces)
        pairs = keys * (query_rows + tokens)
        return pl.pallas_call(
            partial(kernel, seq_count, tokens, extra, layout),
            out_shape=out_shape,
            in_specs=[vmem] * len(operands),
            out_specs=(anywhere if scratch else vmem,) * len(out_shape),
            scratch_shapes=scratch,
            input_output_aliases={len(operands) - 2 + i: i for i in aliases},
            compiler_params=params,
            cost_estimate=pl.CostEstimate(
                flops=8 * pairs * head_dim * weight,
                bytes_accessed=4 * 2**20 * weight,
                transcendentals=2 * pairs * weight,
            ),
            name=name,
        )(*operands)

    def visit(state, arrivals, last=False):
        operands = [queries, other_queries, facts, wanted]
        first = state is None
        kernel = lambda count, size, more, layout, *refs: visit_kernel(
            count, size, more, layout, first, last, *refs
        )
        if not first:
            operands += list(state)
        out_shape = half_shapes * 2 if last else state_shapes
        aliases = () if first or last else (0, 1)
        return run(kernel, arrivals, operands, out_shape, "visit", aliases)

    half = chips // 2
    own_block = chunk[pages:]
    block = lax.ppermute(own_block, "seq", backward)
    ahead, behind = merge(1, ahead, own_block), merge(-1, behind, block)
    ahead, other_queries = lax.optimization_barrier((ahead, other_queries))
    behind, other_queries = lax.optimization_barrier((behind, other_queries))
    state = visit(None, [(0, (0,), chunk)])
    arrivals = [(1, (None,), ahead), (-1, (-1,), behind)]
    for step in range(2, half):
        ahead = lax.ppermute(ahead, "seq", forward)
        behind = lax.ppermute(behind, "seq", backward)
        state = visit(state, arrivals)
        ahead, state = lax.optimization_barrier((ahead, state))
        arrivals = [(step, (step - 1,), ahead), (-step, (-step,), behind)]
    farthest = lax.ppermute(ahead, "seq", forward)
    fresh_farthest = lax.ppermute(behind[pages:], "seq", backward)
    mine, my_pages, theirs, their_pages = visit(state, arrivals, last=True)
    got = lax.ppermute(theirs, "seq", swap)
    got_pages = lax.ppermute(their_pages, "seq", swap)
    other_farthest = lax.ppermute(farthest, "seq", swap)
    other_fresh = lax.ppermute(fresh_farthest, "seq", swap)
    operands = [queries, facts, wanted, mine, my_pages]
    *state, place, choice = run(
        close_kernel, [(half, (half - 1,), farthest), (None, (half,), fresh_farthest)], operands, close_shapes, "close", weight=10
    )
    scratch = [pltpu.VMEM(x.shape, x.dtype) for x in out_shapes]
    scratch.append(pltpu.SemaphoreType.DMA((3,)))
    operands = [queries, facts, *state, place, choice, got, got_pages]
    return run(
        finish_kernel, [(half, (half - 1,), other_farthest), (None, (half,), other_fresh)], operands, out_shapes, "finish",
        scratch=scratch,
    )


def solution(mesh):
    placed = (
        P(("groups", "seq"), None),
        P("groups"),
        P("groups"),
        P("groups"),
        P("groups", None),
        P("groups"),
        P(("groups", "seq"), None),
        P(("groups", "seq"), None),
    )
    return jax.shard_map(
        shards,
        mesh=mesh,
        in_specs=placed,
        out_specs=(P(("groups", "seq"), None), P(("groups", "seq"), None)),
        check_vma=False,
    )
```
